32 devices in a mesh: pipe: 4 (over y, x), dp: 8 (over z, core).
Axes of the slice: x: 2, y: 2, z: 4, core: 2. Of those that a mesh axis runs over, the one named last changes fastest.
Arguments:
- x_big: bfloat16 [4, 8, 14, 14, 1024], P(None, 'dp'), may hold values from -6 to 6
- x_small: bfloat16 [4, 16, 6, 6, 1024], P(None, 'dp'), may hold values from -6 to 6
- cot_big: bfloat16 [4, 8, 7, 7, 2048], P(None, 'dp'), may hold values from -6 to 6
- cot_small: bfloat16 [4, 16, 3, 3, 2048], P(None, 'dp'), may hold values from -6 to 6
- section_weights: bfloat16 [4, 4456448], P('pipe'), may hold values from -0.1875 to 0.1875
- section_norms: float32 [4, 4, 4096], P('pipe'), may hold values from 0.5 to 1.5
- gate_big: int32 [4, 8], P(None, 'dp'), may hold values 0 or 1
- gate_small: int32 [4, 16], P(None, 'dp'), may hold values 0 or 1
- width_step: int32 [4], replicated, may hold values from 1 to 4
Outputs:
- out_big: bfloat16 [4, 8, 7, 7, 2048], P('pipe', 'dp')
- out_small: bfloat16 [4, 16, 3, 3, 2048], P('pipe', 'dp')
- grad_big: bfloat16 [4, 8, 14, 14, 1024], P('pipe', 'dp')
- grad_small: bfloat16 [4, 16, 6, 6, 1024], P('pipe', 'dp')
- weight_grads: float32 [4, 4456448], P('pipe', 'dp')
- norm_grads: float32 [4, 4, 4096], P('pipe')
The draws below stay inside these ranges and needn't reach their ends.
Inputs may be any that keep to these rules, and one draw needn't show every extreme that they name: `gate_big`: 1 keeps the crop's identity-block branch, 0 skips it. `gate_small`: 1 keeps the crop's identity-block branch, 0 skips it. The 96-pixel crops of micro-batch m use the first 512 * width_step[m] / 4 bottleneck channels.
All inputs are finite; a program needn't handle non-finite values.
Results may differ from the reference program's by a relative error of at most 0.017.
Values may be sent and summed in bfloat16 or wider, within the bound.
A program may use at most 576 MiB of HBM per device.

```python
import jax
import jax.numpy as jnp
from jax import lax

C_IN = 1024
C_MID = 512
C_OUT = 2048
S_BIG = 14
S_SMALL = 6
SECTIONS = 4
MICRO = 4
BIG = 8
SMALL = 16
PW = 4456448
NW = 4096


def with_ends(values, rng, low, top_value):
    extent = values.shape
    spot = [jax.random.randint(jax.random.fold_in(rng, axis), (), 0, extent[axis]) for axis in range(len(extent))]
    values = values.at[tuple(spot)].set(low)
    longest = extent.index(max(extent))
    spot[longest] = (spot[longest] + 1) % extent[longest]
    return values.at[tuple(spot)].set(top_value)


def shard_levels(key, shape, split, least, top_value):
    def one(axis_at, parts):
        steps = jax.random.uniform(jax.random.fold_in(jax.random.fold_in(key, 6), axis_at), (parts,), jnp.float32, least / len(split), top_value / len(split))
        return jnp.repeat(jnp.exp(steps), shape[axis_at] // parts).reshape((-1,) + (1,) * (len(shape) - axis_at - 1))

    level = one(*split[0])
    for cut in split[1:]:
        level = level * one(*cut)
    return level


def normal_values(stream_key, shape, spread, reach, cuts=(), held_as=jnp.bfloat16):
    level = shard_levels(stream_key, shape, cuts, -0.22, 0.18) if cuts else 1.0
    drawn = jax.random.normal(stream_key, shape, jnp.float32) * spread * level
    return jnp.minimum(jnp.maximum(drawn, -reach), reach).astype(held_as)


def setup_inputs(seed: int = 0) -> dict:
    arg_keys = jax.random.split(jax.random.key(seed), 10)
    return {
        "x_big": normal_values(arg_keys[0], (MICRO, BIG, S_BIG, S_BIG, C_IN), 1.0, 6.0, ((1, 8),)),
        "x_small": normal_values(arg_keys[1], (MICRO, SMALL, S_SMALL, S_SMALL, C_IN), 1.0, 6.0, ((1, 8),)),
        "cot_big": normal_values(arg_keys[2], (MICRO, BIG, S_BIG // 2, S_BIG // 2, C_OUT), 1.0, 6.0, ((1, 8),)),
        "cot_small": normal_values(arg_keys[3], (MICRO, SMALL, S_SMALL // 2, S_SMALL // 2, C_OUT), 1.0, 6.0, ((1, 8),)),
        "section_weights": normal_values(arg_keys[4], (SECTIONS, PW), C_IN ** -0.5, 0.1875, ((0, 4),)),
        "section_norms": jnp.clip(0.5 + 1.0 * jax.random.uniform(arg_keys[5], (SECTIONS, 4, NW), jnp.float32) ** shard_levels(arg_keys[5], (SECTIONS, 4, NW), ((0, 4),), -0.2, 0.2), 0.5, 1.5),
        "gate_big": with_ends((jax.random.randint(arg_keys[6], (MICRO, BIG), 0, 4) < 3).astype(jnp.int32), jax.random.fold_in(arg_keys[6], 1), 0, 1),
        "gate_small": with_ends((jax.random.randint(arg_keys[7], (MICRO, SMALL), 0, 4) < 3).astype(jnp.int32), jax.random.fold_in(arg_keys[7], 1), 0, 1),
        "width_step": with_ends(jax.random.randint(arg_keys[8], (MICRO,), 1, 5), jax.random.fold_in(arg_keys[8], 1), 1, 4).astype(jnp.int32),
    }


EPS = 1e-05
HIGHEST = lax.Precision.HIGHEST

@jax.custom_vjp
def low(v):
    return lax.optimization_barrier(v.astype(jnp.bfloat16)).astype(jnp.float32)

@jax.custom_vjp
def low_back(v):
    return v

def low_keep(v):
    return (low(v), None)

def low_pass(kept, grad):
    return (grad,)

def back_keep(v):
    return (v, None)

def back_low(kept, grad):
    return (low(grad),)
low.defvjp(low_keep, low_pass)
low_back.defvjp(back_keep, back_low)

def pointwise(inputs, weight):
    return jnp.einsum('nhwc,cd->nhwd', inputs, weight, precision=HIGHEST)

def spatial(inputs, weight, stride):
    kernel = weight.reshape(3, 3, weight.shape[1], weight.shape[2])
    return lax.conv_general_dilated(inputs, kernel, (stride, stride), ((1, 1), (1, 1)), dimension_numbers=('NHWC', 'HWIO', 'NHWC'), precision=HIGHEST)

def batch_norm(values, norm_table, gain_row, offset):
    width = values.shape[-1]
    mean_v = lax.optimization_barrier(jnp.mean(values, axis=(0, 1, 2)))
    var_v = lax.optimization_barrier(jnp.mean(values * values, axis=(0, 1, 2))) - mean_v * mean_v
    centered = (values - mean_v) * lax.rsqrt(var_v + EPS)
    return centered * norm_table[gain_row, offset:offset + width] + norm_table[gain_row + 1, offset:offset + width]

def unpack(weights):
    w_first = weights[0, :C_IN * C_MID].reshape(C_IN, C_MID)
    w_second = weights[1, :9 * C_MID * C_MID].reshape(9, C_MID, C_MID)
    split_at = C_MID * C_OUT
    w_third = weights[2, :split_at].reshape(C_MID, C_OUT)
    w_project = weights[2, split_at:split_at + C_IN * C_OUT].reshape(C_IN, C_OUT)
    begin_b = C_OUT * C_MID
    begin_c = begin_b + 9 * C_MID * C_MID
    w_narrow = weights[3, :begin_b].reshape(C_OUT, C_MID)
    w_spatial = weights[3, begin_b:begin_c].reshape(9, C_MID, C_MID)
    w_widen = weights[3, begin_c:begin_c + C_MID * C_OUT].reshape(C_MID, C_OUT)
    return (w_first, w_second, w_third, w_project, w_narrow, w_spatial, w_widen)

def group_forward(matrices, norms, images, gate_v, keep_mask, gain_row):
    w_first, w_second, w_third, w_project, w_narrow, w_spatial, w_widen = matrices
    pre_one = low_back(pointwise(images, w_first))
    act_one = low(low_back(jax.nn.silu(batch_norm(pre_one, norms[0], gain_row, 0)) * keep_mask))
    pre_two = low_back(spatial(act_one, w_second, 2))
    act_two = low(low_back(jax.nn.silu(batch_norm(pre_two, norms[1], gain_row, 0)) * keep_mask))
    main_pre = low_back(pointwise(act_two, w_third))
    short_pre = low_back(pointwise(images[:, ::2, ::2, :], w_project))
    joined = batch_norm(main_pre, norms[2], gain_row, 0) + batch_norm(short_pre, norms[2], gain_row, C_OUT)
    block_one = low(low_back(jax.nn.silu(joined)))
    pre_a = low_back(pointwise(block_one, w_narrow))
    hidden_a = low(jax.nn.silu(batch_norm(pre_a, norms[3], gain_row, 0)) * keep_mask)
    pre_b = low_back(spatial(hidden_a, w_spatial, 1))
    hidden_b = low(jax.nn.silu(batch_norm(pre_b, norms[3], gain_row, C_MID)) * keep_mask)
    pre_c = low_back(pointwise(hidden_b, w_widen))
    branch = batch_norm(pre_c, norms[3], gain_row, 2 * C_MID)
    return jax.nn.silu(block_one + gate_v[:, None, None, None] * branch)

def reference(x_big, x_small, cot_big, cot_small, section_weights, section_norms, gate_big, gate_small, width_step):
    weights = section_weights.astype(jnp.float32)
    keep_big = jnp.ones((C_MID,), jnp.float32)
    outs_big, outs_small, grads_big, grads_small = ([], [], [], [])
    weight_total = jnp.zeros(weights.shape, jnp.float32)
    norm_total = jnp.zeros(section_norms.shape, jnp.float32)
    for micro_id in range(MICRO):
        gates_b = gate_big[micro_id].astype(jnp.float32)
        gates_s = gate_small[micro_id].astype(jnp.float32)
        keep_small = (jnp.arange(C_MID) < C_MID * width_step[micro_id] // 4).astype(jnp.float32)

        def forward(params, norms, images_big, images_small):
            matrices = unpack(params)
            return (group_forward(matrices, norms, images_big, gates_b, keep_big, 0), group_forward(matrices, norms, images_small, gates_s, keep_small, 2))
        outputs, pullback = jax.vjp(forward, weights, section_norms, x_big[micro_id].astype(jnp.float32), x_small[micro_id].astype(jnp.float32))
        grad_w, grad_n, grad_xb, grad_xs = pullback((cot_big[micro_id].astype(jnp.float32), cot_small[micro_id].astype(jnp.float32)))
        weight_total = weight_total + grad_w
        norm_total = norm_total + grad_n
        outs_big.append(outputs[0])
        outs_small.append(outputs[1])
        grads_big.append(grad_xb)
        grads_small.append(grad_xs)
    return (jnp.stack(outs_big).astype(jnp.bfloat16), jnp.stack(outs_small).astype(jnp.bfloat16), jnp.stack(grads_big).astype(jnp.bfloat16), jnp.stack(grads_small).astype(jnp.bfloat16), weight_total, norm_total)
```

```python
import functools

import jax
import jax.numpy as jnp
import numpy as np
from jax import lax
from jax.experimental import pallas as pl
from jax.experimental.pallas import tpu as pltpu
from jax.sharding import PartitionSpec as P

C_IN = 1024
C_MID = 512
C_OUT = 2048
EPS = 1e-05
W = 512
NQ = C_OUT // W
CH = 16
LANES = W // 128
HALF = W // 2
BF = jnp.bfloat16
F32 = jnp.float32
MESH = pl.DeviceIdType.MESH


def up16(n):
    return -(-n // 16) * 16


class Geometry:
    def __init__(self, crops, sides):
        self.crops, self.sides = crops, sides
        self.in_big = crops[0] * sides[0] ** 2
        self.in_all = self.in_big + crops[1] * sides[1] ** 2
        self.out_big = crops[0] * (sides[0] // 2) ** 2
        self.out_all = self.out_big + crops[1] * (sides[1] // 2) ** 2
        self.IN, self.OUT = up16(self.in_all), up16(self.out_all)

    def pixels(self, halves):
        index, table = 0, {}
        for group in (0, 1):
            side = self.sides[group] // 2 if halves else self.sides[group]
            for crop in range(self.crops[group]):
                for r in range(side):
                    for c in range(side):
                        table[group, crop, r, c] = index
                        index += 1
        return table

    def windows(self, stride):
        ins, outs = self.pixels(stride == 1), self.pixels(True)
        picks = np.zeros((9, self.OUT, self.OUT if stride == 1 else self.IN), np.float32)
        for (group, crop, r, c), row in outs.items():
            for tap in range(9):
                at = (group, crop, stride * r + tap // 3 - 1, stride * c + tap % 3 - 1)
                if at in ins:
                    picks[tap, row, ins[at]] = 1.0
        return picks.reshape(9 * self.OUT, -1)

    def every_second(self):
        ins, outs = self.pixels(False), self.pixels(True)
        picks = np.zeros((self.OUT, self.IN), np.float32)
        for (group, crop, r, c), row in outs.items():
            picks[row, ins[group, crop, 2 * r, 2 * c]] = 1.0
        return picks


def dot(a, b):
    return jnp.dot(a, b, preferred_element_type=F32)


def dot_nt(a, b):
    return lax.dot_general(a, b, (((1,), (1,)), ((), ())), preferred_element_type=F32)


def dot_tn(a, b):
    return lax.dot_general(a, b, (((0,), (0,)), ((), ())), preferred_element_type=F32)


def sigmoid(v):
    return 1.0 / (1.0 + jnp.exp(-v))


def slope_of(v):
    s = sigmoid(v)
    return s * (1.0 + v * (1.0 - s))


def runs_of(n_big, n_all, rows):
    runs = []
    for first in range(0, rows, CH):
        kind = (min(max(n_big - first, 0), CH), min(max(n_all - first, 0), CH))
        if runs and runs[-1][2:] == kind:
            runs[-1] = (runs[-1][0], runs[-1][1] + 1) + kind
        else:
            runs.append((first, 1) + kind)
    return runs


def row_ids():
    return lax.broadcasted_iota(jnp.int32, (CH, W), 0)


def part(v, low, high):
    if low >= high:
        return None
    if low == 0 and high == CH:
        return v
    r = row_ids()
    return jnp.where((r >= low) & (r < high), v, 0.0)


def pick(vb, vs, bc):
    if bc == CH:
        return vb
    if bc == 0:
        return vs
    return jnp.where(row_ids() < bc, vb, vs)


def each_step(blocks, runs, body, carry):
    def one_block(b, carry):
        for first, length, bc, vc in runs:
            if length == 1:
                carry = body(b, first, bc, vc, carry)
            else:
                carry = lax.fori_loop(
                    0,
                    length,
                    lambda i, c: body(b, pl.multiple_of(first + CH * i, CH), bc, vc, c),
                    carry,
                    unroll=min(length, 4) if length % min(length, 4) == 0 else 1,
                )
        return carry

    if blocks == 1:
        return one_block(0, carry)
    return lax.fori_loop(0, blocks, one_block, carry)


def reduce_rows(blocks, runs, fn, count):
    def body(b, first, bc, vc, carry):
        values = fn(b, first, bc, vc)
        new = []
        for i, v in enumerate(values):
            for g, piece in enumerate((part(v, 0, bc), part(v, bc, vc))):
                total = carry[g * count + i]
                new.append((g * count + i, total if piece is None else total + piece[:8] + piece[8:]))
        return tuple(v for _, v in sorted(new, key=lambda t: t[0]))

    zero = jnp.zeros((8, W), F32)
    totals = each_step(blocks, runs, body, (zero,) * (2 * count))
    return [jnp.sum(t, axis=0, keepdims=True) for t in totals]


def map_rows(blocks, runs, fn):
    def body(b, first, bc, vc, carry):
        fn(b, first, bc, vc)
        return carry

    each_step(blocks, runs, body, 0)


def make_kernel(geo, R, NP, MICRO, SR, PC):
    G = R // MICRO
    PR = SR // PC
    ADD = PR // 17 if PR % 17 == 0 else CH
    IN, OUT = geo.IN, geo.OUT
    ROWS = MICRO * OUT
    runs_in = runs_of(geo.in_big, geo.in_all, IN)
    runs_out = runs_of(geo.out_big, geo.out_all, OUT)
    count_in = (float(R * geo.in_big), float(R * (geo.in_all - geo.in_big)))
    count_out = (float(R * geo.out_big), float(R * (geo.out_all - geo.out_big)))

    def kernel(
        x_h, cot_h, gate_v, w4_h, w16_h, nt, keep, p2, p2t, pb, ps, pst,
        out_h, dx_o, dw_o, ng_o,
        wbuf, raw, xb, gateb, stage, rbig, ssm, rsm, fw, dwide, col, tgb, tmp, mrecv, srecv,
        dwl, pbuf, rv,
        own_a, rcv_a, own_b, rcv_b, par, cof, ngs, ngr,
        ld, raw_s, big_s, big_r, sm_s, sm_r, xs_s, xs_r, ct_s, ct_r, gt_s, gt_r,
        out_s, out_r, mn_s, mn_r, sb_s, sb_r, sta_s, sta_r, stb_s, stb_r, stn_s, stn_r,
        pa_s, pa_r, ch_s, ch_r,
    ):
        me_p, me_d = lax.axis_index("pipe"), lax.axis_index("dp")
        my_m, my_c = me_d // G, me_d % G

        def remote(src, dst, ss, rs, p, d):
            return pltpu.make_async_remote_copy(
                src_ref=src, dst_ref=dst, send_sem=ss, recv_sem=rs, device_id=(p, d), device_id_type=MESH
            )

        def push(src, dst, ss, rs, p, d):
            here = (me_p == p) & (me_d == d)

            @pl.when(here)
            def _():
                pltpu.make_async_copy(src, dst, rs).start()

            @pl.when(jnp.logical_not(here))
            def _():
                remote(src, dst, ss, rs, p, d).start()

        def pushed(src, dst, ss, rs, p, d):
            @pl.when(jnp.logical_not((me_p == p) & (me_d == d)))
            def _():
                remote(src, dst, ss, rs, p, d).wait_send()

        def arrived(dst, rs):
            remote(dst, dst, rs, rs, me_p, me_d).wait_recv()

        def sent(src, ss):
            remote(src, src, ss, ss, me_p, me_d).wait_send()

        def load(src, dst, i):
            return pltpu.make_async_copy(src, dst, ld.at[i])

        def send_a(slot):
            def one(k, c):
                remote(
                    own_a.at[slot], rcv_a.at[slot, k - 1], sta_s.at[slot], sta_r.at[slot],
                    me_p, lax.rem(me_d + k, R),
                ).start()
                return c

            lax.fori_loop(1, R, one, 0, unroll=R <= 8)

        def total_a(slot):
            arrived(rcv_a.at[slot], sta_r.at[slot])
            return lax.fori_loop(0, R - 1, lambda k, t: t + rcv_a[slot, k], own_a[slot], unroll=R <= 8)

        def send_b(slot):
            def one(k, c):
                remote(
                    own_b.at[slot], rcv_b.at[slot, k - 1], stb_s.at[slot], stb_r.at[slot],
                    me_p, my_m * G + lax.rem(my_c + k, G),
                ).start()
                return c

            lax.fori_loop(1, G, one, 0, unroll=G <= 8)

        def total_b(slot):
            arrived(rcv_b.at[slot], stb_r.at[slot])
            return lax.fori_loop(0, G - 1, lambda k, t: t + rcv_b[slot, k], own_b[slot], unroll=G <= 8)

        def put(ref, slot, sums):
            for i, s in enumerate(sums):
                ref[slot, pl.ds(i, 1), :] = s

        def finish_norm(total, slot, cb, counts):
            for g in (0, 1):
                mean = total[2 * g : 2 * g + 1] * (1.0 / counts[g])
                var = total[2 * g + 1 : 2 * g + 2] * (1.0 / counts[g]) - mean * mean
                rstd = lax.rsqrt(var + EPS)
                scale = rstd * nt[cb, 2 * g : 2 * g + 1, :]
                par[slot, pl.ds(4 * g, 1), :] = mean
                par[slot, pl.ds(4 * g + 1, 1), :] = rstd
                par[slot, pl.ds(4 * g + 2, 1), :] = scale
                par[slot, pl.ds(4 * g + 3, 1), :] = nt[cb, 2 * g + 1 : 2 * g + 2, :] - mean * scale

        def param(slot, i, bc):
            return pick(par[slot, pl.ds(i, 1), :], par[slot, pl.ds(4 + i, 1), :], bc)

        def normed(u, slot, bc):
            return u * param(slot, 2, bc) + param(slot, 3, bc)

        def centered(u, slot, bc):
            return (u - param(slot, 0, bc)) * param(slot, 1, bc)

        def finish_back(total, slot, counts, names):
            width = 1 + names
            for g in (0, 1):
                for i in range(width):
                    cof[slot, pl.ds(g * 4 + i, 1), :] = total[g * width + i : g * width + i + 1] * (1.0 / counts[g])

        def back(d, z, cslot, which, pslot, bc, vc):
            a = pick(cof[cslot, pl.ds(0, 1), :], cof[cslot, pl.ds(4, 1), :], bc)
            b = pick(cof[cslot, pl.ds(1 + which, 1), :], cof[cslot, pl.ds(5 + which, 1), :], bc)
            du = param(pslot, 2, bc) * (d - a - z * b)
            return (du if vc == CH else part(du, 0, vc) if vc else jnp.zeros_like(du)).astype(BF)

        def kept(v, m, bc):
            return v if bc == CH else v * pick(jnp.ones((1, W), F32), keep[m], bc)

        def rows(first, n=CH):
            return pl.ds(first, n)

        def at(b, first):
            return pl.ds(pl.multiple_of(b * OUT + first, CH), CH)

        n1 = C_IN
        n2 = 9 * C_MID
        n3 = C_MID + C_IN
        nab = C_OUT + 9 * C_MID

        def fetch(count, source, target):
            def copies(b, slot):
                return [
                    pltpu.make_async_copy(source(b, lane), raw.at[slot, lane], raw_s.at[slot, lane])
                    for lane in range(LANES)
                ]

            for copy in copies(0, 0):
                copy.start()

            def one(b, c):
                slot = lax.rem(b, 2)

                @pl.when(b + 1 < count)
                def _():
                    for copy in copies(b + 1, 1 - slot):
                        copy.start()

                for lane, copy in enumerate(copies(b, slot)):
                    copy.wait()
                    values = raw[slot, lane, :, 0, :].astype(F32).astype(BF)
                    wbuf[pl.ds(pl.multiple_of(target(b), W), W), pl.ds(lane * 128, 128)] = values
                return c

            lax.fori_loop(0, count, one, 0)

        def fetch_narrow(blocks):
            fetch(blocks, lambda b, lane: w4_h.at[pl.ds(b * W, W), lane], lambda b: b * W)

        def fetch_wide(first, blocks, target):
            fetch(
                NQ * blocks,
                lambda b, lane: w16_h.at[pl.ds(first + b // NQ * W, W), lax.rem(b, NQ) * LANES + lane],
                lambda b: target(lax.rem(b, NQ), b // NQ * W),
            )

        barrier = pltpu.get_barrier_semaphore()

        @pl.when((me_p == 0) | (me_p == 2))
        def _():
            load(x_h, xb.at[:, pl.ds(0, IN)], 0).start()

        def greet(i, c):
            p, d = i // R, lax.rem(i, R)

            @pl.when((p != me_p) | (d != me_d))
            def _():
                pl.semaphore_signal(barrier, inc=1, device_id=(p, d), device_id_type=MESH)

            return c

        lax.fori_loop(0, NP * R, greet, 0)

        def first_product(m):
            fw[m, pl.ds(0, IN), :] = dot(xb[2 * m, pl.ds(0, IN), :], wbuf[pl.ds(0, W), :]) + dot(
                xb[2 * m + 1, pl.ds(0, IN), :], wbuf[pl.ds(W, W), :]
            )

            def sums(b, f, bc, vc):
                u = fw[m, rows(f), :]
                return (u, u * u)

            put(own_a, m, reduce_rows(1, runs_in, sums, 2))

        @pl.when(me_p == 0)
        def _():
            fetch_narrow(n1 // W)
            load(x_h, xb.at[:, pl.ds(0, IN)], 0).wait()
            first_product(0)

        pl.semaphore_wait(barrier, NP * R - 1)

        ng_o[...] = jnp.zeros_like(ng_o)

        def keep_narrow(first, grad):
            for lane in range(LANES):
                tmp[pl.ds(lane, W, stride=LANES), :] = grad[:, lane * 128 : (lane + 1) * 128]
            start = pl.multiple_of(first * LANES, W)
            dwl[pl.ds(start, W * LANES), :] = tmp[pl.ds(0, W * LANES), :].astype(BF)

        def keep_wide(first, lhs, index):
            step = NQ * LANES
            for half in range(W // HALF):
                for q in range(NQ):
                    grad = dot_tn(lhs(pl.ds(half * HALF, HALF)), dwide[index + q, pl.ds(0, ROWS), :])
                    for lane in range(LANES):
                        part_of = grad[:, lane * 128 : (lane + 1) * 128]
                        tmp[pl.ds(q * LANES + lane, HALF, stride=step), :] = part_of
                dwl[pl.ds((first + half * HALF) * step, HALF * step), :] = tmp[...].astype(BF)

        def reduce_scatter(used_rows):
            n, i, core = R // 2, me_d // 2, lax.rem(me_d, 2)
            filled = -(-used_rows // PR) * PR
            if filled > used_rows:
                dwl[pl.ds(used_rows, filled - used_rows), :] = jnp.zeros((filled - used_rows, 128), BF)

            def start_of(t, side, pc):
                return pl.multiple_of((2 * t + side) * SR + pc * PR, CH)

            def used(t, side, pc):
                return (2 * t + side) * SR + pc * PR < used_rows

            def pair(t, pc):
                return remote(
                    dwl.at[pl.ds(start_of(t, 1 - core, pc), PR)], pbuf.at[t, pc],
                    pa_s.at[t, pc], pa_r.at[t, pc], me_p, me_d + 1 - 2 * core,
                )

            def rightward(t, pc):
                return remote(rv.at[t, pc], rv.at[t, pc], ch_s.at[t, pc], ch_r.at[t, pc], me_p, me_d + 2)

            def leftward(t, pc):
                slot = jnp.where(t == i - 1, n, t)
                return remote(rv.at[t, pc], rv.at[slot, pc], ch_s.at[t, pc], ch_r.at[slot, pc], me_p, me_d - 2)

            def pieces(fn):
                def one(j, c):
                    for pc in range(PC):
                        fn(j, pc)
                    return c

                lax.fori_loop(0, n, one, 0)

            def add(t, pc, others, store):
                first = start_of(t, core, pc)

                def one(s, c):
                    at_s = pl.ds(pl.multiple_of(s * ADD, CH), ADD)
                    v = dwl[pl.ds(pl.multiple_of(first + s * ADD, CH), ADD), :].astype(F32)
                    v += pbuf[t, pc, at_s, :].astype(F32)
                    for slot in others:
                        v += rv[slot, pc, at_s, :].astype(F32)
                    store(at_s, s, v)
                    return c

                lax.fori_loop(0, PR // ADD, one, 0)

            def send_pair(j, pc):
                t = jnp.where(lax.rem(j, 2) == 0, n - 1 - j // 2, j // 2)

                @pl.when(used(t, 1 - core, pc))
                def _():
                    pair(t, pc).start()

            def forward(t, pc, inside, more, copy):
                def store(at_s, s, v):
                    rv[t, pc, at_s, :] = v.astype(BF)

                @pl.when(inside & used(t, core, pc))
                def _():
                    pair(t, pc).wait_recv()

                    @pl.when(more)
                    def _():
                        arrived(rv.at[t, pc], ch_r.at[t, pc])
                        add(t, pc, (t,), store)

                    @pl.when(jnp.logical_not(more))
                    def _():
                        add(t, pc, (), store)

                    copy(t, pc).start()

            def both_ways(j, pc):
                right, left = n - 1 - j, j
                forward(right, pc, right > i, i > 0, rightward)
                forward(left, pc, left < i, i < n - 1, leftward)

            def finish(pc):
                def out_rows(s):
                    return pl.ds(pl.multiple_of(pc * PR + s * ADD, CH), ADD)

                def store(at_s, s, v):
                    dw_o[out_rows(s), :] = v

                @pl.when(jnp.logical_not(used(i, core, pc)))
                def _():
                    dw_o[pl.ds(pc * PR, PR), :] = jnp.zeros((PR, 128), F32)

                @pl.when(used(i, core, pc))
                def _():
                    pair(i, pc).wait_recv()
                    for low, high in ((True, True), (True, False), (False, True)):

                        @pl.when(((i > 0) == low) & ((i < n - 1) == high))
                        def _(low=low, high=high):
                            others = ()
                            if low:
                                arrived(rv.at[i, pc], ch_r.at[i, pc])
                                others += (i,)
                            if high:
                                arrived(rv.at[n, pc], ch_r.at[n, pc])
                                others += (n,)
                            add(i, pc, others, store)

            def sent_all(j, pc):
                @pl.when(used(j, 1 - core, pc))
                def _():
                    pair(j, pc).wait_send()

                @pl.when((j > i) & used(j, core, pc))
                def _():
                    rightward(j, pc).wait_send()

                @pl.when((j < i) & used(j, core, pc))
                def _():
                    leftward(j, pc).wait_send()

            pieces(send_pair)
            pieces(both_ways)
            for pc in range(PC):
                finish(pc)
            pieces(sent_all)

        def add_norm_grads(cb, total):
            for g in (0, 1):
                ng_o[cb, pl.ds(2 * g, 1), :] += total[2 * g + 1 : 2 * g + 2]
                ng_o[cb, pl.ds(2 * g + 1, 1), :] += total[2 * g : 2 * g + 1]

        @pl.when(me_p == 0)
        def _():
            send_a(0)

            def first(m, c):
                first_product(m)
                send_a(m)
                return c

            lax.fori_loop(1, MICRO, first, 0)

            def second(m, c):
                finish_norm(total_a(m), m, 0, count_in)

                def act(b, f, bc, vc):
                    n = normed(fw[m, rows(f), :], m, bc)
                    stage[m, rows(f), :] = kept(n * sigmoid(n), m, bc).astype(BF)

                map_rows(1, runs_in, act)
                push(stage.at[m, pl.ds(0, IN)], rbig.at[m, pl.ds(0, IN)], big_s.at[m], big_r.at[m], 1, me_d)
                return c

            lax.fori_loop(0, MICRO, second, 0)

            def main_copy(m):
                return (tgb.at[pl.ds(2 * m, 2), pl.ds(0, IN)], mrecv, mn_s.at[m], mn_r, m, me_d)

            def third(m, c):
                arrived(rbig.at[m, pl.ds(0, IN)], big_r.at[m])

                def sums(b, f, bc, vc):
                    u = fw[m, rows(f), :]
                    d = kept(rbig[m, rows(f), :].astype(F32) * slope_of(normed(u, m, bc)), m, bc)
                    fw[MICRO + m, rows(f), :] = d
                    return (d, d * centered(u, m, bc))

                put(own_a, MICRO + m, reduce_rows(1, runs_in, sums, 2))
                send_a(MICRO + m)
                total = total_a(MICRO + m)
                finish_back(total, 0, count_in, 1)
                add_norm_grads(0, total)

                def grad(b, f, bc, vc):
                    z = centered(fw[m, rows(f), :], m, bc)
                    dwide[m, rows(f), :] = back(fw[MICRO + m, rows(f), :], z, 0, 0, m, bc, vc)

                map_rows(1, runs_in, grad)
                for h in range(2):
                    piece = dot_nt(dwide[m, pl.ds(0, IN), :], wbuf[pl.ds(h * W, W), :])
                    tgb[2 * m + h, pl.ds(0, IN), :] = piece.astype(BF)
                push(*main_copy(m))
                return c

            lax.fori_loop(0, MICRO, third, 0)
            for h in range(2):
                total = dot_tn(xb[h, pl.ds(0, IN), :], dwide[0, pl.ds(0, IN), :])
                for m in range(1, MICRO):
                    total += dot_tn(xb[2 * m + h, pl.ds(0, IN), :], dwide[m, pl.ds(0, IN), :])
                keep_narrow(h * W, total)
            reduce_scatter(n1 * LANES)
            for m in range(MICRO):
                pushed(stage.at[m, pl.ds(0, IN)], rbig.at[m, pl.ds(0, IN)], big_s.at[m], big_r.at[m], 1, me_d)
                pushed(*main_copy(m))
            for slot in range(2 * MICRO):
                sent(rcv_a.at[slot], sta_s.at[slot])

        @pl.when(me_p == 1)
        def _():
            fetch_narrow(n2 // W)

            def first(m, c):
                arrived(rbig.at[m, pl.ds(0, IN)], big_r.at[m])
                col[:, m] = dot(p2[...], rbig[m, pl.ds(0, IN), :]).astype(BF).reshape(9, OUT, W)
                total = dot(col[0, m], wbuf[pl.ds(0, C_MID), :])
                for tap in range(1, 9):
                    total += dot(col[tap, m], wbuf[pl.ds(tap * C_MID, C_MID), :])
                fw[0, pl.ds(pl.multiple_of(m * OUT, CH), OUT), :] = total

                def sums(b, f, bc, vc):
                    u = fw[0, at(m, f), :]
                    return (u, u * u)

                put(own_a, m, reduce_rows(1, runs_out, sums, 2))
                send_a(m)
                finish_norm(total_a(m), m, 0, count_out)

                def act(b, f, bc, vc):
                    n = normed(fw[0, at(m, f), :], m, bc)
                    ssm[m, rows(f), :] = kept(n * sigmoid(n), m, bc).astype(BF)

                map_rows(1, runs_out, act)
                push(ssm.at[m], rsm.at[my_m], sm_s.at[m], sm_r.at[my_m], 2, m * G + my_c)
                return c

            lax.fori_loop(0, MICRO, first, 0)

            def second(m, c):
                arrived(rsm.at[m], sm_r.at[m])

                def sums(b, f, bc, vc):
                    u = fw[0, at(m, f), :]
                    d = kept(rsm[m, rows(f), :].astype(F32) * slope_of(normed(u, m, bc)), m, bc)
                    fw[1, at(m, f), :] = d
                    return (d, d * centered(u, m, bc))

                put(own_a, MICRO + m, reduce_rows(1, runs_out, sums, 2))
                send_a(MICRO + m)
                total = total_a(MICRO + m)
                finish_back(total, 0, count_out, 1)
                add_norm_grads(0, total)

                def grad(b, f, bc, vc):
                    z = centered(fw[0, at(m, f), :], m, bc)
                    dwide[0, at(m, f), :] = back(fw[1, at(m, f), :], z, 0, 0, m, bc, vc)

                map_rows(1, runs_out, grad)
                du = dwide[0, pl.ds(pl.multiple_of(m * OUT, CH), OUT), :]
                for tap in range(9):
                    tgb[tap, pl.ds(0, OUT), :] = dot_nt(du, wbuf[pl.ds(tap * C_MID, C_MID), :]).astype(BF)
                taps = tgb[:, pl.ds(0, OUT), :].reshape(9 * OUT, W)
                stage[m, pl.ds(0, IN), :] = dot(p2t[...], taps).astype(BF)
                push(stage.at[m, pl.ds(0, IN)], rbig.at[m, pl.ds(0, IN)], big_s.at[m], big_r.at[m], 0, me_d)
                return c

            lax.fori_loop(0, MICRO, second, 0)

            def weights(tap, c):
                grad = dot_tn(col[tap].reshape(ROWS, W), dwide[0, pl.ds(0, ROWS), :])
                keep_narrow(tap * C_MID, grad)
                return c

            lax.fori_loop(0, 9, weights, 0)
            reduce_scatter(n2 * LANES)
            for m in range(MICRO):
                pushed(stage.at[m, pl.ds(0, IN)], rbig.at[m, pl.ds(0, IN)], big_s.at[m], big_r.at[m], 0, me_d)
                pushed(ssm.at[m], rsm.at[my_m], sm_s.at[m], sm_r.at[my_m], 2, m * G + my_c)
            for slot in range(2 * MICRO):
                sent(rcv_a.at[slot], sta_s.at[slot])

        def share_norm_grads():
            ngs[...] = ng_o[...]
            for k in range(1, MICRO):
                remote(
                    ngs, ngr.at[k - 1], stn_s.at[k - 1], stn_r.at[k - 1], me_p, lax.rem(me_d + k * G, R)
                ).start()
            for k in range(1, MICRO):
                arrived(ngr.at[k - 1], stn_r.at[k - 1])
                ng_o[...] += ngr[k - 1]
            for k in range(1, MICRO):
                sent(ngs, stn_s.at[k - 1])

        def sub_copy(m):
            return (col.at[pl.ds(4, 2), m], col.at[pl.ds(0, 2), my_m], xs_s.at[m], xs_r.at[my_m], 2, m * G + my_c)

        def sub_back(k):
            return (col.at[pl.ds(6, 2), k], srecv, sb_s.at[k], sb_r, my_m, k * G + my_c)

        @pl.when(me_p == 2)
        def _():
            load(x_h, xb.at[:, pl.ds(0, IN)], 0).wait()

            def send_x(m, c):
                for h in range(2):
                    col[4 + h, m] = dot(ps[...], xb[2 * m + h, pl.ds(0, IN), :]).astype(BF)
                push(*sub_copy(m))
                return c

            lax.fori_loop(0, MICRO, send_x, 0)
            fetch_wide(0, n3 // W, lambda q, r: q * n3 + r)
            for k in range(MICRO):
                arrived(col.at[pl.ds(0, 2), k], xs_r.at[k])

            def w3(q):
                return wbuf[pl.ds(pl.multiple_of(q * n3, C_MID), C_MID), :]

            def wp(q, h):
                return wbuf[pl.ds(pl.multiple_of(q * n3 + C_MID + h * W, W), W), :]

            def xsub(h):
                return col[h].reshape(ROWS, W)

            def product(index, value, slot):
                fw[index, pl.ds(0, ROWS), :] = value

                def sums(b, f, bc, vc):
                    u = fw[index, at(b, f), :]
                    return (u, u * u)

                put(own_b, slot, reduce_rows(MICRO, runs_out, sums, 2))
                send_b(slot)

            def short(q, c):
                product(NQ + q, dot(xsub(0), wp(q, 0)) + dot(xsub(1), wp(q, 1)), NQ + q)
                return c

            lax.fori_loop(0, NQ, short, 0)
            for k in range(MICRO):
                arrived(rsm.at[k], sm_r.at[k])

            def main(q, c):
                product(q, dot(rsm[...].reshape(ROWS, W), w3(q)), q)
                return c

            lax.fori_loop(0, NQ, main, 0)

            def join(q, c):
                finish_norm(total_b(NQ + q), NQ + q, NQ + q, count_out)
                finish_norm(total_b(q), q, q, count_out)

                def act(b, f, bc, vc):
                    n = normed(fw[q, at(b, f), :], q, bc) + normed(fw[NQ + q, at(b, f), :], NQ + q, bc)
                    stage[q, at(b, f), :] = (n * sigmoid(n)).astype(BF)

                map_rows(MICRO, runs_out, act)
                push(stage.at[q, pl.ds(0, ROWS)], rbig.at[q, pl.ds(0, ROWS)], big_s.at[q], big_r.at[q], 3, me_d)
                return c

            lax.fori_loop(0, NQ, join, 0)

            def slopes(q, c):
                arrived(rbig.at[q, pl.ds(0, ROWS)], big_r.at[q])

                def sums(b, f, bc, vc):
                    um, us = fw[q, at(b, f), :], fw[NQ + q, at(b, f), :]
                    n = normed(um, q, bc) + normed(us, NQ + q, bc)
                    d = rbig[q, at(b, f), :].astype(F32) * slope_of(n)
                    fw[2 * NQ, at(b, f), :] = d
                    return (d, d * centered(um, q, bc), d * centered(us, NQ + q, bc))

                put(own_b, 2 * NQ + q, reduce_rows(MICRO, runs_out, sums, 3))
                send_b(2 * NQ + q)
                total = total_b(2 * NQ + q)
                finish_back(total, 0, count_out, 2)
                for g in (0, 1):
                    ng_o[q, pl.ds(2 * g, 1), :] = total[3 * g + 1 : 3 * g + 2]
                    ng_o[q, pl.ds(2 * g + 1, 1), :] = total[3 * g : 3 * g + 1]
                    ng_o[NQ + q, pl.ds(2 * g, 1), :] = total[3 * g + 2 : 3 * g + 3]
                    ng_o[NQ + q, pl.ds(2 * g + 1, 1), :] = total[3 * g : 3 * g + 1]

                def grad(b, f, bc, vc):
                    d = fw[2 * NQ, at(b, f), :]
                    zm = centered(fw[q, at(b, f), :], q, bc)
                    zs = centered(fw[NQ + q, at(b, f), :], NQ + q, bc)
                    dwide[q, at(b, f), :] = back(d, zm, 0, 0, q, bc, vc)
                    dwide[NQ + q, at(b, f), :] = back(d, zs, 0, 1, NQ + q, bc, vc)

                map_rows(MICRO, runs_out, grad)
                da = dot_nt(dwide[q, pl.ds(0, ROWS), :], w3(q))

                @pl.when(q == 0)
                def _():
                    fw[2 * NQ + 1, pl.ds(0, ROWS), :] = da

                @pl.when(q > 0)
                def _():
                    fw[2 * NQ + 1, pl.ds(0, ROWS), :] += da

                return c

            lax.fori_loop(0, NQ, slopes, 0)

            def back_a2(k, c):
                block = fw[2 * NQ + 1, pl.ds(pl.multiple_of(k * OUT, CH), OUT), :]
                ssm[k] = block.astype(BF)
                push(ssm.at[k], rsm_back(k), sm_s.at[k], sm_r.at[my_m], 1, k * G + my_c)
                return c

            def rsm_back(k):
                return rsm.at[my_m]

            lax.fori_loop(0, MICRO, back_a2, 0)

            for m in range(MICRO):
                pushed(*sub_copy(m))
            for h in range(C_IN // W):
                SUB = 2 * NQ + 2
                for q in range(NQ):
                    piece = dot_nt(dwide[NQ + q, pl.ds(0, ROWS), :], wp(q, h))
                    if q == 0:
                        fw[SUB, pl.ds(0, ROWS), :] = piece
                    else:
                        fw[SUB, pl.ds(0, ROWS), :] += piece
                for k in range(MICRO):
                    col[6 + h, k] = fw[SUB, pl.ds(k * OUT, OUT), :].astype(BF)
            for k in range(MICRO):
                push(*sub_back(k))

            keep_wide(0, lambda r: rsm[:, :, r].reshape(ROWS, HALF), 0)
            for h in range(2):
                keep_wide((h + 1) * W, lambda r, h=h: col[h, :, :, r].reshape(ROWS, HALF), NQ)
            share_norm_grads()
            reduce_scatter(n3 * NQ * LANES)
            for k in range(MICRO):
                pushed(ssm.at[k], rsm_back(k), sm_s.at[k], sm_r.at[my_m], 1, k * G + my_c)
                pushed(*sub_back(k))
            for q in range(NQ):
                pushed(stage.at[q, pl.ds(0, ROWS)], rbig.at[q, pl.ds(0, ROWS)], big_s.at[q], big_r.at[q], 3, me_d)
            for slot in range(3 * NQ):
                sent(rcv_b.at[slot], stb_s.at[slot])

        def block(k):
            return pl.ds(pl.multiple_of(k * OUT, CH), OUT)

        def cot_copy(m):
            return (cot_h.at[m], xb.at[pl.ds(0, NQ), block(my_m)], ct_s.at[m], ct_r.at[my_m], 3, m * G + my_c)

        def gate_copy(m):
            return (gate_v.at[m], gateb.at[my_m], gt_s.at[m], gt_r.at[my_m], 3, m * G + my_c)

        def out_copy(k):
            return (xb.at[pl.ds(NQ, NQ), block(k)], out_h, out_s.at[k], out_r, my_m, k * G + my_c)

        @pl.when(me_p == 3)
        def _():
            for m in range(MICRO):
                push(*gate_copy(m))
                push(*cot_copy(m))
            fetch_narrow(nab // W)
            fetch_wide(nab * W // C_OUT, 1, lambda q, r: nab + q * C_MID)
            A, B, T1, T2 = 2 * NQ, 2 * NQ + 1, 2 * NQ + 2, 2 * NQ + 3
            DB, DA, H1, H2 = NQ, NQ + 1, NQ + 2, NQ + 3
            full = pl.ds(0, ROWS)

            def wa(q):
                return wbuf[pl.ds(pl.multiple_of(q * W, W), W), :]

            def wb(tap):
                return wbuf[pl.ds(pl.multiple_of(C_OUT + tap * C_MID, C_MID), C_MID), :]

            def wc(q):
                return wbuf[pl.ds(pl.multiple_of(nab + q * C_MID, C_MID), C_MID), :]

            def accumulate(index, i, value):
                @pl.when(i == 0)
                def _():
                    fw[index, full, :] = value

                @pl.when(i > 0)
                def _():
                    fw[index, full, :] += value

            def begin(index, slot):
                def sums(b, f, bc, vc):
                    u = fw[index, at(b, f), :]
                    return (u, u * u)

                put(own_b, slot, reduce_rows(MICRO, runs_out, sums, 2))
                send_b(slot)

            def hidden(index, slot, target):
                def act(b, f, bc, vc):
                    n = normed(fw[index, at(b, f), :], slot, bc)
                    dwide[target, at(b, f), :] = kept(n * sigmoid(n), my_m, bc).astype(BF)

                map_rows(MICRO, runs_out, act)

            def gather(source, target):
                def one(k, c):
                    block = dwide[source, pl.ds(pl.multiple_of(k * OUT, CH), OUT), :]
                    target(k, dot(pb[...], block).astype(BF).reshape(9, OUT, W))
                    return c

                lax.fori_loop(0, MICRO, one, 0)

            def narrow(q, c):
                arrived(rbig.at[q, full], big_r.at[q])
                accumulate(A, q, dot(rbig[q, full, :], wa(q)))
                return c

            lax.fori_loop(0, NQ, narrow, 0)
            begin(A, 0)
            finish_norm(total_b(0), 0, 0, count_out)
            hidden(A, 0, H1)

            def to_col(k, v):
                col[:, k] = v

            gather(H1, to_col)

            def conv(tap, c):
                accumulate(B, tap, dot(col[tap].reshape(ROWS, W), wb(tap)))
                return c

            lax.fori_loop(0, 9, conv, 0)
            begin(B, 1)
            finish_norm(total_b(1), 1, 1, count_out)
            hidden(B, 1, H2)

            def widen(q, c):
                fw[q, full, :] = dot(dwide[H2, full, :], wc(q))
                begin(q, 2 + q)
                return c

            lax.fori_loop(0, NQ, widen, 0)
            for k in range(MICRO):
                arrived(gateb.at[k], gt_r.at[k])
                arrived(xb.at[pl.ds(0, NQ), block(k)], ct_r.at[k])

            def gate_at(b, f):
                g = gateb[b, rows(f), :]
                return jnp.concatenate([g] * (W // g.shape[1]), axis=1)

            def ends(q, c):
                finish_norm(total_b(2 + q), 2 + q, 2 + q, count_out)

                def sums(b, f, bc, vc):
                    u = fw[q, at(b, f), :]
                    g = gate_at(b, f)
                    v = rbig[q, at(b, f), :].astype(F32) + g * normed(u, 2 + q, bc)
                    sg = sigmoid(v)
                    xb[NQ + q, at(b, f), :] = (v * sg).astype(BF)
                    d = xb[q, at(b, f), :].astype(F32) * (sg * (1.0 + v * (1.0 - sg)))
                    fw[NQ + q, at(b, f), :] = d
                    d = g * d
                    return (d, d * centered(u, 2 + q, bc))

                put(own_b, 2 + NQ + q, reduce_rows(MICRO, runs_out, sums, 2))
                send_b(2 + NQ + q)
                return c

            lax.fori_loop(0, NQ, ends, 0)

            def ends_back(q, c):
                total = total_b(2 + NQ + q)
                finish_back(total, 0, count_out, 1)
                add_norm_grads(2 + q, total)

                def grad(b, f, bc, vc):
                    z = centered(fw[q, at(b, f), :], 2 + q, bc)
                    d = gate_at(b, f) * fw[NQ + q, at(b, f), :]
                    dwide[q, at(b, f), :] = back(d, z, 0, 0, 2 + q, bc, vc)

                map_rows(MICRO, runs_out, grad)
                accumulate(T1, q, dot_nt(dwide[q, full, :], wc(q)))
                return c

            lax.fori_loop(0, NQ, ends_back, 0)
            for k in range(MICRO):
                push(*out_copy(k))

            def middle(index, pslot, slot, target):
                def sums(b, f, bc, vc):
                    u = fw[index, at(b, f), :]
                    d = kept(fw[T1, at(b, f), :] * slope_of(normed(u, pslot, bc)), my_m, bc)
                    fw[T2, at(b, f), :] = d
                    return (d, d * centered(u, pslot, bc))

                put(own_b, slot, reduce_rows(MICRO, runs_out, sums, 2))
                send_b(slot)
                total = total_b(slot)
                finish_back(total, 0, count_out, 1)
                add_norm_grads(pslot, total)

                def grad(b, f, bc, vc):
                    z = centered(fw[index, at(b, f), :], pslot, bc)
                    dwide[target, at(b, f), :] = back(fw[T2, at(b, f), :], z, 0, 0, pslot, bc, vc)

                map_rows(MICRO, runs_out, grad)

            middle(B, 1, 2 + 2 * NQ, DB)

            def to_taps(k, v):
                tgb[:, pl.ds(pl.multiple_of(k * OUT, CH), OUT), :] = v

            gather(DB, to_taps)

            def conv_back(tap, c):
                accumulate(T1, tap, dot_nt(tgb[tap, full, :], wb(8 - tap)))
                return c

            lax.fori_loop(0, 9, conv_back, 0)
            middle(A, 0, 3 + 2 * NQ, DA)

            def to_y(q, c):
                grad = dot_nt(dwide[DA, full, :], wa(q)) + fw[NQ + q, full, :]
                stage[q, full, :] = grad.astype(BF)
                push(stage.at[q, full], rbig.at[q, full], big_s.at[q], big_r.at[q], 2, me_d)
                return c

            lax.fori_loop(0, NQ, to_y, 0)

            def weights_a(q, c):
                keep_narrow(q * W, dot_tn(rbig[q, full, :], dwide[DA, full, :]))
                return c

            def weights_b(tap, c):
                keep_narrow(C_OUT + tap * C_MID, dot_tn(col[tap].reshape(ROWS, W), dwide[DB, full, :]))
                return c

            lax.fori_loop(0, NQ, weights_a, 0)
            lax.fori_loop(0, 9, weights_b, 0)
            keep_wide(nab * W // C_OUT, lambda r: dwide[H2, full, r], 0)
            share_norm_grads()
            reduce_scatter((nab + NQ * C_MID) * LANES)
            for m in range(MICRO):
                pushed(*gate_copy(m))
                pushed(*cot_copy(m))
                pushed(*out_copy(m))
            for q in range(NQ):
                pushed(stage.at[q, full], rbig.at[q, full], big_s.at[q], big_r.at[q], 2, me_d)
            for slot in range(4 + 2 * NQ):
                sent(rcv_b.at[slot], stb_s.at[slot])

        arrived(srecv, sb_r)
        arrived(mrecv, mn_r)
        for h in range(2):
            dx_o[h] = (mrecv[h].astype(F32) + dot(pst[...], srecv[h])).astype(BF)
        arrived(out_h, out_r)

    return kernel


def solution(mesh):
    R, NP = mesh.shape["dp"], mesh.shape["pipe"]

    def on_device(x_big, x_small, cot_big, cot_small, section_weights, section_norms, gate_big, gate_small, width_step):
        MICRO = x_big.shape[0]
        G = R // MICRO
        geo = Geometry((x_big.shape[1], x_small.shape[1]), (x_big.shape[2], x_small.shape[2]))
        IN, OUT, ROWS = geo.IN, geo.OUT, MICRO * geo.OUT
        PW = section_weights.shape[1]
        NB = section_norms.shape[2] // W
        wide = max(IN, ROWS)

        def joined(big, small, width, length):
            parts = [v.reshape(MICRO, -1, width) for v in (big, small)]
            v = jnp.concatenate(parts, axis=1)
            return jnp.pad(v, ((0, 0), (0, length - v.shape[1]), (0, 0)))

        x = joined(x_big, x_small, C_IN, IN)
        x = x.reshape(MICRO, IN, 2, W).transpose(0, 2, 1, 3).reshape(2 * MICRO, IN, W)
        cot = joined(cot_big, cot_small, C_OUT, OUT).reshape(MICRO, OUT, NQ, W).transpose(0, 2, 1, 3)
        gates = [
            jnp.repeat(g.astype(F32), (v.shape[2]) ** 2, axis=1)
            for g, v in ((gate_big, cot_big), (gate_small, cot_small))
        ]
        gate = joined(gates[0][..., None], gates[1][..., None], 1, OUT)
        gate = jnp.broadcast_to(gate, (MICRO, OUT, 128))
        w4 = section_weights.reshape(PW // W, LANES, 1, 128)
        w16 = section_weights.reshape(PW // C_OUT, NQ * LANES, 1, 128)
        SR = PW // 128 // R
        PC = 4 if SR % (4 * CH) == 0 else 2 if SR % (2 * CH) == 0 else 1
        PR = SR // PC
        nt = section_norms[0].reshape(4, NB, W).transpose(1, 0, 2)
        keep = (jnp.arange(C_MID)[None] < C_MID * width_step[:, None] // 4).astype(F32)[:, None]
        p2 = geo.windows(2)
        sub = geo.every_second()
        consts = [p2, p2.T, geo.windows(1), sub, sub.T]
        consts = [jnp.asarray(c, BF) for c in consts]
        vmem, hbm = pl.BlockSpec(memory_space=pltpu.VMEM), pl.BlockSpec(memory_space=pl.ANY)
        V, D = pltpu.VMEM, pltpu.SemaphoreType.DMA
        out, dx, dw, ng = pl.pallas_call(
            make_kernel(geo, R, NP, MICRO, SR, PC),
            out_shape=(
                jax.ShapeDtypeStruct((NQ, OUT, W), BF),
                jax.ShapeDtypeStruct((2, IN, W), BF),
                jax.ShapeDtypeStruct((SR, 128), F32),
                jax.ShapeDtypeStruct((NB, 8, W), F32),
            ),
            in_specs=[hbm, hbm, vmem, hbm, hbm, vmem, vmem] + [vmem] * 5,
            out_specs=(hbm, vmem, vmem, vmem),
            scratch_shapes=[
                V((PW // W, W), BF),
                V((2, LANES, W, 1, 128), BF),
                V((2 * MICRO, wide, W), BF),
                V((MICRO, OUT, 128), F32),
                V((NQ, wide, W), BF),
                V((NQ, wide, W), BF),
                V((MICRO, OUT, W), BF),
                V((MICRO, OUT, W), BF),
                V((2 * NQ + 4, wide, W), F32),
                V((2 * NQ, wide, W), BF),
                V((9, MICRO, OUT, W), BF),
                V((9, wide, W), BF),
                V((HALF * NQ * LANES, 128), F32),
                V((2, IN, W), BF),
                V((2, OUT, W), BF),
                V((PW // 128, 128), BF),
                V((R // 2, PC, PR, 128), BF),
                V((R // 2 + 1, PC, PR, 128), BF),
                V((2 * MICRO, 4, W), F32),
                V((2 * MICRO, R - 1, 4, W), F32),
                V((3 * NQ, 8, W), F32),
                V((3 * NQ, G - 1, 8, W), F32),
                V((8, 8, W), F32),
                V((1, 8, W), F32),
                V((NB, 8, W), F32),
                V((MICRO - 1, NB, 8, W), F32),
                D((1,)),
                D((2, LANES)),
                D((4,)), D((4,)),
                D((4,)), D((4,)),
                D((4,)), D((4,)),
                D((4,)), D((4,)),
                D((4,)), D((4,)),
                D((4,)), D,
                D((4,)), D,
                D((4,)), D,
                D((2 * MICRO,)), D((2 * MICRO,)),
                D((3 * NQ,)), D((3 * NQ,)),
                D((MICRO - 1,)), D((MICRO - 1,)),
                D((R // 2, PC)), D((R // 2, PC)),
                D((R // 2, PC)), D((R // 2 + 1, PC)),
            ],
            compiler_params=pltpu.CompilerParams(
                collective_id=0, has_side_effects=True, vmem_limit_bytes=63 << 20
            ),
        )(x, cot, gate, w4, w16, nt, keep, *consts)

        def crops(v, width, side_of):
            nb, sb = geo.crops[0], side_of(geo.sides[0])
            ns, ss = geo.crops[1], side_of(geo.sides[1])
            cut = nb * sb * sb
            return (
                v[:cut].reshape(1, nb, sb, sb, width),
                v[cut : cut + ns * ss * ss].reshape(1, ns, ss, ss, width),
            )

        out_big, out_small = crops(out.transpose(1, 0, 2).reshape(OUT, C_OUT), C_OUT, lambda s: s // 2)
        grad_big, grad_small = crops(dx.transpose(1, 0, 2).reshape(IN, C_IN), C_IN, lambda s: s)
        weight = dw.reshape(1, PW // R)
        norm = ng[:, :4].transpose(1, 0, 2).reshape(1, 4, NB * W)
        return out_big, out_small, grad_big, grad_small, weight, norm

    images = P(None, "dp", None, None, None)
    ends = P("pipe", "dp", None, None, None)
    return jax.shard_map(
        on_device,
        mesh=mesh,
        in_specs=(images,) * 4 + (P("pipe", None), P("pipe", None, None), P(None, "dp"), P(None, "dp"), P()),
        out_specs=(ends,) * 4 + (P("pipe", "dp"), P("pipe", None, None)),
        check_vma=False,
    )
```

```python
import functools

import jax
import jax.numpy as jnp
import numpy as np
from jax import lax
from jax.experimental import pallas as pl
from jax.experimental.pallas import tpu as pltpu
from jax.sharding import PartitionSpec as P

C_IN = 1024
C_MID = 512
C_OUT = 2048
EPS = 1e-05
W = 512
NQ = C_OUT // W
CH = 16
LANES = W // 128
HALF = W // 2
BF = jnp.bfloat16
F32 = jnp.float32
MESH = pl.DeviceIdType.MESH


def up16(n):
    return -(-n // 16) * 16


class Geometry:
    def __init__(self, crops, sides):
        self.crops, self.sides = crops, sides
        self.in_big = crops[0] * sides[0] ** 2
        self.in_all = self.in_big + crops[1] * sides[1] ** 2
        self.out_big = crops[0] * (sides[0] // 2) ** 2
        self.out_all = self.out_big + crops[1] * (sides[1] // 2) ** 2
        self.IN, self.OUT = up16(self.in_all), up16(self.out_all)

    def pixels(self, halves):
        index, table = 0, {}
        for group in (0, 1):
            side = self.sides[group] // 2 if halves else self.sides[group]
            crops, sides = range(self.crops[group]), range(side)
            if group == 0:
                places = [(crop, r, c) for crop in crops for r in sides for c in sides]
            else:
                places = [(crop, r, c) for r in sides for c in sides for crop in crops]
            for place in places:
                table[(group,) + place] = index
                index += 1
        return table

    def windows(self, stride):
        ins, outs = self.pixels(stride == 1), self.pixels(True)
        picks = np.zeros((9, self.OUT, self.OUT if stride == 1 else self.IN), np.float32)
        for (group, crop, r, c), row in outs.items():
            for tap in range(9):
                at = (group, crop, stride * r + tap // 3 - 1, stride * c + tap % 3 - 1)
                if at in ins:
                    picks[tap, row, ins[at]] = 1.0
        return picks.reshape(9 * self.OUT, -1)

    def every_second(self):
        ins, outs = self.pixels(False), self.pixels(True)
        picks = np.zeros((self.OUT, self.IN), np.float32)
        for (group, crop, r, c), row in outs.items():
            picks[row, ins[group, crop, 2 * r, 2 * c]] = 1.0
        return picks


def dot(a, b):
    return jnp.dot(a, b, preferred_element_type=F32)


def dot_nt(a, b):
    return lax.dot_general(a, b, (((1,), (1,)), ((), ())), preferred_element_type=F32)


def dot_tn(a, b):
    return lax.dot_general(a, b, (((0,), (0,)), ((), ())), preferred_element_type=F32)


def sigmoid(v):
    return 0.5 * jnp.tanh(0.5 * v) + 0.5


def slope_of(v):
    s = sigmoid(v)
    return s * (1.0 + v * (1.0 - s))


def runs_of(n_big, n_all, rows):
    runs = []
    for first in range(0, rows, CH):
        kind = (min(max(n_big - first, 0), CH), min(max(n_all - first, 0), CH))
        if runs and runs[-1][2:] == kind:
            runs[-1] = (runs[-1][0], runs[-1][1] + 1) + kind
        else:
            runs.append((first, 1) + kind)
    return runs


def row_ids():
    return lax.broadcasted_iota(jnp.int32, (CH, W), 0)


def part(v, low, high):
    if low >= high:
        return None
    if low == 0 and high == CH:
        return v
    r = row_ids()
    return jnp.where((r >= low) & (r < high), v, 0.0)


def pick(vb, vs, bc):
    if bc == CH:
        return vb
    if bc == 0:
        return vs
    return jnp.where(row_ids() < bc, vb, vs)


def each_step(blocks, runs, body, carry):
    def one_block(b, carry):
        for first, length, bc, vc in runs:
            if length == 1:
                carry = body(b, first, bc, vc, carry)
            else:
                carry = lax.fori_loop(
                    0,
                    length,
                    lambda i, c: body(b, pl.multiple_of(first + CH * i, CH), bc, vc, c),
                    carry,
                    unroll=min(length, 4) if length % min(length, 4) == 0 else 1,
                )
        return carry

    if blocks == 1:
        return one_block(0, carry)
    return lax.fori_loop(0, blocks, one_block, carry)


def reduce_rows(blocks, runs, fn, count):
    def body(b, first, bc, vc, carry):
        values = fn(b, first, bc, vc)
        new = []
        for i, v in enumerate(values):
            for g, piece in enumerate((part(v, 0, bc), part(v, bc, vc))):
                total = carry[g * count + i]
                new.append((g * count + i, total if piece is None else total + piece[:8] + piece[8:]))
        return tuple(v for _, v in sorted(new, key=lambda t: t[0]))

    zero = jnp.zeros((8, W), F32)
    totals = each_step(blocks, runs, body, (zero,) * (2 * count))
    return [jnp.sum(t, axis=0, keepdims=True) for t in totals]


def map_rows(blocks, runs, fn):
    def body(b, first, bc, vc, carry):
        fn(b, first, bc, vc)
        return carry

    each_step(blocks, runs, body, 0)


def make_kernel(geo, R, NP, MICRO, SR, PC):
    G = R // MICRO
    N = R // 2
    PR = SR // PC
    RW = SR // (NQ * LANES)
    PRQ = up16(RW * LANES)
    IN, OUT = geo.IN, geo.OUT
    ROWS = MICRO * OUT
    runs_in = runs_of(geo.in_big, geo.in_all, IN)
    runs_out = runs_of(geo.out_big, geo.out_all, OUT)
    count_in = (float(R * geo.in_big), float(R * (geo.in_all - geo.in_big)))
    count_out = (float(R * geo.out_big), float(R * (geo.out_all - geo.out_big)))
    RA, RB = radix(R, 8), radix(G, 4)
    n1 = C_IN
    n2 = 9 * C_MID
    n3 = C_MID + C_IN
    nab = C_OUT + 9 * C_MID
    nabc = nab + C_OUT
    S2 = -(-n3 // RW)

    def kernel(
        x_h, cot_h, gate_big, gate_small, width_step, w4_h, w16_h, nt, p2, pb, ps,
        ob_o, os_o, gb_o, gs_o, dw_o, ng_o,
        wbuf, raw, xb, gate_v, gateb, keep, stage, rbig, ssm, rsm, fw, dwide, col, tgb, tmp, mrecv, srecv, orecv,
        dwl, pbuf, rv, nt2,
        own_a, rcv_a, mid_a, out_a, own_b, rcv_b, mid_b, out_b, par, cof, ngs, ngr,
        ld, raw_s, big_s, big_r, sm_s, sm_t, sm_r, up_s, up_r, xs_s, xs_r, ct_s, ct_r, gt_s, gt_r, w_s, w_r, nt_s, nt_r,
        out_s, out_r, mn_s, mn_r, sb_s, sb_r, sta_s, sta_r, stc_s, stc_r, stb_s, stb_r, std_s, std_r, stn_s, stn_r,
        pa_s, pa_r, ch_s, ch_r,
    ):
        me_p, me_d = lax.axis_index("pipe"), lax.axis_index("dp")
        my_m, my_c = me_d // G, me_d % G
        core = lax.rem(me_d, 2)
        sibling = me_d + 1 - 2 * core
        full = pl.ds(0, ROWS)

        def remote(src, dst, ss, rs, p, d):
            return pltpu.make_async_remote_copy(
                src_ref=src, dst_ref=dst, send_sem=ss, recv_sem=rs, device_id=(p, d), device_id_type=MESH
            )

        def push(src, dst, ss, rs, p, d):
            here = (me_p == p) & (me_d == d)

            @pl.when(here)
            def _():
                pltpu.make_async_copy(src, dst, rs).start()

            @pl.when(jnp.logical_not(here))
            def _():
                remote(src, dst, ss, rs, p, d).start()

        def pushed(src, dst, ss, rs, p, d):
            @pl.when(jnp.logical_not((me_p == p) & (me_d == d)))
            def _():
                remote(src, dst, ss, rs, p, d).wait_send()

        def arrived(dst, rs):
            remote(dst, dst, rs, rs, me_p, me_d).wait_recv()

        def sent(src, ss):
            remote(src, src, ss, ss, me_p, me_d).wait_send()

        def spread_out(src, target, ss, rs, base, place, step, count):
            def one(k, c):
                peer = base + step * lax.rem(place + k, count)
                remote(src, target.at[k - 1], ss, rs, me_p, peer).start()
                return c

            lax.fori_loop(1, count, one, 0, unroll=count <= 8)

        def gather_up(first, received, count):
            return lax.fori_loop(0, count - 1, lambda k, t: t + received[k], first, unroll=count <= 8)

        def summer(own, rcv, mid, out, s1, r1, s2, r2, base, place, count, inner):
            low, high = lax.rem(place, inner), place // inner
            outer = count // inner

            def send(slot):
                spread_out(own.at[slot], rcv.at[slot], s1.at[slot], r1.at[slot], base + high * inner, low, 1, inner)

            def total(slot):
                arrived(rcv.at[slot], r1.at[slot])
                sums = gather_up(own[slot], rcv.at[slot], inner)
                if outer > 1:
                    mid[slot] = sums
                    spread_out(mid.at[slot], out.at[slot], s2.at[slot], r2.at[slot], base + low, high, inner, outer)
                    arrived(out.at[slot], r2.at[slot])
                    sums = gather_up(sums, out.at[slot], outer)
                return sums

            def drain(slot):
                sent(rcv.at[slot], s1.at[slot])
                if outer > 1:
                    sent(out.at[slot], s2.at[slot])

            return send, total, drain

        send_a, total_a, drain_a = summer(
            own_a, rcv_a, mid_a, out_a, sta_s, sta_r, stc_s, stc_r, 0, me_d, R, RA
        )
        send_b, total_b, drain_b = summer(
            own_b, rcv_b, mid_b, out_b, stb_s, stb_r, std_s, std_r, my_m * G, my_c, G, RB
        )

        def put(ref, slot, sums):
            for i, s in enumerate(sums):
                ref[slot, pl.ds(i, 1), :] = s

        def finish_norm(total, slot, table, cb, counts):
            for g in (0, 1):
                mean = total[2 * g : 2 * g + 1] * (1.0 / counts[g])
                var = total[2 * g + 1 : 2 * g + 2] * (1.0 / counts[g]) - mean * mean
                rstd = lax.rsqrt(var + EPS)
                scale = rstd * table[cb, 2 * g : 2 * g + 1, :]
                par[slot, pl.ds(4 * g, 1), :] = mean
                par[slot, pl.ds(4 * g + 1, 1), :] = rstd
                par[slot, pl.ds(4 * g + 2, 1), :] = scale
                par[slot, pl.ds(4 * g + 3, 1), :] = table[cb, 2 * g + 1 : 2 * g + 2, :] - mean * scale

        def param(slot, i, bc):
            return pick(par[slot, pl.ds(i, 1), :], par[slot, pl.ds(4 + i, 1), :], bc)

        def normed(u, slot, bc):
            return u * param(slot, 2, bc) + param(slot, 3, bc)

        def centered(u, slot, bc):
            return (u - param(slot, 0, bc)) * param(slot, 1, bc)

        def put_cof(slot, total, counts):
            for g in (0, 1):
                cof[slot, pl.ds(2 * g, 2), :] = total[2 * g : 2 * g + 2] * (1.0 / counts[g])

        def back(d, z, cslot, zslot, pslot, bc, vc):
            a = pick(cof[cslot, pl.ds(0, 1), :], cof[cslot, pl.ds(2, 1), :], bc)
            b = pick(cof[zslot, pl.ds(1, 1), :], cof[zslot, pl.ds(3, 1), :], bc)
            du = param(pslot, 2, bc) * (d - a - z * b)
            return (du if vc == CH else part(du, 0, vc) if vc else jnp.zeros_like(du)).astype(BF)

        def kept(v, m, bc):
            return v if bc == CH else v * pick(jnp.ones((1, W), F32), keep[m], bc)

        def rows(first, n=CH):
            return pl.ds(first, n)

        def at(b, first):
            return pl.ds(pl.multiple_of(b * OUT + first, CH), CH)

        def block(k):
            return pl.ds(pl.multiple_of(k * OUT, CH), OUT)

        def weight(first):
            return wbuf[pl.ds(pl.multiple_of(first, W), W), :]

        def squares(load):
            def sums(b, f, bc, vc):
                u = load(b, f)
                return (u, u * u)

            return sums

        def add_norm_grads(ref, cb, total):
            for g in (0, 1):
                ref[cb, pl.ds(2 * g, 1), :] += total[2 * g + 1 : 2 * g + 2]
                ref[cb, pl.ds(2 * g + 1, 1), :] += total[2 * g : 2 * g + 1]

        HW = raw.shape[2]

        def fetch(count, source, target):
            def copies(b, slot):
                return [
                    pltpu.make_async_copy(source(b, lane), raw.at[slot, lane], raw_s.at[slot, lane])
                    for lane in range(LANES)
                ]

            for copy in copies(0, 0):
                copy.start()

            def one(b, c):
                slot = lax.rem(b, 2)

                @pl.when(b + 1 < count)
                def _():
                    for copy in copies(b + 1, 1 - slot):
                        copy.start()

                for lane, copy in enumerate(copies(b, slot)):
                    copy.wait()
                    values = raw[slot, lane, :, 0, :].astype(F32).astype(BF)
                    wbuf[pl.ds(pl.multiple_of(target(b), HW), HW), pl.ds(lane * 128, 128)] = values
                return c

            lax.fori_loop(0, count, one, 0)

        def fetch_narrow(count):
            fetch(count // HW, lambda b, lane: w4_h.at[pl.ds(b * HW, HW), lane], lambda b: b * HW)

        def fetch_wide(first, count, target):
            per = count // HW
            fetch(
                NQ * per,
                lambda b, lane: w16_h.at[pl.ds(first + lax.rem(b, per) * HW, HW), b // per * LANES + lane],
                lambda b: target(b // per) + lax.rem(b, per) * HW,
            )

        def ship(source, target, q):
            return remote(wbuf.at[pl.ds(source(q), W)], wbuf.at[pl.ds(target(q), W)], w_s.at[q], w_r.at[q], me_p + 1, me_d)

        def ship_all(source, target, count, go):
            for i in range(count // 2):
                go(ship(source, target, core * (count // 2) + i))

        def pass_on(target, count, go):
            for i in range(count // 2):
                q = core * (count // 2) + i
                ref = wbuf.at[pl.ds(target(q), W)]
                go(ref, q, remote(ref, ref, w_s.at[q], w_r.at[q], me_p, sibling))

        def take(target, count):
            def first(ref, q, copy):
                arrived(ref, w_r.at[q])
                copy.start()

            pass_on(target, count, first)
            for i in range(count // 2):
                q = (1 - core) * (count // 2) + i
                arrived(wbuf.at[pl.ds(target(q), W)], w_r.at[q])

        def w1_at(q):
            return pl.multiple_of(n2 + q * W, W)

        def w3_at(q):
            return pl.multiple_of(nabc + q * W, W)

        def lay_narrow(first, grad):
            for lane in range(LANES):
                tmp[pl.ds(first + lane, W, stride=LANES), :] = grad[:, lane * 128 : (lane + 1) * 128]

        def keep_narrow(first, grad):
            lay_narrow(0, grad)
            start = pl.multiple_of(first * LANES, W)
            dwl[pl.ds(start, W * LANES), :] = tmp[pl.ds(0, W * LANES), :].astype(BF)

        def keep_wide(first, lhs, index):
            step = NQ * LANES
            for half in range(W // HALF):
                for q in range(NQ):
                    grad = dot_tn(lhs(pl.ds(half * HALF, HALF)), dwide[index + q, full, :])
                    for lane in range(LANES):
                        part_of = grad[:, lane * 128 : (lane + 1) * 128]
                        tmp[pl.ds(q * LANES + lane, HALF, stride=step), :] = part_of
                dwl[pl.ds((first + half * HALF) * step, HALF * step), :] = tmp[pl.ds(0, HALF * step), :].astype(BF)

        class Reduction:
            def __init__(self, pieces, rows_of, start, used):
                self.pieces, self.rows_of, self.start, self.used = pieces, rows_of, start, used
                self.step = next(a for a in (64, 48, 32, 16) if rows_of % a == 0)
                self.i = me_d // 2

            def at(self, pc):
                return pl.ds(pc * self.rows_of, self.rows_of)

            def pair(self, t, pc):
                src = dwl.at[pl.ds(pl.multiple_of(self.start(2 * t + 1 - core, pc), CH), self.rows_of)]
                return remote(src, pbuf.at[t, self.at(pc)], pa_s.at[t, pc], pa_r.at[t, pc], me_p, sibling)

            def rightward(self, t, pc):
                ref = rv.at[t, self.at(pc)]
                return remote(ref, ref, ch_s.at[t, pc], ch_r.at[t, pc], me_p, me_d + 2)

            def leftward(self, t, pc):
                slot = jnp.where(t == self.i - 1, N, t)
                src, dst = rv.at[t, self.at(pc)], rv.at[slot, self.at(pc)]
                return remote(src, dst, ch_s.at[t, pc], ch_r.at[slot, pc], me_p, me_d - 2)

            def add(self, t, pc, others, store):
                first, step = self.start(2 * t + core, pc), self.step

                def one(s, c):
                    at_s = pl.ds(pl.multiple_of(pc * self.rows_of + s * step, CH), step)
                    v = dwl[pl.ds(pl.multiple_of(first + s * step, CH), step), :].astype(F32)
                    v += pbuf[t, at_s, :].astype(F32)
                    for slot in others:
                        v += rv[slot, at_s, :].astype(F32)
                    store(at_s, s, v)
                    return c

                lax.fori_loop(0, self.rows_of // step, one, 0)

            def send_pairs(self, pcs, low=0, high=N):
                def one(j, c):
                    t = jnp.where(lax.rem(j, 2) == 0, high - 1 - j // 2, low + j // 2)
                    for pc in pcs:

                        @pl.when(self.used(2 * t + 1 - core, pc))
                        def _(pc=pc):
                            self.pair(t, pc).start()

                    return c

                lax.fori_loop(0, high - low, one, 0)

            def forward(self, t, pc, wanted, received, copy):
                def store(at_s, s, v):
                    rv[t, at_s, :] = v.astype(BF)

                @pl.when(wanted & self.used(2 * t + core, pc))
                def _():
                    self.pair(t, pc).wait_recv()
                    if received:
                        arrived(rv.at[t, self.at(pc)], ch_r.at[t, pc])
                    self.add(t, pc, (t,) if received else (), store)
                    copy(t, pc).start()

            def originate(self, pcs, low=0, high=N):
                def one(j, c):
                    right, left = high - 1 - j, low + j
                    for pc in pcs:
                        self.forward(right, pc, (self.i == 0) & (right > 0), False, self.rightward)
                        self.forward(left, pc, (self.i == N - 1) & (left < N - 1), False, self.leftward)
                    return c

                lax.fori_loop(0, high - low, one, 0)

            def relay(self, pcs, low=0, high=N):
                def one(j, c):
                    right, left = high - 1 - j, low + j
                    for pc in pcs:
                        self.forward(right, pc, (self.i > 0) & (right > self.i), True, self.rightward)
                        self.forward(left, pc, (self.i < N - 1) & (left < self.i), True, self.leftward)
                    return c

                lax.fori_loop(0, high - low, one, 0)

            def finish(self, pc, store):
                i = self.i

                @pl.when(self.used(2 * i + core, pc))
                def _():
                    self.pair(i, pc).wait_recv()
                    for low, high in ((True, True), (True, False), (False, True)):

                        @pl.when(((i > 0) == low) & ((i < N - 1) == high))
                        def _(low=low, high=high):
                            others = ()
                            if low:
                                arrived(rv.at[i, self.at(pc)], ch_r.at[i, pc])
                                others += (i,)
                            if high:
                                arrived(rv.at[N, self.at(pc)], ch_r.at[N, pc])
                                others += (N,)
                            self.add(i, pc, others, store)

            def drain(self):
                def one(j, c):
                    for pc in range(self.pieces):

                        @pl.when(self.used(2 * j + 1 - core, pc))
                        def _(pc=pc):
                            self.pair(j, pc).wait_send()

                        @pl.when((j > self.i) & self.used(2 * j + core, pc))
                        def _(pc=pc):
                            self.rightward(j, pc).wait_send()

                        @pl.when((j < self.i) & self.used(2 * j + core, pc))
                        def _(pc=pc):
                            self.leftward(j, pc).wait_send()

                    return c

                lax.fori_loop(0, N, one, 0)

        def weights_out():
            copy = pltpu.make_async_copy(tmp.at[pl.ds(0, SR)], dw_o, ld.at[1])
            copy.start()
            copy.wait()

        everything = range(PC)

        def flat(used_rows):
            filled = -(-used_rows // PR) * PR
            if filled > used_rows:
                dwl[pl.ds(used_rows, filled - used_rows), :] = jnp.zeros((filled - used_rows, 128), BF)
            return Reduction(PC, PR, lambda s, pc: s * SR + pc * PR, lambda s, pc: s * SR + pc * PR < used_rows)

        def launch(red, low=0, high=N):
            red.send_pairs(everything, low, high)
            red.originate(everything, low, high)

        def finish_flat(red):
            tmp[pl.ds(0, SR), :] = jnp.zeros((SR, 128), F32)
            for pc in everything:

                def store(at_s, s, v):
                    tmp[pl.ds(pl.multiple_of(pc * PR + s * red.step, CH), red.step), :] = v

                red.finish(pc, store)
            weights_out()
            red.drain()

        barrier = pltpu.get_barrier_semaphore()
        load_x = pltpu.make_async_copy(x_h, xb.at[:, pl.ds(0, IN)], ld.at[0])

        @pl.when(me_p < 3)
        def _():
            load_x.start()

        def greet(i, c):
            p, d = i // R, lax.rem(i, R)

            @pl.when((p != me_p) | (d != me_d))
            def _():
                pl.semaphore_signal(barrier, inc=1, device_id=(p, d), device_id_type=MESH)

            return c

        lax.fori_loop(0, NP * R, greet, 0)

        @pl.when(me_p == 0)
        def _():
            fetch_narrow(n1)

        @pl.when(me_p == 2)
        def _():
            fetch_wide(0, C_MID, lambda q: q * n3)

        ng_o[...] = jnp.zeros_like(ng_o)
        ngs[...] = jnp.zeros_like(ngs)
        for m in range(MICRO):
            lanes = lax.broadcasted_iota(jnp.int32, (1, W), 1)
            keep[m] = jnp.where(lanes < C_MID * width_step[m] // 4, 1.0, 0.0)

        pl.semaphore_wait(barrier, NP * R - 1)

        def lay_out(values, lanes, big_o, small_o, big_rows, side):
            fw[0, pl.ds(0, values.shape[0]), :] = values
            for r in range(big_rows // side):
                big_o[r, :, lanes] = fw[0, pl.ds(r * side, side), :].astype(BF)
            crops = geo.crops[1]
            for p in range(small_o.shape[0]):
                small_o[p, :, lanes] = fw[0, pl.ds(big_rows + p * crops, crops), :].astype(BF)

        def finals():
            arrived(orecv, out_r)
            for q in range(NQ):
                lay_out(orecv[q].astype(F32), pl.ds(q * W, W), ob_o, os_o, geo.out_big, geo.sides[0] // 2)
            arrived(srecv, sb_r)
            arrived(mrecv, mn_r)
            for h in range(2):
                total = mrecv[h].astype(F32) + dot_tn(ps[...], srecv[h])
                lay_out(total, pl.ds(h * W, W), gb_o, gs_o, geo.in_big, geo.sides[0])

        def sub_hop(k):
            ref = col.at[pl.ds(6, 2), k]
            return remote(ref, ref, xs_s.at[k], xs_r.at[k], 0, me_d)

        def sub_back(k):
            return (col.at[pl.ds(6, 2), k], srecv, sb_s.at[k], sb_r, my_m, k * G + my_c)

        def nt_copy(count):
            return remote(nt.at[pl.ds(0, count)], nt2.at[pl.ds(0, count)], nt_s, nt_r, me_p + 1, me_d)

        def main_copy(m):
            return (tgb.at[pl.ds(2 * m, 2), pl.ds(0, IN)], mrecv, mn_s.at[m], mn_r, m, me_d)

        def w1_here(q):
            return pl.multiple_of(q * W, W)

        def ng_copy():
            return remote(ngs.at[0], ngr.at[0, 0], stn_s.at[0], stn_r.at[0], 0, me_d)

        @pl.when(me_p == 0)
        def _():
            ship_all(w1_here, w1_at, 2, lambda copy: copy.start())
            nt_copy(1).start()
            load_x.wait()

            def dx(m, c):
                arrived(rbig.at[m, pl.ds(0, IN)], big_r.at[m])
                for h in range(2):
                    tgb[2 * m + h, pl.ds(0, IN), :] = dot_nt(rbig[m, pl.ds(0, IN), :], weight(h * W)).astype(BF)
                push(*main_copy(m))
                return c

            lax.fori_loop(0, MICRO, dx, 0)
            for h in range(2):
                total = dot_tn(xb[h, pl.ds(0, IN), :], rbig[0, pl.ds(0, IN), :])
                for m in range(1, MICRO):
                    total += dot_tn(xb[2 * m + h, pl.ds(0, IN), :], rbig[m, pl.ds(0, IN), :])
                keep_narrow(h * W, total)
            red = flat(n1 * LANES)
            launch(red)
            for k in range(MICRO):
                arrived(col.at[pl.ds(6, 2), k], xs_r.at[k])
                push(*sub_back(k))
            red.relay(everything)
            finish_flat(red)
            finals()
            arrived(ngr.at[0, 0], stn_r.at[0])
            ng_o[0] = ngr[0, 0]
            ship_all(w1_here, w1_at, 2, lambda copy: copy.wait_send())
            nt_copy(1).wait_send()
            for m in range(MICRO):
                pushed(*main_copy(m))
                pushed(*sub_back(m))

        @pl.when(me_p == 1)
        def _():
            A2, D2, D1 = MICRO, MICRO + 1, MICRO + 2
            fetch_narrow(n2)
            load_x.wait()
            take(w1_at, 2)
            arrived(nt2.at[pl.ds(0, 1)], nt_r)

            def first(m, c):
                fw[m, pl.ds(0, IN), :] = dot(xb[2 * m, pl.ds(0, IN), :], weight(n2)) + dot(
                    xb[2 * m + 1, pl.ds(0, IN), :], weight(n2 + W)
                )
                put(own_a, m, reduce_rows(1, runs_in, squares(lambda b, f: fw[m, rows(f), :]), 2))
                send_a(m)
                return c

            lax.fori_loop(0, MICRO, first, 0)

            def conv(m):
                finish_norm(total_a(m), m, nt2, 0, count_in)

                def act(b, f, bc, vc):
                    n = normed(fw[m, rows(f), :], m, bc)
                    stage[m, rows(f), :] = kept(n * sigmoid(n), m, bc).astype(BF)

                map_rows(1, runs_in, act)
                col[:, m] = dot(p2[...], stage[m, pl.ds(0, IN), :]).astype(BF).reshape(9, OUT, W)
                total = dot(col[0, m], weight(0))
                for tap in range(1, 9):
                    total += dot(col[tap, m], weight(tap * C_MID))
                fw[A2, block(m), :] = total
                put(own_a, MICRO + m, reduce_rows(1, runs_out, squares(lambda b, f: fw[A2, at(m, f), :]), 2))
                send_a(MICRO + m)

            def a2_copy(m, p):
                sems = sm_s if p == 2 else sm_t
                return (ssm.at[m], rsm.at[my_m], sems.at[m], sm_r.at[my_m], p, m * G + my_c)

            def give(m):
                slot = MICRO + m
                finish_norm(total_a(slot), slot, nt, 0, count_out)

                def act(b, f, bc, vc):
                    n = normed(fw[A2, at(m, f), :], slot, bc)
                    ssm[m, rows(f), :] = kept(n * sigmoid(n), m, bc).astype(BF)

                map_rows(1, runs_out, act)
                push(*a2_copy(m, 3))
                push(*a2_copy(m, 2))

            def forward(step, c):
                @pl.when(step < MICRO)
                def _():
                    conv(step)

                @pl.when(step > 0)
                def _():
                    give(step - 1)

                return c

            lax.fori_loop(0, MICRO + 1, forward, 0)

            def back_two(m):
                arrived(rsm.at[m], sm_r.at[m])
                slot = MICRO + m

                def sums(b, f, bc, vc):
                    u = fw[A2, at(m, f), :]
                    d = kept(rsm[m, rows(f), :].astype(F32) * slope_of(normed(u, slot, bc)), m, bc)
                    fw[D2, at(m, f), :] = d
                    return (d, d * centered(u, slot, bc))

                put(own_a, 2 * MICRO + m, reduce_rows(1, runs_out, sums, 2))
                send_a(2 * MICRO + m)

            def back_mid(m):
                total = total_a(2 * MICRO + m)
                slot = MICRO + m
                put_cof(0, total, count_out)
                add_norm_grads(ng_o, 0, total)

                def grad(b, f, bc, vc):
                    z = centered(fw[A2, at(m, f), :], slot, bc)
                    dwide[0, at(m, f), :] = back(fw[D2, at(m, f), :], z, 0, 0, slot, bc, vc)

                map_rows(1, runs_out, grad)

            def back_one(m):
                du = dwide[0, block(m), :]
                for tap in range(9):
                    tgb[tap, pl.ds(0, OUT), :] = dot_nt(du, weight(tap * C_MID)).astype(BF)
                taps = tgb[:, pl.ds(0, OUT), :].reshape(9 * OUT, W)
                stage[m, pl.ds(0, IN), :] = dot_tn(p2[...], taps).astype(BF)

                def sums(b, f, bc, vc):
                    u = fw[m, rows(f), :]
                    d = kept(stage[m, rows(f), :].astype(F32) * slope_of(normed(u, m, bc)), m, bc)
                    fw[D1 + m, rows(f), :] = d
                    return (d, d * centered(u, m, bc))

                put(own_a, 3 * MICRO + m, reduce_rows(1, runs_in, sums, 2))
                send_a(3 * MICRO + m)

            def du1_copy(m):
                ref = pl.ds(0, IN)
                return remote(stage.at[m, ref], rbig.at[m, ref], big_s.at[m], big_r.at[m], 0, me_d)

            def back_out(m):
                total = total_a(3 * MICRO + m)
                put_cof(0, total, count_in)
                add_norm_grads(ngs, 0, total)

                def grad(b, f, bc, vc):
                    z = centered(fw[m, rows(f), :], m, bc)
                    stage[m, rows(f), :] = back(fw[D1 + m, rows(f), :], z, 0, 0, m, bc, vc)

                map_rows(1, runs_in, grad)
                du1_copy(m).start()

            def backward(step, c):
                @pl.when(step < MICRO)
                def _():
                    back_two(step)

                @pl.when((step > 0) & (step <= MICRO))
                def _():
                    back_mid(step - 1)
                    back_one(step - 1)

                @pl.when(step > 1)
                def _():
                    back_out(step - 2)

                return c

            def weights(tap, c):
                keep_narrow(tap * C_MID, dot_tn(col[tap].reshape(ROWS, W), dwide[0, full, :]))
                return c

            lax.fori_loop(0, MICRO + 2, backward, 0)
            ng_copy().start()
            lax.fori_loop(0, 9, weights, 0)
            red = flat(n2 * LANES)
            launch(red)
            red.relay(everything)
            finals()
            finish_flat(red)
            pass_on(w1_at, 2, lambda ref, q, copy: copy.wait_send())
            ng_copy().wait_send()
            for m in range(MICRO):
                du1_copy(m).wait_send()
                pushed(*a2_copy(m, 2))
                pushed(*a2_copy(m, 3))
            for slot in range(4 * MICRO):
                drain_a(slot)

        def share_copy(k):
            return remote(ngs, ngr.at[k - 1], stn_s.at[k - 1], stn_r.at[k - 1], me_p, lax.rem(me_d + k * G, R))

        def share_norm_grads():
            ngs[...] = ng_o[...]
            for k in range(1, MICRO):
                share_copy(k).start()

        def take_norm_grads():
            for k in range(1, MICRO):
                arrived(ngr.at[k - 1], stn_r.at[k - 1])
                ng_o[...] += ngr[k - 1]
            for k in range(1, MICRO):
                share_copy(k).wait_send()

        def sub_copy(m):
            return (col.at[pl.ds(4, 2), m], col.at[pl.ds(0, 2), my_m], xs_s.at[m], xs_r.at[my_m], 2, m * G + my_c)

        def w3_here(q):
            return pl.multiple_of(q * n3, W)

        @pl.when(me_p == 2)
        def _():
            ship_all(w3_here, w3_at, NQ, lambda copy: copy.start())
            nt_copy(NQ).start()
            load_x.wait()

            def send_x(m, c):
                for h in range(2):
                    col[4 + h, m] = dot(ps[...], xb[2 * m + h, pl.ds(0, IN), :]).astype(BF)
                push(*sub_copy(m))
                return c

            lax.fori_loop(0, MICRO, send_x, 0)
            fetch_wide(C_MID, C_IN, lambda q: q * n3 + C_MID)
            for k in range(MICRO):
                arrived(col.at[pl.ds(0, 2), k], xs_r.at[k])

            def w3(q):
                return weight(q * n3)

            def wp(q, h):
                return weight(q * n3 + C_MID + h * W)

            def xsub(h):
                return col[h].reshape(ROWS, W)

            def product(index, value, slot):
                fw[index, full, :] = value
                put(own_b, slot, reduce_rows(MICRO, runs_out, squares(lambda b, f: fw[index, at(b, f), :]), 2))
                send_b(slot)

            def up_copy(q):
                return remote(stage.at[q, full], stage.at[q, full], up_s.at[q], up_r.at[q], 3, me_d)

            def short(q):
                product(NQ + q, dot(xsub(0), wp(q, 0)) + dot(xsub(1), wp(q, 1)), NQ + q)

            def short_out(q):
                finish_norm(total_b(NQ + q), NQ + q, nt, NQ + q, count_out)

                def act(b, f, bc, vc):
                    stage[q, at(b, f), :] = normed(fw[NQ + q, at(b, f), :], NQ + q, bc).astype(BF)

                map_rows(MICRO, runs_out, act)
                up_copy(q).start()

            def shorts(step, c):
                @pl.when(step < NQ)
                def _():
                    short(step)

                @pl.when(step > 0)
                def _():
                    short_out(step - 1)

                return c

            lax.fori_loop(0, NQ + 1, shorts, 0)
            for k in range(MICRO):
                arrived(rsm.at[k], sm_r.at[k])

            def main(q, c):
                product(q, dot(rsm[...].reshape(ROWS, W), w3(q)), q)
                return c

            lax.fori_loop(0, NQ, main, 0)

            def main_norm(q, c):
                finish_norm(total_b(q), q, nt, q, count_out)
                return c

            lax.fori_loop(0, NQ, main_norm, 0)
            tmp[...] = jnp.zeros_like(tmp)
            red = Reduction(
                NQ, PRQ, lambda s, pc: (pc * S2 + s) * PRQ, lambda s, pc: s < S2
            )
            D, SUB = 2 * NQ, 2 * NQ + 1

            def lay_part(s, q):
                start = pl.multiple_of((q * S2 + s) * PRQ, CH)
                at_s = pl.multiple_of(s * RW * LANES, 8)
                dwl[pl.ds(start, RW * LANES), :] = tmp[pl.ds(at_s, RW * LANES), :].astype(BF)

            for q in range(NQ):
                arrived(rbig.at[q, full], big_r.at[q])

                def sums(b, f, bc, vc):
                    um, us = fw[q, at(b, f), :], fw[NQ + q, at(b, f), :]
                    n = normed(um, q, bc) + normed(us, NQ + q, bc)
                    d = rbig[q, at(b, f), :].astype(F32) * slope_of(n)
                    fw[D, at(b, f), :] = d
                    return (d, d * centered(um, q, bc), d * centered(us, NQ + q, bc))

                db, mb, sb, ds, ms, ss = reduce_rows(MICRO, runs_out, sums, 3)
                put(own_b, 2 * NQ + q, (db, mb, ds, ms))
                put(own_b, 3 * NQ + q, (db, sb, ds, ss))
                send_b(2 * NQ + q)
                send_b(3 * NQ + q)
                for i, cb in ((0, q), (1, NQ + q)):
                    total = total_b((2 + i) * NQ + q)
                    put_cof(i, total, count_out)
                    add_norm_grads(ng_o, cb, total)

                def grad(b, f, bc, vc):
                    d = fw[D, at(b, f), :]
                    zm = centered(fw[q, at(b, f), :], q, bc)
                    zs = centered(fw[NQ + q, at(b, f), :], NQ + q, bc)
                    dwide[q, at(b, f), :] = back(d, zm, 0, 0, q, bc, vc)
                    dwide[NQ + q, at(b, f), :] = back(d, zs, 1, 1, NQ + q, bc, vc)

                map_rows(MICRO, runs_out, grad)
                lay_narrow(0, dot_tn(rsm[...].reshape(ROWS, W), dwide[q, full, :]))
                for h in range(2):
                    lay_narrow((1 + h) * W * LANES, dot_tn(xsub(h), dwide[NQ + q, full, :]))

                def lay(s, c):
                    lay_part(s, q)
                    return c

                lax.fori_loop(0, S2, lay, 0)
                red.send_pairs((q,))
                for h in range(2):
                    piece = dot_nt(dwide[NQ + q, full, :], wp(q, h))
                    fw[SUB + h, full, :] = piece if q == 0 else fw[SUB + h, full, :] + piece
                red.originate((q,))

            share_norm_grads()
            for h in range(2):
                for k in range(MICRO):
                    col[6 + h, k] = fw[SUB + h, block(k), :].astype(BF)
            for m in range(MICRO):
                pushed(*sub_copy(m))
            for k in range(MICRO):
                sub_hop(k).start()
            for q in range(NQ):
                red.relay((q,))
            finals()
            take_norm_grads()
            for q in range(NQ):

                def store(at_s, s, v):
                    tmp[pl.ds(pl.multiple_of(SR + s * red.step, CH), red.step), :] = v

                red.finish(q, store)

                @pl.when(red.used(me_d, q))
                def _():
                    for lane in range(LANES):
                        values = tmp[pl.ds(SR + lane, RW, stride=LANES), :]
                        tmp[pl.ds(q * LANES + lane, RW, stride=NQ * LANES), :] = values

            @pl.when(jnp.logical_not(red.used(me_d, 0)))
            def _():
                tmp[pl.ds(0, SR), :] = jnp.zeros((SR, 128), F32)

            weights_out()
            red.drain()
            ship_all(w3_here, w3_at, NQ, lambda copy: copy.wait_send())
            nt_copy(NQ).wait_send()
            for k in range(MICRO):
                sub_hop(k).wait_send()
            for q in range(NQ):
                up_copy(q).wait_send()
            for slot in range(4 * NQ):
                drain_b(slot)

        def cot_copy(m):
            return (cot_h.at[m], xb.at[pl.ds(0, NQ), block(my_m)], ct_s.at[m], ct_r.at[my_m], 3, m * G + my_c)

        def gate_copy(m):
            return (gate_v.at[m], gateb.at[my_m], gt_s.at[m], gt_r.at[my_m], 3, m * G + my_c)

        def out_copy(k):
            return (xb.at[pl.ds(NQ, NQ), block(k)], orecv, out_s.at[k], out_r, my_m, k * G + my_c)

        @pl.when(me_p == 3)
        def _():
            r = lax.broadcasted_iota(jnp.int32, (OUT, 128), 0)
            small = r - geo.out_big
            for m in range(MICRO):
                g = jnp.zeros((OUT, 128), F32)
                for i in range(geo.crops[0]):
                    area = geo.out_big // geo.crops[0]
                    g = jnp.where((r >= i * area) & (r < (i + 1) * area), gate_big[i, m].astype(F32), g)
                for i in range(geo.crops[1]):
                    mine = (small >= 0) & (lax.rem(small + geo.crops[1] * OUT, geo.crops[1]) == i)
                    g = jnp.where(mine, gate_small[i, m].astype(F32), g)
                gate_v[m] = g
            for m in range(MICRO):
                push(*gate_copy(m))
                push(*cot_copy(m))
            fetch_narrow(nab)
            fetch_wide(nab * W // C_OUT, C_MID, lambda q: nab + q * C_MID)
            take(w3_at, NQ)
            arrived(nt2, nt_r)
            A, B, T1, T2, U3 = 2 * NQ, 2 * NQ + 1, 2 * NQ + 2, 2 * NQ + 3, 2 * NQ + 4
            DB, DA, H1, H2 = NQ, NQ + 1, NQ + 2, NQ + 3
            S3, PM = 4 + 2 * NQ, 2 + NQ

            def wa(q):
                return weight(q * W)

            def wb(tap):
                return weight(C_OUT + tap * C_MID)

            def wc(q):
                return weight(nab + q * C_MID)

            def w3(q):
                return weight(nabc + q * C_MID)

            def accumulate(index, i, value):
                @pl.when(i == 0)
                def _():
                    fw[index, full, :] = value

                @pl.when(i > 0)
                def _():
                    fw[index, full, :] += value

            def begin(index, slot):
                put(own_b, slot, reduce_rows(MICRO, runs_out, squares(lambda b, f: fw[index, at(b, f), :]), 2))
                send_b(slot)

            def hidden(index, slot, target):
                def act(b, f, bc, vc):
                    n = normed(fw[index, at(b, f), :], slot, bc)
                    dwide[target, at(b, f), :] = kept(n * sigmoid(n), my_m, bc).astype(BF)

                map_rows(MICRO, runs_out, act)

            def gather(source, target):
                def one(k, c):
                    target(k, dot(pb[...], dwide[source, block(k), :]).astype(BF).reshape(9, OUT, W))
                    return c

                lax.fori_loop(0, MICRO, one, 0)

            for k in range(MICRO):
                arrived(rsm.at[k], sm_r.at[k])

            def main(q, c):
                fw[U3 + q, full, :] = dot(rsm[...].reshape(ROWS, W), w3(q))
                begin(U3 + q, S3 + q)
                return c

            lax.fori_loop(0, NQ, main, 0)

            def join(q, c):
                finish_norm(total_b(S3 + q), PM + q, nt2, q, count_out)
                arrived(stage.at[q, full], up_r.at[q])

                def act(b, f, bc, vc):
                    n = normed(fw[U3 + q, at(b, f), :], PM + q, bc) + stage[q, at(b, f), :].astype(F32)
                    rbig[q, at(b, f), :] = (n * sigmoid(n)).astype(BF)

                map_rows(MICRO, runs_out, act)
                accumulate(A, q, dot(rbig[q, full, :], wa(q)))
                return c

            lax.fori_loop(0, NQ, join, 0)
            begin(A, 0)
            finish_norm(total_b(0), 0, nt, 0, count_out)
            hidden(A, 0, H1)

            def to_col(k, v):
                col[:, k] = v

            gather(H1, to_col)

            def conv(tap, c):
                accumulate(B, tap, dot(col[tap].reshape(ROWS, W), wb(tap)))
                return c

            lax.fori_loop(0, 9, conv, 0)
            begin(B, 1)
            finish_norm(total_b(1), 1, nt, 1, count_out)
            hidden(B, 1, H2)

            def widen(q, c):
                fw[q, full, :] = dot(dwide[H2, full, :], wc(q))
                begin(q, 2 + q)
                return c

            lax.fori_loop(0, NQ, widen, 0)
            for k in range(MICRO):
                arrived(gateb.at[k], gt_r.at[k])
                arrived(xb.at[pl.ds(0, NQ), block(k)], ct_r.at[k])

            def gate_at(b, f):
                g = gateb[b, rows(f), :]
                return jnp.concatenate([g] * LANES, axis=1)

            def ends(q, c):
                finish_norm(total_b(2 + q), 2 + q, nt, 2 + q, count_out)

                def sums(b, f, bc, vc):
                    u = fw[q, at(b, f), :]
                    g = gate_at(b, f)
                    v = rbig[q, at(b, f), :].astype(F32) + g * normed(u, 2 + q, bc)
                    sg = sigmoid(v)
                    xb[NQ + q, at(b, f), :] = (v * sg).astype(BF)
                    d = xb[q, at(b, f), :].astype(F32) * (sg * (1.0 + v * (1.0 - sg)))
                    fw[NQ + q, at(b, f), :] = d
                    d = g * d
                    return (d, d * centered(u, 2 + q, bc))

                put(own_b, 2 + NQ + q, reduce_rows(MICRO, runs_out, sums, 2))
                send_b(2 + NQ + q)
                return c

            lax.fori_loop(0, NQ, ends, 0)

            def ends_back(q, c):
                total = total_b(2 + NQ + q)
                put_cof(0, total, count_out)
                add_norm_grads(ng_o, 2 + q, total)

                def grad(b, f, bc, vc):
                    z = centered(fw[q, at(b, f), :], 2 + q, bc)
                    d = gate_at(b, f) * fw[NQ + q, at(b, f), :]
                    dwide[q, at(b, f), :] = back(d, z, 0, 0, 2 + q, bc, vc)

                map_rows(MICRO, runs_out, grad)
                accumulate(T1, q, dot_nt(dwide[q, full, :], wc(q)))
                return c

            lax.fori_loop(0, NQ, ends_back, 0)
            for k in range(MICRO):
                push(*out_copy(k))

            def middle(index, pslot, slot, target):
                def sums(b, f, bc, vc):
                    u = fw[index, at(b, f), :]
                    d = kept(fw[T1, at(b, f), :] * slope_of(normed(u, pslot, bc)), my_m, bc)
                    fw[T2, at(b, f), :] = d
                    return (d, d * centered(u, pslot, bc))

                put(own_b, slot, reduce_rows(MICRO, runs_out, sums, 2))
                send_b(slot)
                total = total_b(slot)
                put_cof(0, total, count_out)
                add_norm_grads(ng_o, pslot, total)

                def grad(b, f, bc, vc):
                    z = centered(fw[index, at(b, f), :], pslot, bc)
                    dwide[target, at(b, f), :] = back(fw[T2, at(b, f), :], z, 0, 0, pslot, bc, vc)

                map_rows(MICRO, runs_out, grad)

            middle(B, 1, 2 + 2 * NQ, DB)

            def to_taps(k, v):
                tgb[:, block(k), :] = v

            gather(DB, to_taps)

            def conv_back(tap, c):
                accumulate(T1, tap, dot_nt(tgb[tap, full, :], wb(8 - tap)))
                return c

            lax.fori_loop(0, 9, conv_back, 0)
            middle(A, 0, 3 + 2 * NQ, DA)

            def dy_copy(q):
                return remote(stage.at[q, full], rbig.at[q, full], big_s.at[q], big_r.at[q], 2, me_d)

            def to_y(q, c):
                fw[T2, full, :] = dot_nt(dwide[DA, full, :], wa(q))

                def sums(b, f, bc, vc):
                    dy = (fw[T2, at(b, f), :] + fw[NQ + q, at(b, f), :]).astype(BF)
                    u = fw[U3 + q, at(b, f), :]
                    n = normed(u, PM + q, bc) + stage[q, at(b, f), :].astype(F32)
                    stage[q, at(b, f), :] = dy
                    d = dy.astype(F32) * slope_of(n)
                    fw[q, at(b, f), :] = d
                    return (d, d * centered(u, PM + q, bc))

                put(own_b, S3 + NQ + q, reduce_rows(MICRO, runs_out, sums, 2))
                send_b(S3 + NQ + q)
                dy_copy(q).start()
                return c

            lax.fori_loop(0, NQ, to_y, 0)

            def through_w3(q, c):
                put_cof(0, total_b(S3 + NQ + q), count_out)

                def grad(b, f, bc, vc):
                    z = centered(fw[U3 + q, at(b, f), :], PM + q, bc)
                    xb[q, at(b, f), :] = back(fw[q, at(b, f), :], z, 0, 0, PM + q, bc, vc)

                map_rows(MICRO, runs_out, grad)
                accumulate(T1, q, dot_nt(xb[q, full, :], w3(q)))
                return c

            lax.fori_loop(0, NQ, through_w3, 0)

            def da2_copy(k):
                return remote(ssm.at[k], rsm.at[my_m], sm_s.at[k], sm_r.at[my_m], 1, k * G + my_c)

            def back_a2(k, c):
                ssm[k] = fw[T1, block(k), :].astype(BF)
                da2_copy(k).start()
                return c

            lax.fori_loop(0, MICRO, back_a2, 0)

            def weights_a(q, c):
                keep_narrow(q * W, dot_tn(rbig[q, full, :], dwide[DA, full, :]))
                return c

            def weights_b(tap, c):
                keep_narrow(C_OUT + tap * C_MID, dot_tn(col[tap].reshape(ROWS, W), dwide[DB, full, :]))
                return c

            share_norm_grads()
            red = flat(nabc * LANES)
            t1, t2 = (C_OUT + C_MID) * LANES // (2 * SR), -(-(nab - C_MID) * LANES // (2 * SR))
            order = ((t2, N), (0, t1), (t1, t2))
            keep_wide(nab * W // C_OUT, lambda r: dwide[H2, full, r], 0)
            weights_b(8, 0)
            launch(red, *order[0])
            lax.fori_loop(0, NQ, weights_a, 0)
            weights_b(0, 0)
            launch(red, *order[1])
            lax.fori_loop(1, 8, weights_b, 0)
            launch(red, *order[2])
            for low, high in order:
                red.relay(everything, low, high)
            finals()
            take_norm_grads()
            finish_flat(red)
            pass_on(w3_at, NQ, lambda ref, q, copy: copy.wait_send())
            for m in range(MICRO):
                pushed(*gate_copy(m))
                pushed(*cot_copy(m))
                pushed(*out_copy(m))
                da2_copy(m).wait_send()
            for q in range(NQ):
                dy_copy(q).wait_send()
            for slot in range(S3 + 2 * NQ):
                drain_b(slot)

    return kernel


def radix(count, most):
    if count <= most:
        return count
    return next(r for r in range(most, 0, -1) if count % r == 0)


def handed_on(arrays):
    count = len(arrays)

    def kernel(*refs):
        for i in range(count):
            refs[count + i][...] = refs[i][...]

    vmem = pl.BlockSpec(memory_space=pltpu.VMEM)
    return pl.pallas_call(
        kernel,
        out_shape=tuple(jax.ShapeDtypeStruct(a.shape, a.dtype) for a in arrays),
        in_specs=[vmem] * count,
        out_specs=(vmem,) * count,
    )(*arrays)


def solution(mesh):
    R, NP = mesh.shape["dp"], mesh.shape["pipe"]

    def on_device(x_big, x_small, cot_big, cot_small, section_weights, section_norms, gate_big, gate_small, width_step):
        MICRO = x_big.shape[0]
        G = R // MICRO
        geo = Geometry((x_big.shape[1], x_small.shape[1]), (x_big.shape[2], x_small.shape[2]))
        IN, OUT, ROWS = geo.IN, geo.OUT, MICRO * geo.OUT
        PW = section_weights.shape[1]
        NB = section_norms.shape[2] // W
        wide = max(IN, ROWS)

        def joined(big, small, width, length):
            parts = [big.reshape(MICRO, -1, width), small.transpose(0, 2, 3, 1, 4).reshape(MICRO, -1, width)]
            v = jnp.concatenate(parts, axis=1)
            return jnp.pad(v, ((0, 0), (0, length - v.shape[1]), (0, 0)))

        x = joined(x_big, x_small, C_IN, IN)
        x = x.reshape(MICRO, IN, 2, W).transpose(0, 2, 1, 3).reshape(2 * MICRO, IN, W)
        cot = joined(cot_big, cot_small, C_OUT, OUT).reshape(MICRO, OUT, NQ, W).transpose(0, 2, 1, 3)
        w4 = section_weights.reshape(PW // W, LANES, 1, 128)
        w16 = section_weights.reshape(PW // C_OUT, NQ * LANES, 1, 128)
        SR = PW // 128 // R
        PC = 4 if SR % (4 * CH) == 0 else 2 if SR % (2 * CH) == 0 else 1
        RW = SR // (NQ * LANES)
        SRP = max(SR, NQ * up16(RW * LANES))
        tmp_rows = max(HALF * NQ * LANES, -(-(C_MID + C_IN) // RW) * RW * LANES, SR + up16(RW * LANES))
        nt = section_norms[0].reshape(4, NB, W).transpose(1, 0, 2)
        p2 = geo.windows(2)
        sub = geo.every_second()
        consts = [p2, geo.windows(1), sub]
        consts = [jnp.asarray(c, BF) for c in consts]
        vmem, hbm = pl.BlockSpec(memory_space=pltpu.VMEM), pl.BlockSpec(memory_space=pl.ANY)
        smem = pl.BlockSpec(memory_space=pltpu.SMEM)
        V, D = pltpu.VMEM, pltpu.SemaphoreType.DMA
        RA, RB = radix(R, 8), radix(G, 4)
        nb, sb, ns, ss = geo.crops[0], geo.sides[0], geo.crops[1], geo.sides[1]
        SA, SB = 4 * MICRO, 4 + 4 * NQ

        def sums(slots, first, all_of):
            later = max(all_of // first - 1, 1)
            kept_slots = slots if all_of > first else 1
            return [
                V((slots, 4, W), F32),
                V((slots, max(first - 1, 1), 4, W), F32),
                V((kept_slots, 4, W), F32),
                V((kept_slots, later, 4, W), F32),
            ]

        results = pl.pallas_call(
            make_kernel(geo, R, NP, MICRO, SR, PC),
            out_shape=(
                jax.ShapeDtypeStruct((nb * sb // 2, sb // 2, C_OUT), BF),
                jax.ShapeDtypeStruct((ss * ss // 4, ns, C_OUT), BF),
                jax.ShapeDtypeStruct((nb * sb, sb, C_IN), BF),
                jax.ShapeDtypeStruct((ss * ss, ns, C_IN), BF),
                jax.ShapeDtypeStruct((SR, 128), F32),
                jax.ShapeDtypeStruct((NB, 4, W), F32),
            ),
            in_specs=[hbm, hbm, smem, smem, smem, hbm, hbm, vmem] + [vmem] * 3,
            out_specs=(vmem, vmem, vmem, vmem, hbm, vmem),
            scratch_shapes=[
                V((PW // W + C_OUT, W), BF),
                V((2, LANES, 128, 1, 128), BF),
                V((2 * MICRO, wide, W), BF),
                V((MICRO, OUT, 128), F32),
                V((MICRO, OUT, 128), F32),
                V((MICRO, 1, W), F32),
                V((NQ, wide, W), BF),
                V((NQ, wide, W), BF),
                V((MICRO, OUT, W), BF),
                V((MICRO, OUT, W), BF),
                V((3 * NQ + 4, wide, W), F32),
                V((2 * NQ, wide, W), BF),
                V((9, MICRO, OUT, W), BF),
                V((9, wide, W), BF),
                V((tmp_rows, 128), F32),
                V((2, IN, W), BF),
                V((2, OUT, W), BF),
                V((NQ, OUT, W), BF),
                V((PW // 128, 128), BF),
                V((R // 2, SRP, 128), BF),
                V((R // 2 + 1, SRP, 128), BF),
                V((NQ, 4, W), F32),
                *sums(SA, RA, R),
                *sums(SB, RB, G),
                V((max(2 * MICRO, 2 + 2 * NQ), 8, W), F32),
                V((2, 4, W), F32),
                V((NB, 4, W), F32),
                V((MICRO - 1, NB, 4, W), F32),
                D((2,)),
                D((2, LANES)),
                D((4,)), D((4,)),
                D((4,)), D((4,)), D((4,)),
                D((4,)), D((4,)),
                D((4,)), D((4,)),
                D((4,)), D((4,)),
                D((4,)), D((4,)),
                D((4,)), D((4,)),
                D, D,
                D((4,)), D,
                D((4,)), D,
                D((4,)), D,
                D((SA,)), D((SA,)), D((SA,)), D((SA,)),
                D((SB,)), D((SB,)), D((SB,)), D((SB,)),
                D((MICRO - 1,)), D((MICRO - 1,)),
                D((R // 2, 4)), D((R // 2, 4)),
                D((R // 2, 4)), D((R // 2 + 1, 4)),
            ],
            compiler_params=pltpu.CompilerParams(
                collective_id=0, has_side_effects=True, vmem_limit_bytes=63 << 20
            ),
        )(x, cot, gate_big.T, gate_small.T, width_step, w4, w16, nt, *consts)

        ob, os, gb, gs, dw, ng = handed_on(results)

        def small(v, side, width):
            return v.reshape(side, side, ns, width).transpose(2, 0, 1, 3)[None]

        return (
            ob.reshape(1, nb, sb // 2, sb // 2, C_OUT),
            small(os, ss // 2, C_OUT),
            gb.reshape(1, nb, sb, sb, C_IN),
            small(gs, ss, C_IN),
            dw.reshape(1, PW // R),
            ng.transpose(1, 0, 2).reshape(1, 4, NB * W),
        )

    images = P(None, "dp", None, None, None)
    ends = P("pipe", "dp", None, None, None)
    return jax.shard_map(
        on_device,
        mesh=mesh,
        in_specs=(images,) * 4 + (P("pipe", None), P("pipe", None, None), P(None, "dp"), P(None, "dp"), P()),
        out_specs=(ends,) * 4 + (P("pipe", "dp"), P("pipe", None, None)),
        check_vma=False,
    )
```

```python
import functools

import jax
import jax.numpy as jnp
import numpy as np
from jax import lax
from jax.experimental import pallas as pl
from jax.experimental.pallas import tpu as pltpu
from jax.sharding import PartitionSpec as P

C_IN = 1024
C_MID = 512
C_OUT = 2048
EPS = 1e-05
W = 512
NQ = C_OUT // W
CH = 16
LANES = W // 128
HALF = W // 2
BF = jnp.bfloat16
F32 = jnp.float32
MESH = pl.DeviceIdType.MESH


def up16(n):
    return -(-n // 16) * 16


class Geometry:
    def __init__(self, crops, sides):
        self.crops, self.sides = crops, sides
        self.in_big = crops[0] * sides[0] ** 2
        self.in_all = self.in_big + crops[1] * sides[1] ** 2
        self.out_big = crops[0] * (sides[0] // 2) ** 2
        self.out_all = self.out_big + crops[1] * (sides[1] // 2) ** 2
        self.IN, self.OUT = up16(self.in_all), up16(self.out_all)

    def pixels(self, halves):
        index, table = 0, {}
        for group in (0, 1):
            side = self.sides[group] // 2 if halves else self.sides[group]
            crops, sides = range(self.crops[group]), range(side)
            if group == 0:
                places = [(crop, r, c) for crop in crops for r in sides for c in sides]
            else:
                places = [(crop, r, c) for r in sides for c in sides for crop in crops]
            for place in places:
                table[(group,) + place] = index
                index += 1
        return table

    def windows(self, stride):
        ins, outs = self.pixels(stride == 1), self.pixels(True)
        picks = np.zeros((9, self.OUT, self.OUT if stride == 1 else self.IN), np.float32)
        for (group, crop, r, c), row in outs.items():
            for tap in range(9):
                at = (group, crop, stride * r + tap // 3 - 1, stride * c + tap % 3 - 1)
                if at in ins:
                    picks[tap, row, ins[at]] = 1.0
        return picks.reshape(9 * self.OUT, -1)

    def every_second(self):
        ins, outs = self.pixels(False), self.pixels(True)
        picks = np.zeros((self.OUT, self.IN), np.float32)
        for (group, crop, r, c), row in outs.items():
            picks[row, ins[group, crop, 2 * r, 2 * c]] = 1.0
        return picks


def dot(a, b):
    return jnp.dot(a, b, preferred_element_type=F32)


def dot_nt(a, b):
    return lax.dot_general(a, b, (((1,), (1,)), ((), ())), preferred_element_type=F32)


def dot_tn(a, b):
    return lax.dot_general(a, b, (((0,), (0,)), ((), ())), preferred_element_type=F32)


def sigmoid(v):
    return 0.5 * jnp.tanh(0.5 * v) + 0.5


def slope_of(v):
    s = sigmoid(v)
    return s * (1.0 + v * (1.0 - s))


def runs_of(n_big, n_all, rows):
    runs = []
    for first in range(0, rows, CH):
        kind = (min(max(n_big - first, 0), CH), min(max(n_all - first, 0), CH))
        if runs and runs[-1][2:] == kind:
            runs[-1] = (runs[-1][0], runs[-1][1] + 1) + kind
        else:
            runs.append((first, 1) + kind)
    return runs


def row_ids():
    return lax.broadcasted_iota(jnp.int32, (CH, W), 0)


def part(v, low, high):
    if low >= high:
        return None
    if low == 0 and high == CH:
        return v
    r = row_ids()
    return jnp.where((r >= low) & (r < high), v, 0.0)


def pick(vb, vs, bc):
    if bc == CH:
        return vb
    if bc == 0:
        return vs
    return jnp.where(row_ids() < bc, vb, vs)


def each_step(blocks, runs, body, carry):
    def one_block(b, carry):
        for first, length, bc, vc in runs:
            if length == 1:
                carry = body(b, first, bc, vc, carry)
            else:
                carry = lax.fori_loop(
                    0,
                    length,
                    lambda i, c: body(b, pl.multiple_of(first + CH * i, CH), bc, vc, c),
                    carry,
                    unroll=min(length, 4) if length % min(length, 4) == 0 else 1,
                )
        return carry

    if blocks == 1:
        return one_block(0, carry)
    return lax.fori_loop(0, blocks, one_block, carry)


def reduce_rows(blocks, runs, fn, count):
    def body(b, first, bc, vc, carry):
        values = fn(b, first, bc, vc)
        new = []
        for i, v in enumerate(values):
            for g, piece in enumerate((part(v, 0, bc), part(v, bc, vc))):
                total = carry[g * count + i]
                new.append((g * count + i, total if piece is None else total + piece[:8] + piece[8:]))
        return tuple(v for _, v in sorted(new, key=lambda t: t[0]))

    zero = jnp.zeros((8, W), F32)
    totals = each_step(blocks, runs, body, (zero,) * (2 * count))
    return [jnp.sum(t, axis=0, keepdims=True) for t in totals]


def map_rows(blocks, runs, fn):
    def body(b, first, bc, vc, carry):
        fn(b, first, bc, vc)
        return carry

    each_step(blocks, runs, body, 0)


def make_kernel(geo, R, NP, MICRO, SR, PC):
    G = R // MICRO
    N = R // 2
    PR = SR // PC
    RW = SR // (NQ * LANES)
    PRQ = up16(RW * LANES)
    IN, OUT = geo.IN, geo.OUT
    ROWS = MICRO * OUT
    runs_in = runs_of(geo.in_big, geo.in_all, IN)
    runs_out = runs_of(geo.out_big, geo.out_all, OUT)
    count_in = (float(R * geo.in_big), float(R * (geo.in_all - geo.in_big)))
    count_out = (float(R * geo.out_big), float(R * (geo.out_all - geo.out_big)))
    RA, RB = radix(R, 8), radix(G, 4)
    n1 = C_IN
    n2 = 9 * C_MID
    n3 = C_MID + C_IN
    nab = C_OUT + 9 * C_MID
    nabc = nab + C_OUT
    S2 = -(-n3 // RW)

    def kernel(
        x_h, cot_h, gate_big, gate_small, width_step, w4_h, w16_h, nt, p2, pb, ps,
        ob_o, os_o, gb_o, gs_o, dw_o, ng_o,
        wbuf, raw, xb, gate_v, gateb, keep, stage, rbig, ssm, rsm, fw, dwide, col, tgb, tmp, mrecv, srecv, orecv,
        dwl, pbuf, rv, nt2,
        own_a, rcv_a, mid_a, out_a, own_b, rcv_b, mid_b, out_b, par, cof, ngs, ngr,
        ld, raw_s, big_s, big_r, sm_s, sm_t, sm_r, up_s, up_r, xs_s, xs_r, ct_s, ct_r, gt_s, gt_r, w_s, w_r, nt_s, nt_r,
        out_s, out_r, mn_s, mn_r, sb_s, sb_r, sta_s, sta_r, stc_s, stc_r, stb_s, stb_r, std_s, std_r, stn_s, stn_r,
        pa_s, pa_r, ch_s, ch_r,
    ):
        me_p, me_d = lax.axis_index("pipe"), lax.axis_index("dp")
        my_m, my_c = me_d // G, me_d % G
        core = lax.rem(me_d, 2)
        sibling = me_d + 1 - 2 * core
        full = pl.ds(0, ROWS)

        def remote(src, dst, ss, rs, p, d):
            return pltpu.make_async_remote_copy(
                src_ref=src, dst_ref=dst, send_sem=ss, recv_sem=rs, device_id=(p, d), device_id_type=MESH
            )

        def push(src, dst, ss, rs, p, d):
            here = (me_p == p) & (me_d == d)

            @pl.when(here)
            def _():
                pltpu.make_async_copy(src, dst, rs).start()

            @pl.when(jnp.logical_not(here))
            def _():
                remote(src, dst, ss, rs, p, d).start()

        def pushed(src, dst, ss, rs, p, d):
            @pl.when(jnp.logical_not((me_p == p) & (me_d == d)))
            def _():
                remote(src, dst, ss, rs, p, d).wait_send()

        def arrived(dst, rs):
            remote(dst, dst, rs, rs, me_p, me_d).wait_recv()

        def sent(src, ss):
            remote(src, src, ss, ss, me_p, me_d).wait_send()

        def spread_out(src, target, ss, rs, base, place, step, count):
            def one(k, c):
                peer = base + step * lax.rem(place + k, count)
                remote(src, target.at[k - 1], ss, rs, me_p, peer).start()
                return c

            lax.fori_loop(1, count, one, 0, unroll=count <= 8)

        def gather_up(first, received, count):
            return lax.fori_loop(0, count - 1, lambda k, t: t + received[k], first, unroll=count <= 8)

        def summer(own, rcv, mid, out, s1, r1, s2, r2, base, place, count, inner):
            low, high = lax.rem(place, inner), place // inner
            outer = count // inner

            def send(slot):
                spread_out(own.at[slot], rcv.at[slot], s1.at[slot], r1.at[slot], base + high * inner, low, 1, inner)

            def total(slot):
                arrived(rcv.at[slot], r1.at[slot])
                sums = gather_up(own[slot], rcv.at[slot], inner)
                if outer > 1:
                    mid[slot] = sums
                    spread_out(mid.at[slot], out.at[slot], s2.at[slot], r2.at[slot], base + low, high, inner, outer)
                    arrived(out.at[slot], r2.at[slot])
                    sums = gather_up(sums, out.at[slot], outer)
                return sums

            def drain(slot):
                sent(rcv.at[slot], s1.at[slot])
                if outer > 1:
                    sent(out.at[slot], s2.at[slot])

            return send, total, drain

        send_a, total_a, drain_a = summer(
            own_a, rcv_a, mid_a, out_a, sta_s, sta_r, stc_s, stc_r, 0, me_d, R, RA
        )
        send_b, total_b, drain_b = summer(
            own_b, rcv_b, mid_b, out_b, stb_s, stb_r, std_s, std_r, my_m * G, my_c, G, RB
        )

        def put(ref, slot, sums):
            for i, s in enumerate(sums):
                ref[slot, pl.ds(i, 1), :] = s

        def finish_norm(total, slot, table, cb, counts):
            for g in (0, 1):
                mean = total[2 * g : 2 * g + 1] * (1.0 / counts[g])
                var = total[2 * g + 1 : 2 * g + 2] * (1.0 / counts[g]) - mean * mean
                rstd = lax.rsqrt(var + EPS)
                scale = rstd * table[cb, 2 * g : 2 * g + 1, :]
                par[slot, pl.ds(4 * g, 1), :] = mean
                par[slot, pl.ds(4 * g + 1, 1), :] = rstd
                par[slot, pl.ds(4 * g + 2, 1), :] = scale
                par[slot, pl.ds(4 * g + 3, 1), :] = table[cb, 2 * g + 1 : 2 * g + 2, :] - mean * scale

        def param(slot, i, bc):
            return pick(par[slot, pl.ds(i, 1), :], par[slot, pl.ds(4 + i, 1), :], bc)

        def normed(u, slot, bc):
            return u * param(slot, 2, bc) + param(slot, 3, bc)

        def centered(u, slot, bc):
            return (u - param(slot, 0, bc)) * param(slot, 1, bc)

        def put_cof(slot, total, counts):
            for g in (0, 1):
                cof[slot, pl.ds(2 * g, 2), :] = total[2 * g : 2 * g + 2] * (1.0 / counts[g])

        def back(d, z, cslot, zslot, pslot, bc, vc):
            a = pick(cof[cslot, pl.ds(0, 1), :], cof[cslot, pl.ds(2, 1), :], bc)
            b = pick(cof[zslot, pl.ds(1, 1), :], cof[zslot, pl.ds(3, 1), :], bc)
            du = param(pslot, 2, bc) * (d - a - z * b)
            return (du if vc == CH else part(du, 0, vc) if vc else jnp.zeros_like(du)).astype(BF)

        def kept(v, m, bc):
            return v if bc == CH else v * pick(jnp.ones((1, W), F32), keep[m], bc)

        def rows(first, n=CH):
            return pl.ds(first, n)

        def at(b, first):
            return pl.ds(pl.multiple_of(b * OUT + first, CH), CH)

        def block(k):
            return pl.ds(pl.multiple_of(k * OUT, CH), OUT)

        def weight(first):
            return wbuf[pl.ds(pl.multiple_of(first, W), W), :]

        def squares(load):
            def sums(b, f, bc, vc):
                u = load(b, f)
                return (u, u * u)

            return sums

        def add_norm_grads(ref, cb, total):
            for g in (0, 1):
                ref[cb, pl.ds(2 * g, 1), :] += total[2 * g + 1 : 2 * g + 2]
                ref[cb, pl.ds(2 * g + 1, 1), :] += total[2 * g : 2 * g + 1]

        SLOTS, HW = raw.shape[0], raw.shape[2]

        def fetch(count, source, target):
            def copies(b, slot):
                return [
                    pltpu.make_async_copy(source(b, lane), raw.at[slot, lane], raw_s.at[slot, lane])
                    for lane in range(LANES)
                ]

            for ahead in range(min(SLOTS - 1, count)):
                for copy in copies(ahead, ahead):
                    copy.start()

            def one(b, c):
                slot = lax.rem(b, SLOTS)

                @pl.when(b + SLOTS - 1 < count)
                def _():
                    for copy in copies(b + SLOTS - 1, lax.rem(b + SLOTS - 1, SLOTS)):
                        copy.start()

                for lane, copy in enumerate(copies(b, slot)):
                    copy.wait()
                    values = raw[slot, lane, :, 0, :].astype(F32).astype(BF)
                    wbuf[pl.ds(pl.multiple_of(target(b), HW), HW), pl.ds(lane * 128, 128)] = values
                return c

            lax.fori_loop(0, count, one, 0)

        def fetch_narrow(count):
            fetch(count // HW, lambda b, lane: w4_h.at[pl.ds(b * HW, HW), lane], lambda b: b * HW)

        def fetch_wide(first, count, target):
            per = count // HW
            fetch(
                NQ * per,
                lambda b, lane: w16_h.at[pl.ds(first + lax.rem(b, per) * HW, HW), b // per * LANES + lane],
                lambda b: target(b // per) + lax.rem(b, per) * HW,
            )

        def halves(count):
            return [core * (count // 2) + i for i in range(count // 2)]

        def ship(source, target, q, ss, p):
            return remote(wbuf.at[pl.ds(source(q), W)], wbuf.at[pl.ds(target(q), W)], ss.at[q], w_r.at[q], p, me_d)

        def pass_on(target, count, go):
            for q in halves(count):
                ref = wbuf.at[pl.ds(target(q), W)]
                go(ref, q, remote(ref, ref, w_s.at[q], w_r.at[q], me_p, sibling))

        def take(target, count):
            def first(ref, q, copy):
                arrived(ref, w_r.at[q])
                copy.start()

            pass_on(target, count, first)
            for i in range(count // 2):
                q = (1 - core) * (count // 2) + i
                arrived(wbuf.at[pl.ds(target(q), W)], w_r.at[q])

        def w1_at(q):
            return pl.multiple_of(n2 + q * W, W)

        def w3_at(q):
            return pl.multiple_of(nabc + q * W, W)

        def w3_between(q):
            return pl.multiple_of(n1 + q * W, W)

        def lay_narrow(first, grad):
            for lane in range(LANES):
                tmp[pl.ds(first + lane, W, stride=LANES), :] = grad[:, lane * 128 : (lane + 1) * 128]

        def keep_narrow(first, grad):
            lay_narrow(0, grad)
            start = pl.multiple_of(first * LANES, W)
            dwl[pl.ds(start, W * LANES), :] = tmp[pl.ds(0, W * LANES), :].astype(BF)

        def keep_wide(first, lhs, index):
            step = NQ * LANES
            for half in range(W // HALF):
                for q in range(NQ):
                    grad = dot_tn(lhs(pl.ds(half * HALF, HALF)), dwide[index + q, full, :])
                    for lane in range(LANES):
                        part_of = grad[:, lane * 128 : (lane + 1) * 128]
                        tmp[pl.ds(q * LANES + lane, HALF, stride=step), :] = part_of
                dwl[pl.ds((first + half * HALF) * step, HALF * step), :] = tmp[pl.ds(0, HALF * step), :].astype(BF)

        class Reduction:
            def __init__(self, pieces, rows_of, start, used):
                self.pieces, self.rows_of, self.start, self.used = pieces, rows_of, start, used
                self.step = next(a for a in (64, 48, 32, 16) if rows_of % a == 0)
                self.i = me_d // 2

            def at(self, pc):
                return pl.ds(pl.multiple_of(pc * self.rows_of, CH), self.rows_of)

            def each(self, pcs, fn):
                if len(pcs) == 1:
                    fn(pcs[0])
                    return

                def one(pc, c):
                    fn(pc)
                    return c

                lax.fori_loop(pcs[0], pcs[-1] + 1, one, 0)

            def pair(self, t, pc):
                src = dwl.at[pl.ds(pl.multiple_of(self.start(2 * t + 1 - core, pc), CH), self.rows_of)]
                return remote(src, pbuf.at[t, self.at(pc)], pa_s.at[t, pc], pa_r.at[t, pc], me_p, sibling)

            def rightward(self, t, pc):
                ref = rv.at[t, self.at(pc)]
                return remote(ref, ref, ch_s.at[t, pc], ch_r.at[t, pc], me_p, me_d + 2)

            def leftward(self, t, pc):
                slot = jnp.where(t == self.i - 1, N, t)
                src, dst = rv.at[t, self.at(pc)], rv.at[slot, self.at(pc)]
                return remote(src, dst, ch_s.at[t, pc], ch_r.at[slot, pc], me_p, me_d - 2)

            def add(self, t, pc, others, store):
                first, step = self.start(2 * t + core, pc), self.step

                def one(s, c):
                    at_s = pl.ds(pl.multiple_of(pc * self.rows_of + s * step, CH), step)
                    v = dwl[pl.ds(pl.multiple_of(first + s * step, CH), step), :].astype(F32)
                    v += pbuf[t, at_s, :].astype(F32)
                    for slot in others:
                        v += rv[slot, at_s, :].astype(F32)
                    store(at_s, s, v)
                    return c

                lax.fori_loop(0, self.rows_of // step, one, 0)

            def send_pairs(self, pcs, low=0, high=N):
                def one(j, c):
                    t = jnp.where(lax.rem(j, 2) == 0, high - 1 - j // 2, low + j // 2)

                    def send(pc):
                        @pl.when(self.used(2 * t + 1 - core, pc))
                        def _():
                            self.pair(t, pc).start()

                    self.each(pcs, send)
                    return c

                lax.fori_loop(0, high - low, one, 0)

            def forward(self, t, pc, wanted, received, copy):
                def store(at_s, s, v):
                    rv[t, at_s, :] = v.astype(BF)

                @pl.when(wanted & self.used(2 * t + core, pc))
                def _():
                    self.pair(t, pc).wait_recv()
                    if received:
                        arrived(rv.at[t, self.at(pc)], ch_r.at[t, pc])
                    self.add(t, pc, (t,) if received else (), store)
                    copy(t, pc).start()

            def originate(self, pcs, low=0, high=N):
                def one(j, c):
                    right, left = high - 1 - j, low + j

                    def both(pc):
                        self.forward(right, pc, (self.i == 0) & (right > 0), False, self.rightward)
                        self.forward(left, pc, (self.i == N - 1) & (left < N - 1), False, self.leftward)

                    self.each(pcs, both)
                    return c

                lax.fori_loop(0, high - low, one, 0)

            def relay(self, pcs, low=0, high=N):
                def one(j, c):
                    right, left = high - 1 - j, low + j

                    def both(pc):
                        self.forward(right, pc, (self.i > 0) & (right > self.i), True, self.rightward)
                        self.forward(left, pc, (self.i < N - 1) & (left < self.i), True, self.leftward)

                    self.each(pcs, both)
                    return c

                lax.fori_loop(0, high - low, one, 0)

            def finish(self, pc, store):
                i = self.i

                @pl.when(self.used(2 * i + core, pc))
                def _():
                    self.pair(i, pc).wait_recv()
                    for low, high in ((True, True), (True, False), (False, True)):

                        @pl.when(((i > 0) == low) & ((i < N - 1) == high))
                        def _(low=low, high=high):
                            others = ()
                            if low:
                                arrived(rv.at[i, self.at(pc)], ch_r.at[i, pc])
                                others += (i,)
                            if high:
                                arrived(rv.at[N, self.at(pc)], ch_r.at[N, pc])
                                others += (N,)
                            self.add(i, pc, others, store)

            def drain(self):
                def one(j, c):
                    def waits(pc):
                        @pl.when(self.used(2 * j + 1 - core, pc))
                        def _():
                            self.pair(j, pc).wait_send()

                        @pl.when((j > self.i) & self.used(2 * j + core, pc))
                        def _():
                            self.rightward(j, pc).wait_send()

                        @pl.when((j < self.i) & self.used(2 * j + core, pc))
                        def _():
                            self.leftward(j, pc).wait_send()

                    self.each(range(self.pieces), waits)
                    return c

                lax.fori_loop(0, N, one, 0)

        def weights_out():
            copy = pltpu.make_async_copy(tmp.at[pl.ds(0, SR)], dw_o, ld.at[1])
            copy.start()
            copy.wait()

        everything = range(PC)

        def flat(used_rows):
            filled = -(-used_rows // PR) * PR
            if filled > used_rows:
                dwl[pl.ds(used_rows, filled - used_rows), :] = jnp.zeros((filled - used_rows, 128), BF)
            return Reduction(PC, PR, lambda s, pc: s * SR + pc * PR, lambda s, pc: s * SR + pc * PR < used_rows)

        def launch(red, low=0, high=N):
            red.send_pairs(everything, low, high)
            red.originate(everything, low, high)

        def finish_flat(red):
            tmp[pl.ds(0, SR), :] = jnp.zeros((SR, 128), F32)

            def finish(pc):
                def store(at_s, s, v):
                    tmp[pl.ds(pl.multiple_of(pc * PR + s * red.step, CH), red.step), :] = v

                red.finish(pc, store)

            red.each(everything, finish)
            weights_out()
            red.drain()

        barrier = pltpu.get_barrier_semaphore()
        load_x = pltpu.make_async_copy(x_h, xb.at[:, pl.ds(0, IN)], ld.at[0])

        @pl.when(me_p < 3)
        def _():
            load_x.start()

        def greet(i, c):
            p, d = i // R, lax.rem(i, R)

            @pl.when((p != me_p) | (d != me_d))
            def _():
                pl.semaphore_signal(barrier, inc=1, device_id=(p, d), device_id_type=MESH)

            return c

        lax.fori_loop(0, NP * R, greet, 0)

        @pl.when(me_p == 0)
        def _():
            fetch_narrow(n1)

        @pl.when(me_p == 2)
        def _():
            fetch_wide(0, C_MID, lambda q: q * n3)

        ng_o[...] = jnp.zeros_like(ng_o)
        ngs[...] = jnp.zeros_like(ngs)
        for m in range(MICRO):
            lanes = lax.broadcasted_iota(jnp.int32, (1, W), 1)
            keep[m] = jnp.where(lanes < C_MID * width_step[m] // 4, 1.0, 0.0)

        pl.semaphore_wait(barrier, NP * R - 1)

        def lay_out(values, lanes, big_o, small_o, big_rows, side):
            fw[0, pl.ds(0, values.shape[0]), :] = values
            for r in range(big_rows // side):
                big_o[r, :, lanes] = fw[0, pl.ds(r * side, side), :].astype(BF)
            crops = geo.crops[1]
            for p in range(small_o.shape[0]):
                small_o[p, :, lanes] = fw[0, pl.ds(big_rows + p * crops, crops), :].astype(BF)

        def finals():
            arrived(orecv, out_r)
            for q in range(NQ):
                lay_out(orecv[q].astype(F32), pl.ds(q * W, W), ob_o, os_o, geo.out_big, geo.sides[0] // 2)
            arrived(srecv, sb_r)
            arrived(mrecv, mn_r)
            for h in range(2):
                total = mrecv[h].astype(F32) + dot_tn(ps[...], srecv[h])
                lay_out(total, pl.ds(h * W, W), gb_o, gs_o, geo.in_big, geo.sides[0])

        def sub_hop(k):
            ref = col.at[pl.ds(6, 2), k]
            return remote(ref, ref, xs_s.at[k], xs_r.at[k], 0, me_d)

        def sub_back(k):
            return (col.at[pl.ds(6, 2), k], srecv, sb_s.at[k], sb_r, my_m, k * G + my_c)

        def nt_copy(count):
            return remote(nt.at[pl.ds(0, count)], nt2.at[pl.ds(0, count)], nt_s, nt_r, me_p + 1, me_d)

        def main_copy(m):
            return (tgb.at[pl.ds(2 * m, 2), pl.ds(0, IN)], mrecv, mn_s.at[m], mn_r, m, me_d)

        def w1_here(q):
            return pl.multiple_of(q * W, W)

        def section_0(m, first):
            fw[m, pl.ds(0, IN), :] = dot(xb[2 * m, pl.ds(0, IN), :], weight(first)) + dot(
                xb[2 * m + 1, pl.ds(0, IN), :], weight(first + W)
            )
            put(own_a, m, reduce_rows(1, runs_in, squares(lambda b, f: fw[m, rows(f), :]), 2))
            send_a(m)

        @pl.when(me_p == 0)
        def _():
            for q in halves(2):
                ship(w1_here, w1_at, q, w_s, 1).start()
            nt_copy(1).start()
            for q in halves(NQ):
                arrived(wbuf.at[pl.ds(w3_between(q), W)], w_r.at[q])
                ship(w3_between, w3_at, q, big_s, 3).start()
            load_x.wait()

            def first(m, c):
                section_0(m, 0)
                return c

            lax.fori_loop(0, MICRO, first, 0)
            for m in range(MICRO):
                finish_norm(total_a(m), m, nt, 0, count_in)

            def back_sums(m):
                arrived(rbig.at[m, pl.ds(0, IN)], big_r.at[m])

                def sums(b, f, bc, vc):
                    u = fw[m, rows(f), :]
                    d = kept(rbig[m, rows(f), :].astype(F32) * slope_of(normed(u, m, bc)), m, bc)
                    fw[MICRO + m, rows(f), :] = d
                    return (d, d * centered(u, m, bc))

                put(own_a, MICRO + m, reduce_rows(1, runs_in, sums, 2))
                send_a(MICRO + m)

            def dx(m):
                total = total_a(MICRO + m)
                put_cof(0, total, count_in)
                add_norm_grads(ng_o, 0, total)

                def grad(b, f, bc, vc):
                    z = centered(fw[m, rows(f), :], m, bc)
                    dwide[m, rows(f), :] = back(fw[MICRO + m, rows(f), :], z, 0, 0, m, bc, vc)

                map_rows(1, runs_in, grad)
                for h in range(2):
                    tgb[2 * m + h, pl.ds(0, IN), :] = dot_nt(dwide[m, pl.ds(0, IN), :], weight(h * W)).astype(BF)
                push(*main_copy(m))

            def backward(step, c):
                @pl.when(step < MICRO)
                def _():
                    back_sums(step)

                @pl.when(step > 0)
                def _():
                    dx(step - 1)

                return c

            lax.fori_loop(0, MICRO + 1, backward, 0)
            for h in range(2):
                total = dot_tn(xb[h, pl.ds(0, IN), :], dwide[0, pl.ds(0, IN), :])
                for m in range(1, MICRO):
                    total += dot_tn(xb[2 * m + h, pl.ds(0, IN), :], dwide[m, pl.ds(0, IN), :])
                keep_narrow(h * W, total)
            red = flat(n1 * LANES)
            launch(red)
            for k in range(MICRO):
                arrived(col.at[pl.ds(6, 2), k], xs_r.at[k])
                push(*sub_back(k))
            red.relay(everything)
            finish_flat(red)
            finals()
            for slot in range(2 * MICRO):
                drain_a(slot)
            for q in halves(2):
                ship(w1_here, w1_at, q, w_s, 1).wait_send()
            for q in halves(NQ):
                ship(w3_between, w3_at, q, big_s, 3).wait_send()
            nt_copy(1).wait_send()
            for m in range(MICRO):
                pushed(*main_copy(m))
                pushed(*sub_back(m))

        @pl.when(me_p == 1)
        def _():
            A2, D2 = MICRO, MICRO + 1
            fetch_narrow(n2)
            load_x.wait()
            take(w1_at, 2)
            arrived(nt2.at[pl.ds(0, 1)], nt_r)

            def first(m, c):
                section_0(m, n2)
                return c

            lax.fori_loop(0, MICRO, first, 0)

            def windows(m, c):
                finish_norm(total_a(m), m, nt2, 0, count_in)

                def act(b, f, bc, vc):
                    n = normed(fw[m, rows(f), :], m, bc)
                    stage[m, rows(f), :] = kept(n * sigmoid(n), m, bc).astype(BF)

                map_rows(1, runs_in, act)
                col[:, m] = dot(p2[...], stage[m, pl.ds(0, IN), :]).astype(BF).reshape(9, OUT, W)
                return c

            def conv(tap, c):
                fw[A2, full, :] += dot(col[tap].reshape(ROWS, W), weight(tap * C_MID))
                return c

            def conv_sums(m, c):
                put(own_a, MICRO + m, reduce_rows(1, runs_out, squares(lambda b, f: fw[A2, at(m, f), :]), 2))
                send_a(MICRO + m)
                return c

            def a2_copy(m):
                return remote(ssm.at[m], rsm.at[my_m], sm_s.at[m], sm_r.at[my_m], 3, m * G + my_c)

            def give(m, c):
                slot = MICRO + m
                finish_norm(total_a(slot), slot, nt, 0, count_out)

                def act(b, f, bc, vc):
                    n = normed(fw[A2, at(m, f), :], slot, bc)
                    ssm[m, rows(f), :] = kept(n * sigmoid(n), m, bc).astype(BF)

                map_rows(1, runs_out, act)
                a2_copy(m).start()
                return c

            lax.fori_loop(0, MICRO, windows, 0)
            fw[A2, full, :] = dot(col[0].reshape(ROWS, W), weight(0))
            lax.fori_loop(1, 9, conv, 0)
            lax.fori_loop(0, MICRO, conv_sums, 0)
            lax.fori_loop(0, MICRO, give, 0)

            def back_two(m):
                arrived(rsm.at[m], sm_r.at[m])
                slot = MICRO + m

                def sums(b, f, bc, vc):
                    u = fw[A2, at(m, f), :]
                    d = kept(rsm[m, rows(f), :].astype(F32) * slope_of(normed(u, slot, bc)), m, bc)
                    fw[D2, at(m, f), :] = d
                    return (d, d * centered(u, slot, bc))

                put(own_a, 2 * MICRO + m, reduce_rows(1, runs_out, sums, 2))
                send_a(2 * MICRO + m)

            def back_mid(m):
                total = total_a(2 * MICRO + m)
                slot = MICRO + m
                put_cof(0, total, count_out)
                add_norm_grads(ng_o, 0, total)

                def grad(b, f, bc, vc):
                    z = centered(fw[A2, at(m, f), :], slot, bc)
                    dwide[0, at(m, f), :] = back(fw[D2, at(m, f), :], z, 0, 0, slot, bc, vc)

                map_rows(1, runs_out, grad)

            def back_taps(tap, c):
                tgb[tap, full, :] = dot_nt(dwide[0, full, :], weight(tap * C_MID)).astype(BF)
                return c

            def back_one(m, c):
                taps = tgb[:, block(m), :].reshape(9 * OUT, W)
                stage[m, pl.ds(0, IN), :] = dot_tn(p2[...], taps).astype(BF)
                da1_copy(m).start()
                return c

            def da1_copy(m):
                ref = pl.ds(0, IN)
                return remote(stage.at[m, ref], rbig.at[m, ref], big_s.at[m], big_r.at[m], 0, me_d)

            def backward(step, c):
                @pl.when(step < MICRO)
                def _():
                    back_two(step)

                @pl.when(step > 0)
                def _():
                    back_mid(step - 1)

                return c

            def weights(tap, c):
                keep_narrow(tap * C_MID, dot_tn(col[tap].reshape(ROWS, W), dwide[0, full, :]))
                return c

            lax.fori_loop(0, MICRO + 1, backward, 0)
            lax.fori_loop(0, 9, back_taps, 0)
            lax.fori_loop(0, MICRO, back_one, 0)
            lax.fori_loop(0, 9, weights, 0)
            red = flat(n2 * LANES)
            red.send_pairs(everything)
            red.originate(everything)
            red.relay(everything)
            finals()
            finish_flat(red)
            pass_on(w1_at, 2, lambda ref, q, copy: copy.wait_send())
            for m in range(MICRO):
                da1_copy(m).wait_send()
                a2_copy(m).wait_send()
            for slot in range(3 * MICRO):
                drain_a(slot)

        def share_copy(k):
            return remote(ngs, ngr.at[k - 1], stn_s.at[k - 1], stn_r.at[k - 1], me_p, lax.rem(me_d + k * G, R))

        def share_norm_grads():
            ngs[...] = ng_o[...]
            for k in range(1, MICRO):
                share_copy(k).start()

        def take_norm_grads():
            for k in range(1, MICRO):
                arrived(ngr.at[k - 1], stn_r.at[k - 1])
                ng_o[...] += ngr[k - 1]
            for k in range(1, MICRO):
                share_copy(k).wait_send()

        def sub_copy(m):
            return (col.at[pl.ds(4, 2), m], col.at[pl.ds(0, 2), my_m], xs_s.at[m], xs_r.at[my_m], 2, m * G + my_c)

        def w3_here(q):
            return pl.multiple_of(q * n3, W)

        @pl.when(me_p == 2)
        def _():
            for q in halves(NQ):
                ship(w3_here, w3_between, q, w_s, 0).start()
            nt_copy(NQ).start()
            load_x.wait()

            def send_x(m, c):
                for h in range(2):
                    col[4 + h, m] = dot(ps[...], xb[2 * m + h, pl.ds(0, IN), :]).astype(BF)
                push(*sub_copy(m))
                return c

            lax.fori_loop(0, MICRO, send_x, 0)
            fetch_wide(C_MID, C_IN, lambda q: q * n3 + C_MID)
            for k in range(MICRO):
                arrived(col.at[pl.ds(0, 2), k], xs_r.at[k])

            def w3(q):
                return weight(q * n3)

            def wp(q, h):
                return weight(q * n3 + C_MID + h * W)

            def xsub(h):
                return col[h].reshape(ROWS, W)

            def product(index, value, slot):
                fw[index, full, :] = value
                put(own_b, slot, reduce_rows(MICRO, runs_out, squares(lambda b, f: fw[index, at(b, f), :]), 2))
                send_b(slot)

            def up_copy(q):
                return remote(stage.at[q, full], stage.at[q, full], up_s.at[q], up_r.at[q], 3, me_d)

            def short(q):
                product(NQ + q, dot(xsub(0), wp(q, 0)) + dot(xsub(1), wp(q, 1)), NQ + q)

            def short_out(q):
                finish_norm(total_b(NQ + q), NQ + q, nt, NQ + q, count_out)

                def act(b, f, bc, vc):
                    stage[q, at(b, f), :] = normed(fw[NQ + q, at(b, f), :], NQ + q, bc).astype(BF)

                map_rows(MICRO, runs_out, act)
                up_copy(q).start()

            def shorts(step, c):
                @pl.when(step < NQ)
                def _():
                    short(step)

                @pl.when(step > 0)
                def _():
                    short_out(step - 1)

                return c

            lax.fori_loop(0, NQ + 1, shorts, 0)
            for k in range(MICRO):
                arrived(rsm.at[k], sm_r.at[k])

            def main(q, c):
                product(q, dot(rsm[...].reshape(ROWS, W), w3(q)), q)
                return c

            lax.fori_loop(0, NQ, main, 0)

            def main_norm(q, c):
                finish_norm(total_b(q), q, nt, q, count_out)
                return c

            lax.fori_loop(0, NQ, main_norm, 0)
            tmp[...] = jnp.zeros_like(tmp)
            red = Reduction(
                NQ, PRQ, lambda s, pc: (pc * S2 + s) * PRQ, lambda s, pc: s < S2
            )
            D, SUB = 2 * NQ, 2 * NQ + 1

            def lay_part(s, q):
                start = pl.multiple_of((q * S2 + s) * PRQ, CH)
                at_s = pl.multiple_of(s * RW * LANES, 8)
                dwl[pl.ds(start, RW * LANES), :] = tmp[pl.ds(at_s, RW * LANES), :].astype(BF)

            for q in range(NQ):
                arrived(rbig.at[q, full], big_r.at[q])

                def sums(b, f, bc, vc):
                    um, us = fw[q, at(b, f), :], fw[NQ + q, at(b, f), :]
                    n = normed(um, q, bc) + normed(us, NQ + q, bc)
                    d = rbig[q, at(b, f), :].astype(F32) * slope_of(n)
                    fw[D, at(b, f), :] = d
                    return (d, d * centered(um, q, bc), d * centered(us, NQ + q, bc))

                db, mb, sb, ds, ms, ss = reduce_rows(MICRO, runs_out, sums, 3)
                put(own_b, 2 * NQ + q, (db, mb, ds, ms))
                put(own_b, 3 * NQ + q, (db, sb, ds, ss))
                send_b(2 * NQ + q)
                send_b(3 * NQ + q)
                for i, cb in ((0, q), (1, NQ + q)):
                    total = total_b((2 + i) * NQ + q)
                    put_cof(i, total, count_out)
                    add_norm_grads(ng_o, cb, total)

                def grad(b, f, bc, vc):
                    d = fw[D, at(b, f), :]
                    zm = centered(fw[q, at(b, f), :], q, bc)
                    zs = centered(fw[NQ + q, at(b, f), :], NQ + q, bc)
                    dwide[q, at(b, f), :] = back(d, zm, 0, 0, q, bc, vc)
                    dwide[NQ + q, at(b, f), :] = back(d, zs, 1, 1, NQ + q, bc, vc)

                map_rows(MICRO, runs_out, grad)
                lay_narrow(0, dot_tn(rsm[...].reshape(ROWS, W), dwide[q, full, :]))
                for h in range(2):
                    lay_narrow((1 + h) * W * LANES, dot_tn(xsub(h), dwide[NQ + q, full, :]))

                def lay(s, c):
                    lay_part(s, q)
                    return c

                lax.fori_loop(0, S2, lay, 0)
                red.send_pairs((q,))
                for h in range(2):
                    piece = dot_nt(dwide[NQ + q, full, :], wp(q, h))
                    fw[SUB + h, full, :] = piece if q == 0 else fw[SUB + h, full, :] + piece
                red.originate((q,))

            share_norm_grads()
            for h in range(2):
                for k in range(MICRO):
                    col[6 + h, k] = fw[SUB + h, block(k), :].astype(BF)
            for m in range(MICRO):
                pushed(*sub_copy(m))
            for k in range(MICRO):
                sub_hop(k).start()
            for q in range(NQ):
                red.relay((q,))
            finals()
            take_norm_grads()
            for q in range(NQ):

                def store(at_s, s, v):
                    tmp[pl.ds(pl.multiple_of(SR + s * red.step, CH), red.step), :] = v

                red.finish(q, store)

                @pl.when(red.used(me_d, q))
                def _():
                    for lane in range(LANES):
                        values = tmp[pl.ds(SR + lane, RW, stride=LANES), :]
                        tmp[pl.ds(q * LANES + lane, RW, stride=NQ * LANES), :] = values

            @pl.when(jnp.logical_not(red.used(me_d, 0)))
            def _():
                tmp[pl.ds(0, SR), :] = jnp.zeros((SR, 128), F32)

            weights_out()
            red.drain()
            for q in halves(NQ):
                ship(w3_here, w3_between, q, w_s, 0).wait_send()
            nt_copy(NQ).wait_send()
            for k in range(MICRO):
                sub_hop(k).wait_send()
            for q in range(NQ):
                up_copy(q).wait_send()
            for slot in range(4 * NQ):
                drain_b(slot)

        def cot_copy(m):
            return (cot_h.at[m], xb.at[pl.ds(0, NQ), block(my_m)], ct_s.at[m], ct_r.at[my_m], 3, m * G + my_c)

        def gate_copy(m):
            return (gate_v.at[m], gateb.at[my_m], gt_s.at[m], gt_r.at[my_m], 3, m * G + my_c)

        def out_copy(k):
            return (xb.at[pl.ds(NQ, NQ), block(k)], orecv, out_s.at[k], out_r, my_m, k * G + my_c)

        @pl.when(me_p == 3)
        def _():
            r = lax.broadcasted_iota(jnp.int32, (OUT, 128), 0)
            small = r - geo.out_big
            for m in range(MICRO):
                g = jnp.zeros((OUT, 128), F32)
                for i in range(geo.crops[0]):
                    area = geo.out_big // geo.crops[0]
                    g = jnp.where((r >= i * area) & (r < (i + 1) * area), gate_big[i, m].astype(F32), g)
                for i in range(geo.crops[1]):
                    mine = (small >= 0) & (lax.rem(small + geo.crops[1] * OUT, geo.crops[1]) == i)
                    g = jnp.where(mine, gate_small[i, m].astype(F32), g)
                gate_v[m] = g
            for m in range(MICRO):
                push(*gate_copy(m))
                push(*cot_copy(m))
            fetch_narrow(nab)
            fetch_wide(nab * W // C_OUT, C_MID, lambda q: nab + q * C_MID)
            take(w3_at, NQ)
            arrived(nt2, nt_r)
            A, B, T1, T2, U3 = 2 * NQ, 2 * NQ + 1, 2 * NQ + 2, 2 * NQ + 3, 2 * NQ + 4
            DB, DA, H1, H2 = NQ, NQ + 1, NQ + 2, NQ + 3
            S3, PM = 4 + 2 * NQ, 2 + NQ

            def wa(q):
                return weight(q * W)

            def wb(tap):
                return weight(C_OUT + tap * C_MID)

            def wc(q):
                return weight(nab + q * C_MID)

            def w3(q):
                return weight(nabc + q * C_MID)

            def begin(index, slot):
                put(own_b, slot, reduce_rows(MICRO, runs_out, squares(lambda b, f: fw[index, at(b, f), :]), 2))
                send_b(slot)

            def hidden(index, slot, target):
                def act(b, f, bc, vc):
                    n = normed(fw[index, at(b, f), :], slot, bc)
                    dwide[target, at(b, f), :] = kept(n * sigmoid(n), my_m, bc).astype(BF)

                map_rows(MICRO, runs_out, act)

            def gather(source, target):
                def one(k, c):
                    target(k, dot(pb[...], dwide[source, block(k), :]).astype(BF).reshape(9, OUT, W))
                    return c

                lax.fori_loop(0, MICRO, one, 0)

            def a2_on(k):
                return remote(rsm.at[k], rsm.at[k], sm_t.at[k], sm_r.at[k], 2, me_d)

            for k in range(MICRO):
                arrived(rsm.at[k], sm_r.at[k])
                a2_on(k).start()

            def main(q, c):
                fw[U3 + q, full, :] = dot(rsm[...].reshape(ROWS, W), w3(q))
                begin(U3 + q, S3 + q)
                return c

            lax.fori_loop(0, NQ, main, 0)

            def join(q, c):
                finish_norm(total_b(S3 + q), PM + q, nt2, q, count_out)
                arrived(stage.at[q, full], up_r.at[q])

                def act(b, f, bc, vc):
                    n = normed(fw[U3 + q, at(b, f), :], PM + q, bc) + stage[q, at(b, f), :].astype(F32)
                    rbig[q, at(b, f), :] = (n * sigmoid(n)).astype(BF)

                map_rows(MICRO, runs_out, act)
                return c

            lax.fori_loop(0, NQ, join, 0)
            fw[A, full, :] = sum(dot(rbig[q, full, :], wa(q)) for q in range(NQ))
            begin(A, 0)
            finish_norm(total_b(0), 0, nt, 0, count_out)
            hidden(A, 0, H1)

            def to_col(k, v):
                col[:, k] = v

            gather(H1, to_col)

            fw[B, full, :] = sum(dot(col[tap].reshape(ROWS, W), wb(tap)) for tap in range(9))
            begin(B, 1)
            finish_norm(total_b(1), 1, nt, 1, count_out)
            hidden(B, 1, H2)

            def widen(q, c):
                fw[q, full, :] = dot(dwide[H2, full, :], wc(q))
                begin(q, 2 + q)
                return c

            lax.fori_loop(0, NQ, widen, 0)
            for k in range(MICRO):
                arrived(gateb.at[k], gt_r.at[k])
                arrived(xb.at[pl.ds(0, NQ), block(k)], ct_r.at[k])

            def gate_at(b, f):
                g = gateb[b, rows(f), :]
                return jnp.concatenate([g] * LANES, axis=1)

            def ends(q, c):
                finish_norm(total_b(2 + q), 2 + q, nt, 2 + q, count_out)

                def sums(b, f, bc, vc):
                    u = fw[q, at(b, f), :]
                    g = gate_at(b, f)
                    v = rbig[q, at(b, f), :].astype(F32) + g * normed(u, 2 + q, bc)
                    sg = sigmoid(v)
                    xb[NQ + q, at(b, f), :] = (v * sg).astype(BF)
                    d = xb[q, at(b, f), :].astype(F32) * (sg * (1.0 + v * (1.0 - sg)))
                    fw[NQ + q, at(b, f), :] = d
                    d = g * d
                    return (d, d * centered(u, 2 + q, bc))

                put(own_b, 2 + NQ + q, reduce_rows(MICRO, runs_out, sums, 2))
                send_b(2 + NQ + q)
                return c

            lax.fori_loop(0, NQ, ends, 0)

            def ends_back(q, c):
                total = total_b(2 + NQ + q)
                put_cof(0, total, count_out)
                add_norm_grads(ng_o, 2 + q, total)

                def grad(b, f, bc, vc):
                    z = centered(fw[q, at(b, f), :], 2 + q, bc)
                    d = gate_at(b, f) * fw[NQ + q, at(b, f), :]
                    dwide[q, at(b, f), :] = back(d, z, 0, 0, 2 + q, bc, vc)

                map_rows(MICRO, runs_out, grad)
                return c

            lax.fori_loop(0, NQ, ends_back, 0)
            fw[T1, full, :] = sum(dot_nt(dwide[q, full, :], wc(q)) for q in range(NQ))
            for k in range(MICRO):
                push(*out_copy(k))

            def middle(index, pslot, slot, target):
                def sums(b, f, bc, vc):
                    u = fw[index, at(b, f), :]
                    d = kept(fw[T1, at(b, f), :] * slope_of(normed(u, pslot, bc)), my_m, bc)
                    fw[T2, at(b, f), :] = d
                    return (d, d * centered(u, pslot, bc))

                put(own_b, slot, reduce_rows(MICRO, runs_out, sums, 2))
                send_b(slot)
                total = total_b(slot)
                put_cof(0, total, count_out)
                add_norm_grads(ng_o, pslot, total)

                def grad(b, f, bc, vc):
                    z = centered(fw[index, at(b, f), :], pslot, bc)
                    dwide[target, at(b, f), :] = back(fw[T2, at(b, f), :], z, 0, 0, pslot, bc, vc)

                map_rows(MICRO, runs_out, grad)

            middle(B, 1, 2 + 2 * NQ, DB)

            def to_taps(k, v):
                tgb[:, block(k), :] = v

            gather(DB, to_taps)

            fw[T1, full, :] = sum(dot_nt(tgb[tap, full, :], wb(8 - tap)) for tap in range(9))
            middle(A, 0, 3 + 2 * NQ, DA)

            def dy_copy(q):
                return remote(stage.at[q, full], rbig.at[q, full], big_s.at[q], big_r.at[q], 2, me_d)

            def to_y(q, c):
                fw[T2, full, :] = dot_nt(dwide[DA, full, :], wa(q))

                def sums(b, f, bc, vc):
                    dy = (fw[T2, at(b, f), :] + fw[NQ + q, at(b, f), :]).astype(BF)
                    u = fw[U3 + q, at(b, f), :]
                    n = normed(u, PM + q, bc) + stage[q, at(b, f), :].astype(F32)
                    stage[q, at(b, f), :] = dy
                    d = dy.astype(F32) * slope_of(n)
                    fw[q, at(b, f), :] = d
                    return (d, d * centered(u, PM + q, bc))

                put(own_b, S3 + NQ + q, reduce_rows(MICRO, runs_out, sums, 2))
                send_b(S3 + NQ + q)
                dy_copy(q).start()
                return c

            lax.fori_loop(0, NQ, to_y, 0)

            def through_w3(q, c):
                put_cof(0, total_b(S3 + NQ + q), count_out)

                def grad(b, f, bc, vc):
                    z = centered(fw[U3 + q, at(b, f), :], PM + q, bc)
                    xb[q, at(b, f), :] = back(fw[q, at(b, f), :], z, 0, 0, PM + q, bc, vc)

                map_rows(MICRO, runs_out, grad)
                return c

            lax.fori_loop(0, NQ, through_w3, 0)
            fw[T1, full, :] = sum(dot_nt(xb[q, full, :], w3(q)) for q in range(NQ))

            def da2_copy(k):
                return remote(ssm.at[k], rsm.at[my_m], sm_s.at[k], sm_r.at[my_m], 1, k * G + my_c)

            def back_a2(k, c):
                ssm[k] = fw[T1, block(k), :].astype(BF)
                da2_copy(k).start()
                return c

            lax.fori_loop(0, MICRO, back_a2, 0)

            def weights_a(q, c):
                keep_narrow(q * W, dot_tn(rbig[q, full, :], dwide[DA, full, :]))
                return c

            def weights_b(tap, c):
                keep_narrow(C_OUT + tap * C_MID, dot_tn(col[tap].reshape(ROWS, W), dwide[DB, full, :]))
                return c

            share_norm_grads()
            red = flat(nabc * LANES)
            t1, t2 = (C_OUT + C_MID) * LANES // (2 * SR), -(-(nab - C_MID) * LANES // (2 * SR))
            order = ((t2, N), (0, t1), (t1, t2))
            keep_wide(nab * W // C_OUT, lambda r: dwide[H2, full, r], 0)
            weights_b(8, 0)
            launch(red, *order[0])
            lax.fori_loop(0, NQ, weights_a, 0)
            weights_b(0, 0)
            launch(red, *order[1])
            lax.fori_loop(1, 8, weights_b, 0)
            launch(red, *order[2])
            for low, high in order:
                red.relay(everything, low, high)
            finals()
            take_norm_grads()
            finish_flat(red)
            pass_on(w3_at, NQ, lambda ref, q, copy: copy.wait_send())
            for m in range(MICRO):
                pushed(*gate_copy(m))
                pushed(*cot_copy(m))
                pushed(*out_copy(m))
                da2_copy(m).wait_send()
                a2_on(m).wait_send()
            for q in range(NQ):
                dy_copy(q).wait_send()
            for slot in range(S3 + 2 * NQ):
                drain_b(slot)

    return kernel


def radix(count, most):
    if count <= most:
        return count
    return next(r for r in range(most, 0, -1) if count % r == 0)


def handed_on(arrays):
    count = len(arrays)

    def kernel(*refs):
        for i in range(count):
            refs[count + i][...] = refs[i][...]

    vmem = pl.BlockSpec(memory_space=pltpu.VMEM)
    return pl.pallas_call(
        kernel,
        out_shape=tuple(jax.ShapeDtypeStruct(a.shape, a.dtype) for a in arrays),
        in_specs=[vmem] * count,
        out_specs=(vmem,) * count,
    )(*arrays)


def solution(mesh):
    R, NP = mesh.shape["dp"], mesh.shape["pipe"]

    def on_device(x_big, x_small, cot_big, cot_small, section_weights, section_norms, gate_big, gate_small, width_step):
        MICRO = x_big.shape[0]
        G = R // MICRO
        geo = Geometry((x_big.shape[1], x_small.shape[1]), (x_big.shape[2], x_small.shape[2]))
        IN, OUT, ROWS = geo.IN, geo.OUT, MICRO * geo.OUT
        PW = section_weights.shape[1]
        NB = section_norms.shape[2] // W
        wide = max(IN, ROWS)

        def joined(big, small, width, length):
            parts = [big.reshape(MICRO, -1, width), small.transpose(0, 2, 3, 1, 4).reshape(MICRO, -1, width)]
            v = jnp.concatenate(parts, axis=1)
            return jnp.pad(v, ((0, 0), (0, length - v.shape[1]), (0, 0)))

        x = joined(x_big, x_small, C_IN, IN)
        x = x.reshape(MICRO, IN, 2, W).transpose(0, 2, 1, 3).reshape(2 * MICRO, IN, W)
        cot = joined(cot_big, cot_small, C_OUT, OUT).reshape(MICRO, OUT, NQ, W).transpose(0, 2, 1, 3)
        w4 = section_weights.reshape(PW // W, LANES, 1, 128)
        w16 = section_weights.reshape(PW // C_OUT, NQ * LANES, 1, 128)
        SR = PW // 128 // R
        PC = 4 if SR % (4 * CH) == 0 else 2 if SR % (2 * CH) == 0 else 1
        RW = SR // (NQ * LANES)
        SRP = max(SR, NQ * up16(RW * LANES))
        tmp_rows = max(HALF * NQ * LANES, -(-(C_MID + C_IN) // RW) * RW * LANES, SR + up16(RW * LANES))
        nt = section_norms[0].reshape(4, NB, W).transpose(1, 0, 2)
        p2 = geo.windows(2)
        sub = geo.every_second()
        consts = [p2, geo.windows(1), sub]
        consts = [jnp.asarray(c, BF) for c in consts]
        vmem, hbm = pl.BlockSpec(memory_space=pltpu.VMEM), pl.BlockSpec(memory_space=pl.ANY)
        smem = pl.BlockSpec(memory_space=pltpu.SMEM)
        V, D = pltpu.VMEM, pltpu.SemaphoreType.DMA
        RA, RB = radix(R, 8), radix(G, 4)
        nb, sb, ns, ss = geo.crops[0], geo.sides[0], geo.crops[1], geo.sides[1]
        SA, SB = 3 * MICRO, 4 + 4 * NQ

        def sums(slots, first, all_of):
            later = max(all_of // first - 1, 1)
            kept_slots = slots if all_of > first else 1
            return [
                V((slots, 4, W), F32),
                V((slots, max(first - 1, 1), 4, W), F32),
                V((kept_slots, 4, W), F32),
                V((kept_slots, later, 4, W), F32),
            ]

        results = pl.pallas_call(
            make_kernel(geo, R, NP, MICRO, SR, PC),
            out_shape=(
                jax.ShapeDtypeStruct((nb * sb // 2, sb // 2, C_OUT), BF),
                jax.ShapeDtypeStruct((ss * ss // 4, ns, C_OUT), BF),
                jax.ShapeDtypeStruct((nb * sb, sb, C_IN), BF),
                jax.ShapeDtypeStruct((ss * ss, ns, C_IN), BF),
                jax.ShapeDtypeStruct((SR, 128), F32),
                jax.ShapeDtypeStruct((NB, 4, W), F32),
            ),
            in_specs=[hbm, hbm, smem, smem, smem, hbm, hbm, vmem] + [vmem] * 3,
            out_specs=(vmem, vmem, vmem, vmem, hbm, vmem),
            scratch_shapes=[
                V((PW // W + C_OUT, W), BF),
                V((4, LANES, 128, 1, 128), BF),
                V((2 * MICRO, wide, W), BF),
                V((MICRO, OUT, 128), F32),
                V((MICRO, OUT, 128), F32),
                V((MICRO, 1, W), F32),
                V((NQ, wide, W), BF),
                V((NQ, wide, W), BF),
                V((MICRO, OUT, W), BF),
                V((MICRO, OUT, W), BF),
                V((3 * NQ + 4, wide, W), F32),
                V((2 * NQ, wide, W), BF),
                V((9, MICRO, OUT, W), BF),
                V((9, wide, W), BF),
                V((tmp_rows, 128), F32),
                V((2, IN, W), BF),
                V((2, OUT, W), BF),
                V((NQ, OUT, W), BF),
                V((PW // 128, 128), BF),
                V((R // 2, SRP, 128), BF),
                V((R // 2 + 1, SRP, 128), BF),
                V((NQ, 4, W), F32),
                *sums(SA, RA, R),
                *sums(SB, RB, G),
                V((max(2 * MICRO, 2 + 2 * NQ), 8, W), F32),
                V((2, 4, W), F32),
                V((NB, 4, W), F32),
                V((MICRO - 1, NB, 4, W), F32),
                D((2,)),
                D((4, LANES)),
                D((4,)), D((4,)),
                D((4,)), D((4,)), D((4,)),
                D((4,)), D((4,)),
                D((4,)), D((4,)),
                D((4,)), D((4,)),
                D((4,)), D((4,)),
                D((4,)), D((4,)),
                D, D,
                D((4,)), D,
                D((4,)), D,
                D((4,)), D,
                D((SA,)), D((SA,)), D((SA,)), D((SA,)),
                D((SB,)), D((SB,)), D((SB,)), D((SB,)),
                D((MICRO - 1,)), D((MICRO - 1,)),
                D((R // 2, 4)), D((R // 2, 4)),
                D((R // 2, 4)), D((R // 2 + 1, 4)),
            ],
            compiler_params=pltpu.CompilerParams(
                collective_id=0, has_side_effects=True, vmem_limit_bytes=63 << 20
            ),
        )(x, cot, gate_big.T, gate_small.T, width_step, w4, w16, nt, *consts)

        ob, os, gb, gs, dw, ng = handed_on(results)

        def small(v, side, width):
            return v.reshape(side, side, ns, width).transpose(2, 0, 1, 3)[None]

        return (
            ob.reshape(1, nb, sb // 2, sb // 2, C_OUT),
            small(os, ss // 2, C_OUT),
            gb.reshape(1, nb, sb, sb, C_IN),
            small(gs, ss, C_IN),
            dw.reshape(1, PW // R),
            ng.transpose(1, 0, 2).reshape(1, 4, NB * W),
        )

    images = P(None, "dp", None, None, None)
    ends = P("pipe", "dp", None, None, None)
    return jax.shard_map(
        on_device,
        mesh=mesh,
        in_specs=(images,) * 4 + (P("pipe", None), P("pipe", None, None), P(None, "dp"), P(None, "dp"), P()),
        out_specs=(ends,) * 4 + (P("pipe", "dp"), P("pipe", None, None)),
        check_vma=False,
    )
```

```python
import functools

import jax
import jax.numpy as jnp
import numpy as np
from jax import lax
from jax.experimental import pallas as pl
from jax.experimental.pallas import tpu as pltpu
from jax.sharding import PartitionSpec as P

C_IN = 1024
C_MID = 512
C_OUT = 2048
EPS = 1e-05
W = 512
NQ = C_OUT // W
CH = 16
LANES = W // 128
HALF = W // 2
BF = jnp.bfloat16
F32 = jnp.float32
MESH = pl.DeviceIdType.MESH


def up16(n):
    return -(-n // 16) * 16


class Geometry:
    def __init__(self, crops, sides):
        self.crops, self.sides = crops, sides
        self.in_big = crops[0] * sides[0] ** 2
        self.in_all = self.in_big + crops[1] * sides[1] ** 2
        self.out_big = crops[0] * (sides[0] // 2) ** 2
        self.out_all = self.out_big + crops[1] * (sides[1] // 2) ** 2
        self.IN, self.OUT = up16(self.in_all), up16(self.out_all)

    def pixels(self, halves):
        index, table = 0, {}
        for group in (0, 1):
            side = self.sides[group] // 2 if halves else self.sides[group]
            crops, sides = range(self.crops[group]), range(side)
            if group == 0:
                places = [(crop, r, c) for crop in crops for r in sides for c in sides]
            else:
                places = [(crop, r, c) for r in sides for c in sides for crop in crops]
            for place in places:
                table[(group,) + place] = index
                index += 1
        return table

    def windows(self, stride):
        ins, outs = self.pixels(stride == 1), self.pixels(True)
        picks = np.zeros((9, self.OUT, self.OUT if stride == 1 else self.IN), np.float32)
        for (group, crop, r, c), row in outs.items():
            for tap in range(9):
                at = (group, crop, stride * r + tap // 3 - 1, stride * c + tap % 3 - 1)
                if at in ins:
                    picks[tap, row, ins[at]] = 1.0
        return picks.reshape(9 * self.OUT, -1)

    def every_second(self):
        ins, outs = self.pixels(False), self.pixels(True)
        picks = np.zeros((self.OUT, self.IN), np.float32)
        for (group, crop, r, c), row in outs.items():
            picks[row, ins[group, crop, 2 * r, 2 * c]] = 1.0
        return picks


def dot(a, b):
    return jnp.dot(a, b, preferred_element_type=F32)


def dot_nt(a, b):
    return lax.dot_general(a, b, (((1,), (1,)), ((), ())), preferred_element_type=F32)


def dot_tn(a, b):
    return lax.dot_general(a, b, (((0,), (0,)), ((), ())), preferred_element_type=F32)


def sigmoid(v):
    return 0.5 * jnp.tanh(0.5 * v) + 0.5


def slope_of(v):
    s = sigmoid(v)
    return s * (1.0 + v * (1.0 - s))


def runs_of(n_big, n_all, rows):
    runs = []
    for first in range(0, rows, CH):
        kind = (min(max(n_big - first, 0), CH), min(max(n_all - first, 0), CH))
        if runs and runs[-1][2:] == kind:
            runs[-1] = (runs[-1][0], runs[-1][1] + 1) + kind
        else:
            runs.append((first, 1) + kind)
    return runs


def row_ids():
    return lax.broadcasted_iota(jnp.int32, (CH, W), 0)


def part(v, low, high):
    if low >= high:
        return None
    if low == 0 and high == CH:
        return v
    r = row_ids()
    return jnp.where((r >= low) & (r < high), v, 0.0)


def pick(vb, vs, bc):
    if bc == CH:
        return vb
    if bc == 0:
        return vs
    return jnp.where(row_ids() < bc, vb, vs)


def each_step(blocks, runs, body, carry):
    def one_block(b, carry):
        for first, length, bc, vc in runs:
            if length == 1:
                carry = body(b, first, bc, vc, carry)
            else:
                carry = lax.fori_loop(
                    0,
                    length,
                    lambda i, c: body(b, pl.multiple_of(first + CH * i, CH), bc, vc, c),
                    carry,
                    unroll=min(length, 4) if length % min(length, 4) == 0 else 1,
                )
        return carry

    if blocks == 1:
        return one_block(0, carry)
    return lax.fori_loop(0, blocks, one_block, carry)


def reduce_rows(blocks, runs, fn, count):
    def body(b, first, bc, vc, carry):
        values = fn(b, first, bc, vc)
        new = []
        for i, v in enumerate(values):
            for g, piece in enumerate((part(v, 0, bc), part(v, bc, vc))):
                total = carry[g * count + i]
                new.append((g * count + i, total if piece is None else total + piece[:8] + piece[8:]))
        return tuple(v for _, v in sorted(new, key=lambda t: t[0]))

    zero = jnp.zeros((8, W), F32)
    totals = each_step(blocks, runs, body, (zero,) * (2 * count))
    return [jnp.sum(t, axis=0, keepdims=True) for t in totals]


def map_rows(blocks, runs, fn):
    def body(b, first, bc, vc, carry):
        fn(b, first, bc, vc)
        return carry

    each_step(blocks, runs, body, 0)


def make_kernel(geo, R, NP, MICRO, SR, PC):
    G = R // MICRO
    N = R // 2
    PR = SR // PC
    RW = SR // (NQ * LANES)
    PRQ = up16(RW * LANES)
    IN, OUT = geo.IN, geo.OUT
    ROWS = MICRO * OUT
    runs_in = runs_of(geo.in_big, geo.in_all, IN)
    runs_out = runs_of(geo.out_big, geo.out_all, OUT)
    count_in = (float(R * geo.in_big), float(R * (geo.in_all - geo.in_big)))
    count_out = (float(R * geo.out_big), float(R * (geo.out_all - geo.out_big)))
    RA, RB = radix(R, 8), radix(G, 4)
    n1 = C_IN
    n2 = 9 * C_MID
    n3 = C_MID + C_IN
    nab = C_OUT + 9 * C_MID
    nabc = nab + C_OUT
    S2 = -(-n3 // RW)

    def kernel(
        x_h, cot_h, gate_big, gate_small, width_step, w4_h, w16_h, nt, p2, pb, ps,
        ob_o, os_o, gb_o, gs_o, dw_o, ng_o,
        wbuf, raw, xb, gate_v, gateb, keep, stage, rbig, ssm, rsm, fw, dwide, col, tgb, tmp, mrecv, srecv, orecv,
        dwl, pbuf, rv, nt2,
        own_a, rcv_a, mid_a, out_a, own_b, rcv_b, mid_b, out_b, par, cof, ngs, ngr,
        ld, raw_s, big_s, big_r, sm_s, sm_t, sm_r, up_s, up_r, xs_s, xs_r, ct_s, ct_r, gt_s, gt_r, w_s, w_r, nt_s, nt_r,
        out_s, out_r, mn_s, mn_r, sb_s, sb_r, sta_s, sta_r, stc_s, stc_r, stb_s, stb_r, std_s, std_r, stn_s, stn_r,
        pa_s, pa_r, ch_s, ch_r,
    ):
        me_p, me_d = lax.axis_index("pipe"), lax.axis_index("dp")
        my_m, my_c = me_d // G, me_d % G
        core = lax.rem(me_d, 2)
        sibling = me_d + 1 - 2 * core
        full = pl.ds(0, ROWS)

        def remote(src, dst, ss, rs, p, d):
            return pltpu.make_async_remote_copy(
                src_ref=src, dst_ref=dst, send_sem=ss, recv_sem=rs, device_id=(p, d), device_id_type=MESH
            )

        def push(src, dst, ss, rs, p, d):
            here = (me_p == p) & (me_d == d)

            @pl.when(here)
            def _():
                pltpu.make_async_copy(src, dst, rs).start()

            @pl.when(jnp.logical_not(here))
            def _():
                remote(src, dst, ss, rs, p, d).start()

        def pushed(src, dst, ss, rs, p, d):
            @pl.when(jnp.logical_not((me_p == p) & (me_d == d)))
            def _():
                remote(src, dst, ss, rs, p, d).wait_send()

        def arrived(dst, rs):
            remote(dst, dst, rs, rs, me_p, me_d).wait_recv()

        def sent(src, ss):
            remote(src, src, ss, ss, me_p, me_d).wait_send()

        def spread_out(src, target, ss, rs, base, place, step, count):
            def one(k, c):
                peer = base + step * lax.rem(place + k, count)
                remote(src, target.at[k - 1], ss, rs, me_p, peer).start()
                return c

            lax.fori_loop(1, count, one, 0, unroll=count <= 8)

        def gather_up(first, received, count):
            return lax.fori_loop(0, count - 1, lambda k, t: t + received[k], first, unroll=count <= 8)

        def summer(own, rcv, mid, out, s1, r1, s2, r2, base, place, count, inner):
            low, high = lax.rem(place, inner), place // inner
            outer = count // inner

            def send(slot):
                spread_out(own.at[slot], rcv.at[slot], s1.at[slot], r1.at[slot], base + high * inner, low, 1, inner)

            def total(slot):
                arrived(rcv.at[slot], r1.at[slot])
                sums = gather_up(own[slot], rcv.at[slot], inner)
                if outer > 1:
                    mid[slot] = sums
                    spread_out(mid.at[slot], out.at[slot], s2.at[slot], r2.at[slot], base + low, high, inner, outer)
                    arrived(out.at[slot], r2.at[slot])
                    sums = gather_up(sums, out.at[slot], outer)
                return sums

            def drain(slot):
                sent(rcv.at[slot], s1.at[slot])
                if outer > 1:
                    sent(out.at[slot], s2.at[slot])

            return send, total, drain

        send_a, total_a, drain_a = summer(
            own_a, rcv_a, mid_a, out_a, sta_s, sta_r, stc_s, stc_r, 0, me_d, R, RA
        )
        send_b, total_b, drain_b = summer(
            own_b, rcv_b, mid_b, out_b, stb_s, stb_r, std_s, std_r, my_m * G, my_c, G, RB
        )

        def put(ref, slot, sums):
            for i, s in enumerate(sums):
                ref[slot, pl.ds(i, 1), :] = s

        def finish_norm(total, slot, table, cb, counts):
            for g in (0, 1):
                mean = total[2 * g : 2 * g + 1] * (1.0 / counts[g])
                var = total[2 * g + 1 : 2 * g + 2] * (1.0 / counts[g]) - mean * mean
                rstd = lax.rsqrt(var + EPS)
                scale = rstd * table[cb, 2 * g : 2 * g + 1, :]
                par[slot, pl.ds(4 * g, 1), :] = mean
                par[slot, pl.ds(4 * g + 1, 1), :] = rstd
                par[slot, pl.ds(4 * g + 2, 1), :] = scale
                par[slot, pl.ds(4 * g + 3, 1), :] = table[cb, 2 * g + 1 : 2 * g + 2, :] - mean * scale

        def param(slot, i, bc):
            return pick(par[slot, pl.ds(i, 1), :], par[slot, pl.ds(4 + i, 1), :], bc)

        def normed(u, slot, bc):
            return u * param(slot, 2, bc) + param(slot, 3, bc)

        def centered(u, slot, bc):
            return (u - param(slot, 0, bc)) * param(slot, 1, bc)

        def put_cof(slot, total, counts):
            for g in (0, 1):
                cof[slot, pl.ds(2 * g, 2), :] = total[2 * g : 2 * g + 2] * (1.0 / counts[g])

        def back(d, z, cslot, zslot, pslot, bc, vc):
            a = pick(cof[cslot, pl.ds(0, 1), :], cof[cslot, pl.ds(2, 1), :], bc)
            b = pick(cof[zslot, pl.ds(1, 1), :], cof[zslot, pl.ds(3, 1), :], bc)
            du = param(pslot, 2, bc) * (d - a - z * b)
            return (du if vc == CH else part(du, 0, vc) if vc else jnp.zeros_like(du)).astype(BF)

        def kept(v, m, bc):
            return v if bc == CH else v * pick(jnp.ones((1, W), F32), keep[m], bc)

        def rows(first, n=CH):
            return pl.ds(first, n)

        def at(b, first):
            return pl.ds(pl.multiple_of(b * OUT + first, CH), CH)

        def block(k):
            return pl.ds(pl.multiple_of(k * OUT, CH), OUT)

        def weight(first):
            return wbuf[pl.ds(pl.multiple_of(first, W), W), :]

        def squares(load):
            def sums(b, f, bc, vc):
                u = load(b, f)
                return (u, u * u)

            return sums

        def add_norm_grads(ref, cb, total):
            for g in (0, 1):
                ref[cb, pl.ds(2 * g, 1), :] += total[2 * g + 1 : 2 * g + 2]
                ref[cb, pl.ds(2 * g + 1, 1), :] += total[2 * g : 2 * g + 1]

        SLOTS, HW = raw.shape[0], raw.shape[2]

        def fetch(count, source, target):
            def copies(b, slot):
                return [
                    pltpu.make_async_copy(source(b, lane), raw.at[slot, lane], raw_s.at[slot, lane])
                    for lane in range(LANES)
                ]

            for ahead in range(min(SLOTS - 1, count)):
                for copy in copies(ahead, ahead):
                    copy.start()

            def one(b, c):
                slot = lax.rem(b, SLOTS)

                @pl.when(b + SLOTS - 1 < count)
                def _():
                    for copy in copies(b + SLOTS - 1, lax.rem(b + SLOTS - 1, SLOTS)):
                        copy.start()

                for lane, copy in enumerate(copies(b, slot)):
                    copy.wait()
                    values = raw[slot, lane, :, 0, :].astype(F32).astype(BF)
                    wbuf[pl.ds(pl.multiple_of(target(b), HW), HW), pl.ds(lane * 128, 128)] = values
                return c

            lax.fori_loop(0, count, one, 0)

        def fetch_narrow(count):
            fetch(count // HW, lambda b, lane: w4_h.at[pl.ds(b * HW, HW), lane], lambda b: b * HW)

        def fetch_wide(first, count, target):
            per = count // HW
            fetch(
                NQ * per,
                lambda b, lane: w16_h.at[pl.ds(first + lax.rem(b, per) * HW, HW), b // per * LANES + lane],
                lambda b: target(b // per) + lax.rem(b, per) * HW,
            )

        def halves(count):
            return [core * (count // 2) + i for i in range(count // 2)]

        def ship(source, target, q, ss, p):
            return remote(wbuf.at[pl.ds(source(q), W)], wbuf.at[pl.ds(target(q), W)], ss.at[q], w_r.at[q], p, me_d)

        def pass_on(target, count, go):
            for q in halves(count):
                ref = wbuf.at[pl.ds(target(q), W)]
                go(ref, q, remote(ref, ref, w_s.at[q], w_r.at[q], me_p, sibling))

        def take(target, count):
            def first(ref, q, copy):
                arrived(ref, w_r.at[q])
                copy.start()

            pass_on(target, count, first)
            for i in range(count // 2):
                q = (1 - core) * (count // 2) + i
                arrived(wbuf.at[pl.ds(target(q), W)], w_r.at[q])

        def w1_at(q):
            return pl.multiple_of(n2 + q * W, W)

        def w3_at(q):
            return pl.multiple_of(nabc + q * W, W)

        def w3_between(q):
            return pl.multiple_of(n1 + q * W, W)

        def lay_narrow(first, grad):
            for lane in range(LANES):
                tmp[pl.ds(first + lane, W, stride=LANES), :] = grad[:, lane * 128 : (lane + 1) * 128]

        def keep_narrow(first, grad):
            lay_narrow(0, grad)
            start = pl.multiple_of(first * LANES, W)
            dwl[pl.ds(start, W * LANES), :] = tmp[pl.ds(0, W * LANES), :].astype(BF)

        def keep_wide(first, lhs, index):
            step = NQ * LANES
            for half in range(W // HALF):
                for q in range(NQ):
                    grad = dot_tn(lhs(pl.ds(half * HALF, HALF)), dwide[index + q, full, :])
                    for lane in range(LANES):
                        part_of = grad[:, lane * 128 : (lane + 1) * 128]
                        tmp[pl.ds(q * LANES + lane, HALF, stride=step), :] = part_of
                dwl[pl.ds((first + half * HALF) * step, HALF * step), :] = tmp[pl.ds(0, HALF * step), :].astype(BF)

        class Reduction:
            def __init__(self, pieces, rows_of, start, used):
                self.pieces, self.rows_of, self.start, self.used = pieces, rows_of, start, used
                self.step = next(a for a in (64, 48, 32, 16) if rows_of % a == 0)
                self.i = me_d // 2

            def at(self, pc):
                return pl.ds(pl.multiple_of(pc * self.rows_of, CH), self.rows_of)

            def each(self, pcs, fn):
                if len(pcs) == 1:
                    fn(pcs[0])
                    return

                def one(pc, c):
                    fn(pc)
                    return c

                lax.fori_loop(pcs[0], pcs[-1] + 1, one, 0)

            def pair(self, t, pc):
                src = dwl.at[pl.ds(pl.multiple_of(self.start(2 * t + 1 - core, pc), CH), self.rows_of)]
                return remote(src, pbuf.at[t, self.at(pc)], pa_s.at[t, pc], pa_r.at[t, pc], me_p, sibling)

            def rightward(self, t, pc):
                ref = rv.at[t, self.at(pc)]
                return remote(ref, ref, ch_s.at[t, pc], ch_r.at[t, pc], me_p, me_d + 2)

            def leftward(self, t, pc):
                slot = jnp.where(t == self.i - 1, N, t)
                src, dst = rv.at[t, self.at(pc)], rv.at[slot, self.at(pc)]
                return remote(src, dst, ch_s.at[t, pc], ch_r.at[slot, pc], me_p, me_d - 2)

            def add(self, t, pc, others, store):
                first, step = self.start(2 * t + core, pc), self.step

                def one(s, c):
                    at_s = pl.ds(pl.multiple_of(pc * self.rows_of + s * step, CH), step)
                    v = dwl[pl.ds(pl.multiple_of(first + s * step, CH), step), :].astype(F32)
                    v += pbuf[t, at_s, :].astype(F32)
                    for slot in others:
                        v += rv[slot, at_s, :].astype(F32)
                    store(at_s, s, v)
                    return c

                lax.fori_loop(0, self.rows_of // step, one, 0)

            def send_pairs(self, pcs, low=0, high=N):
                def one(j, c):
                    t = jnp.where(lax.rem(j, 2) == 0, high - 1 - j // 2, low + j // 2)

                    def send(pc):
                        @pl.when(self.used(2 * t + 1 - core, pc))
                        def _():
                            self.pair(t, pc).start()

                    self.each(pcs, send)
                    return c

                lax.fori_loop(0, high - low, one, 0)

            def forward(self, t, pc, wanted, received, copy):
                def store(at_s, s, v):
                    rv[t, at_s, :] = v.astype(BF)

                @pl.when(wanted & self.used(2 * t + core, pc))
                def _():
                    self.pair(t, pc).wait_recv()
                    if received:
                        arrived(rv.at[t, self.at(pc)], ch_r.at[t, pc])
                    self.add(t, pc, (t,) if received else (), store)
                    copy(t, pc).start()

            def originate(self, pcs, low=0, high=N):
                def one(j, c):
                    right, left = high - 1 - j, low + j

                    def both(pc):
                        self.forward(right, pc, (self.i == 0) & (right > 0), False, self.rightward)
                        self.forward(left, pc, (self.i == N - 1) & (left < N - 1), False, self.leftward)

                    self.each(pcs, both)
                    return c

                lax.fori_loop(0, high - low, one, 0)

            def relay(self, pcs, low=0, high=N):
                def one(j, c):
                    right, left = high - 1 - j, low + j

                    def both(pc):
                        self.forward(right, pc, (self.i > 0) & (right > self.i), True, self.rightward)
                        self.forward(left, pc, (self.i < N - 1) & (left < self.i), True, self.leftward)

                    self.each(pcs, both)
                    return c

                lax.fori_loop(0, high - low, one, 0)

            def finish(self, pc, store):
                i = self.i

                @pl.when(self.used(2 * i + core, pc))
                def _():
                    self.pair(i, pc).wait_recv()
                    for low, high in ((True, True), (True, False), (False, True)):

                        @pl.when(((i > 0) == low) & ((i < N - 1) == high))
                        def _(low=low, high=high):
                            others = ()
                            if low:
                                arrived(rv.at[i, self.at(pc)], ch_r.at[i, pc])
                                others += (i,)
                            if high:
                                arrived(rv.at[N, self.at(pc)], ch_r.at[N, pc])
                                others += (N,)
                            self.add(i, pc, others, store)

            def drain(self):
                def one(j, c):
                    def waits(pc):
                        @pl.when(self.used(2 * j + 1 - core, pc))
                        def _():
                            self.pair(j, pc).wait_send()

                        @pl.when((j > self.i) & self.used(2 * j + core, pc))
                        def _():
                            self.rightward(j, pc).wait_send()

                        @pl.when((j < self.i) & self.used(2 * j + core, pc))
                        def _():
                            self.leftward(j, pc).wait_send()

                    self.each(range(self.pieces), waits)
                    return c

                lax.fori_loop(0, N, one, 0)

        def weights_out():
            copy = pltpu.make_async_copy(tmp.at[pl.ds(0, SR)], dw_o, ld.at[1])
            copy.start()
            copy.wait()

        everything = range(PC)

        def flat(used_rows, pieces=PC):
            PR = SR // pieces
            filled = -(-used_rows // PR) * PR
            if filled > used_rows:
                dwl[pl.ds(used_rows, filled - used_rows), :] = jnp.zeros((filled - used_rows, 128), BF)
            return Reduction(pieces, PR, lambda s, pc: s * SR + pc * PR, lambda s, pc: s * SR + pc * PR < used_rows)

        def launch(red, low=0, high=N):
            red.send_pairs(range(red.pieces), low, high)
            red.originate(range(red.pieces), low, high)

        def finish_flat(red):
            tmp[pl.ds(0, SR), :] = jnp.zeros((SR, 128), F32)

            def finish(pc):
                def store(at_s, s, v):
                    first = pc * red.rows_of + s * red.step
                    tmp[pl.ds(pl.multiple_of(first, CH), red.step), :] = v

                red.finish(pc, store)

            red.each(range(red.pieces), finish)
            weights_out()
            red.drain()

        barrier = pltpu.get_barrier_semaphore()
        loads_x = [
            pltpu.make_async_copy(
                x_h.at[:, :, pl.ds(h * W, W)], xb.at[pl.ds(h * MICRO, MICRO), pl.ds(0, IN)], ld.at[2 * h]
            )
            for h in range(2)
        ]

        @pl.when(me_p < 3)
        def _():
            for copy in loads_x:
                copy.start()

        def greet(i, c):
            p, d = i // R, lax.rem(i, R)

            @pl.when((p != me_p) | (d != me_d))
            def _():
                pl.semaphore_signal(barrier, inc=1, device_id=(p, d), device_id_type=MESH)

            return c

        lax.fori_loop(0, NP * R, greet, 0)

        @pl.when(me_p == 0)
        def _():
            fetch_narrow(n1)

        @pl.when(me_p == 2)
        def _():
            fetch_wide(0, C_MID, lambda q: q * n3)

        ng_o[...] = jnp.zeros_like(ng_o)
        ngs[...] = jnp.zeros_like(ngs)
        for m in range(MICRO):
            lanes = lax.broadcasted_iota(jnp.int32, (1, W), 1)
            keep[m] = jnp.where(lanes < C_MID * width_step[m] // 4, 1.0, 0.0)

        pl.semaphore_wait(barrier, NP * R - 1)

        def lay_out(values, lanes, big_o, small_o, big_rows, side):
            fw[0, pl.ds(0, values.shape[0]), :] = values
            for r in range(big_rows // side):
                big_o[r, :, lanes] = fw[0, pl.ds(r * side, side), :].astype(BF)
            crops = geo.crops[1]
            for p in range(small_o.shape[0]):
                small_o[p, :, lanes] = fw[0, pl.ds(big_rows + p * crops, crops), :].astype(BF)

        def finals():
            arrived(orecv, out_r)
            for q in range(NQ):
                lay_out(orecv[q].astype(F32), pl.ds(q * W, W), ob_o, os_o, geo.out_big, geo.sides[0] // 2)
            arrived(srecv, sb_r)
            arrived(mrecv, mn_r)
            for h in range(2):
                total = mrecv[h].astype(F32) + dot_tn(ps[...], srecv[h])
                lay_out(total, pl.ds(h * W, W), gb_o, gs_o, geo.in_big, geo.sides[0])

        def sub_hop(k):
            ref = col.at[pl.ds(6, 2), k]
            return remote(ref, ref, xs_s.at[k], xs_r.at[k], 0, me_d)

        def sub_back(k):
            return (col.at[pl.ds(6, 2), k], srecv, sb_s.at[k], sb_r, my_m, k * G + my_c)

        def nt_copy(count):
            return remote(nt.at[pl.ds(0, count)], nt2.at[pl.ds(0, count)], nt_s, nt_r, me_p + 1, me_d)

        def main_copy(m):
            return (tgb.at[pl.ds(2 * m, 2), pl.ds(0, IN)], mrecv, mn_s.at[m], mn_r, m, me_d)

        def w1_here(q):
            return pl.multiple_of(q * W, W)

        def section_0(m, first):
            fw[m, pl.ds(0, IN), :] = dot(xb[m, pl.ds(0, IN), :], weight(first)) + dot(
                xb[MICRO + m, pl.ds(0, IN), :], weight(first + W)
            )
            put(own_a, m, reduce_rows(1, runs_in, squares(lambda b, f: fw[m, rows(f), :]), 2))
            send_a(m)

        @pl.when(me_p == 0)
        def _():
            for q in halves(2):
                ship(w1_here, w1_at, q, w_s, 1).start()
            nt_copy(1).start()
            for q in halves(NQ):
                arrived(wbuf.at[pl.ds(w3_between(q), W)], w_r.at[q])
                ship(w3_between, w3_at, q, big_s, 3).start()
            for copy in loads_x:
                copy.wait()

            def first(m, c):
                section_0(m, 0)
                return c

            lax.fori_loop(0, MICRO, first, 0)
            for m in range(MICRO):
                finish_norm(total_a(m), m, nt, 0, count_in)

            tmp[pl.ds(0, n1 * LANES), :] = jnp.zeros((n1 * LANES, 128), F32)

            def back_sums(m):
                arrived(rbig.at[m, pl.ds(0, IN)], big_r.at[m])

                def sums(b, f, bc, vc):
                    u = fw[m, rows(f), :]
                    d = kept(rbig[m, rows(f), :].astype(F32) * slope_of(normed(u, m, bc)), m, bc)
                    fw[MICRO + m, rows(f), :] = d
                    return (d, d * centered(u, m, bc))

                put(own_a, MICRO + m, reduce_rows(1, runs_in, sums, 2))
                send_a(MICRO + m)

            def dx(m):
                total = total_a(MICRO + m)
                put_cof(0, total, count_in)
                add_norm_grads(ng_o, 0, total)

                def grad(b, f, bc, vc):
                    z = centered(fw[m, rows(f), :], m, bc)
                    dwide[m, rows(f), :] = back(fw[MICRO + m, rows(f), :], z, 0, 0, m, bc, vc)

                map_rows(1, runs_in, grad)
                for h in range(2):
                    tgb[2 * m + h, pl.ds(0, IN), :] = dot_nt(dwide[m, pl.ds(0, IN), :], weight(h * W)).astype(BF)
                push(*main_copy(m))
                for h in range(2):
                    grad = dot_tn(xb[h * MICRO + m, pl.ds(0, IN), :], dwide[m, pl.ds(0, IN), :])
                    for lane in range(LANES):
                        at_l = pl.ds(h * W * LANES + lane, W, stride=LANES)
                        tmp[at_l, :] += grad[:, lane * 128 : (lane + 1) * 128]

            def backward(step, c):
                @pl.when(step < MICRO)
                def _():
                    back_sums(step)

                @pl.when(step > 0)
                def _():
                    dx(step - 1)

                return c

            lax.fori_loop(0, MICRO + 1, backward, 0)
            dwl[pl.ds(0, n1 * LANES), :] = tmp[pl.ds(0, n1 * LANES), :].astype(BF)
            red = flat(n1 * LANES, 2 * PC if PR % (2 * CH) == 0 else PC)
            launch(red)
            for k in range(MICRO):
                arrived(col.at[pl.ds(6, 2), k], xs_r.at[k])
                push(*sub_back(k))
            red.relay(range(red.pieces))
            finish_flat(red)
            finals()
            for slot in range(2 * MICRO):
                drain_a(slot)
            for q in halves(2):
                ship(w1_here, w1_at, q, w_s, 1).wait_send()
            for q in halves(NQ):
                ship(w3_between, w3_at, q, big_s, 3).wait_send()
            nt_copy(1).wait_send()
            for m in range(MICRO):
                pushed(*main_copy(m))
                pushed(*sub_back(m))

        @pl.when(me_p == 1)
        def _():
            A2, D2 = MICRO, MICRO + 1
            fetch_narrow(n2)
            for copy in loads_x:
                copy.wait()
            take(w1_at, 2)
            arrived(nt2.at[pl.ds(0, 1)], nt_r)

            def first(m, c):
                section_0(m, n2)
                return c

            lax.fori_loop(0, MICRO, first, 0)

            def windows(m, c):
                finish_norm(total_a(m), m, nt2, 0, count_in)

                def act(b, f, bc, vc):
                    n = normed(fw[m, rows(f), :], m, bc)
                    stage[m, rows(f), :] = kept(n * sigmoid(n), m, bc).astype(BF)

                map_rows(1, runs_in, act)
                col[:, m] = dot(p2[...], stage[m, pl.ds(0, IN), :]).astype(BF).reshape(9, OUT, W)
                return c

            def conv(tap, c):
                fw[A2, full, :] += dot(col[tap].reshape(ROWS, W), weight(tap * C_MID))
                return c

            def conv_sums(m, c):
                put(own_a, MICRO + m, reduce_rows(1, runs_out, squares(lambda b, f: fw[A2, at(m, f), :]), 2))
                send_a(MICRO + m)
                return c

            def a2_copy(m):
                return remote(ssm.at[m], rsm.at[my_m], sm_s.at[m], sm_r.at[my_m], 3, m * G + my_c)

            def give(m, c):
                slot = MICRO + m
                finish_norm(total_a(slot), slot, nt, 0, count_out)

                def act(b, f, bc, vc):
                    n = normed(fw[A2, at(m, f), :], slot, bc)
                    ssm[m, rows(f), :] = kept(n * sigmoid(n), m, bc).astype(BF)

                map_rows(1, runs_out, act)
                a2_copy(m).start()
                return c

            lax.fori_loop(0, MICRO, windows, 0)
            fw[A2, full, :] = dot(col[0].reshape(ROWS, W), weight(0))
            lax.fori_loop(1, 9, conv, 0)
            lax.fori_loop(0, MICRO, conv_sums, 0)
            lax.fori_loop(0, MICRO, give, 0)

            def back_two(m):
                arrived(rsm.at[m], sm_r.at[m])
                slot = MICRO + m

                def sums(b, f, bc, vc):
                    u = fw[A2, at(m, f), :]
                    d = kept(rsm[m, rows(f), :].astype(F32) * slope_of(normed(u, slot, bc)), m, bc)
                    fw[D2, at(m, f), :] = d
                    return (d, d * centered(u, slot, bc))

                put(own_a, 2 * MICRO + m, reduce_rows(1, runs_out, sums, 2))
                send_a(2 * MICRO + m)

            def back_mid(m):
                total = total_a(2 * MICRO + m)
                slot = MICRO + m
                put_cof(0, total, count_out)
                add_norm_grads(ng_o, 0, total)

                def grad(b, f, bc, vc):
                    z = centered(fw[A2, at(m, f), :], slot, bc)
                    dwide[0, at(m, f), :] = back(fw[D2, at(m, f), :], z, 0, 0, slot, bc, vc)

                map_rows(1, runs_out, grad)

            def back_taps(tap, c):
                tgb[tap, full, :] = dot_nt(dwide[0, full, :], weight(tap * C_MID)).astype(BF)
                return c

            def back_one(m, c):
                taps = tgb[:, block(m), :].reshape(9 * OUT, W)
                stage[m, pl.ds(0, IN), :] = dot_tn(p2[...], taps).astype(BF)
                da1_copy(m).start()
                return c

            def da1_copy(m):
                ref = pl.ds(0, IN)
                return remote(stage.at[m, ref], rbig.at[m, ref], big_s.at[m], big_r.at[m], 0, me_d)

            def backward(step, c):
                @pl.when(step < MICRO)
                def _():
                    back_two(step)

                @pl.when(step > 0)
                def _():
                    back_mid(step - 1)

                return c

            def weights(tap, c):
                keep_narrow(tap * C_MID, dot_tn(col[tap].reshape(ROWS, W), dwide[0, full, :]))
                return c

            lax.fori_loop(0, MICRO + 1, backward, 0)
            for tap in range(9):
                back_taps(tap, 0)
            lax.fori_loop(0, MICRO, back_one, 0)
            for tap in range(9):
                weights(tap, 0)
            red = flat(n2 * LANES)
            red.send_pairs(everything)
            red.originate(everything)
            red.relay(everything)
            finals()
            finish_flat(red)
            pass_on(w1_at, 2, lambda ref, q, copy: copy.wait_send())
            for m in range(MICRO):
                da1_copy(m).wait_send()
                a2_copy(m).wait_send()
            for slot in range(3 * MICRO):
                drain_a(slot)

        def share_copy(k):
            return remote(ngs, ngr.at[k - 1], stn_s.at[k - 1], stn_r.at[k - 1], me_p, lax.rem(me_d + k * G, R))

        def share_norm_grads():
            ngs[...] = ng_o[...]
            for k in range(1, MICRO):
                share_copy(k).start()

        def take_norm_grads():
            for k in range(1, MICRO):
                arrived(ngr.at[k - 1], stn_r.at[k - 1])
                ng_o[...] += ngr[k - 1]
            for k in range(1, MICRO):
                share_copy(k).wait_send()

        def sub_copy(m):
            return (col.at[pl.ds(4, 2), m], col.at[pl.ds(0, 2), my_m], xs_s.at[m], xs_r.at[my_m], 2, m * G + my_c)

        def w3_here(q):
            return pl.multiple_of(q * n3, W)

        @pl.when(me_p == 2)
        def _():
            for q in halves(NQ):
                ship(w3_here, w3_between, q, w_s, 0).start()
            nt_copy(NQ).start()
            for copy in loads_x:
                copy.wait()

            def send_x(m, c):
                for h in range(2):
                    col[4 + h, m] = dot(ps[...], xb[h * MICRO + m, pl.ds(0, IN), :]).astype(BF)
                push(*sub_copy(m))
                return c

            lax.fori_loop(0, MICRO, send_x, 0)
            fetch_wide(C_MID, C_IN, lambda q: q * n3 + C_MID)
            for k in range(MICRO):
                arrived(col.at[pl.ds(0, 2), k], xs_r.at[k])

            def w3(q):
                return weight(q * n3)

            def wp(q, h):
                return weight(q * n3 + C_MID + h * W)

            def xsub(h):
                return col[h].reshape(ROWS, W)

            def product(index, value, slot):
                fw[index, full, :] = value
                put(own_b, slot, reduce_rows(MICRO, runs_out, squares(lambda b, f: fw[index, at(b, f), :]), 2))
                send_b(slot)

            def up_copy(q):
                return remote(stage.at[q, full], stage.at[q, full], up_s.at[q], up_r.at[q], 3, me_d)

            def short(q):
                product(NQ + q, dot(xsub(0), wp(q, 0)) + dot(xsub(1), wp(q, 1)), NQ + q)

            def short_out(q):
                finish_norm(total_b(NQ + q), NQ + q, nt, NQ + q, count_out)

                def act(b, f, bc, vc):
                    stage[q, at(b, f), :] = normed(fw[NQ + q, at(b, f), :], NQ + q, bc).astype(BF)

                map_rows(MICRO, runs_out, act)
                up_copy(q).start()

            def shorts(step, c):
                @pl.when(step < NQ)
                def _():
                    short(step)

                @pl.when(step > 0)
                def _():
                    short_out(step - 1)

                return c

            lax.fori_loop(0, NQ + 1, shorts, 0)
            for k in range(MICRO):
                arrived(rsm.at[k], sm_r.at[k])

            def main(q, c):
                product(q, dot(rsm[...].reshape(ROWS, W), w3(q)), q)
                return c

            lax.fori_loop(0, NQ, main, 0)

            def main_norm(q, c):
                finish_norm(total_b(q), q, nt, q, count_out)
                return c

            lax.fori_loop(0, NQ, main_norm, 0)
            tmp[...] = jnp.zeros_like(tmp)
            red = Reduction(
                NQ, PRQ, lambda s, pc: (pc * S2 + s) * PRQ, lambda s, pc: s < S2
            )
            D, SUB = 2 * NQ, 2 * NQ + 1

            def lay_part(s, q):
                start = pl.multiple_of((q * S2 + s) * PRQ, CH)
                at_s = pl.multiple_of(s * RW * LANES, 8)
                dwl[pl.ds(start, RW * LANES), :] = tmp[pl.ds(at_s, RW * LANES), :].astype(BF)

            for q in range(NQ):
                arrived(rbig.at[q, full], big_r.at[q])

                def sums(b, f, bc, vc):
                    um, us = fw[q, at(b, f), :], fw[NQ + q, at(b, f), :]
                    n = normed(um, q, bc) + normed(us, NQ + q, bc)
                    d = rbig[q, at(b, f), :].astype(F32) * slope_of(n)
                    fw[D, at(b, f), :] = d
                    return (d, d * centered(um, q, bc), d * centered(us, NQ + q, bc))

                db, mb, sb, ds, ms, ss = reduce_rows(MICRO, runs_out, sums, 3)
                put(own_b, 2 * NQ + q, (db, mb, ds, ms))
                put(own_b, 3 * NQ + q, (db, sb, ds, ss))
                send_b(2 * NQ + q)
                send_b(3 * NQ + q)
                for i, cb in ((0, q), (1, NQ + q)):
                    total = total_b((2 + i) * NQ + q)
                    put_cof(i, total, count_out)
                    add_norm_grads(ng_o, cb, total)

                def grad(b, f, bc, vc):
                    d = fw[D, at(b, f), :]
                    zm = centered(fw[q, at(b, f), :], q, bc)
                    zs = centered(fw[NQ + q, at(b, f), :], NQ + q, bc)
                    dwide[q, at(b, f), :] = back(d, zm, 0, 0, q, bc, vc)
                    dwide[NQ + q, at(b, f), :] = back(d, zs, 1, 1, NQ + q, bc, vc)

                map_rows(MICRO, runs_out, grad)
                lay_narrow(0, dot_tn(rsm[...].reshape(ROWS, W), dwide[q, full, :]))
                for h in range(2):
                    lay_narrow((1 + h) * W * LANES, dot_tn(xsub(h), dwide[NQ + q, full, :]))

                def lay(s, c):
                    lay_part(s, q)
                    return c

                lax.fori_loop(0, S2, lay, 0)
                red.send_pairs((q,))
                for h in range(2):
                    piece = dot_nt(dwide[NQ + q, full, :], wp(q, h))
                    fw[SUB + h, full, :] = piece if q == 0 else fw[SUB + h, full, :] + piece
                red.originate((q,))

            share_norm_grads()
            for h in range(2):
                for k in range(MICRO):
                    col[6 + h, k] = fw[SUB + h, block(k), :].astype(BF)
            for m in range(MICRO):
                pushed(*sub_copy(m))
            for k in range(MICRO):
                sub_hop(k).start()
            for q in range(NQ):
                red.relay((q,))
            finals()
            take_norm_grads()
            for q in range(NQ):

                def store(at_s, s, v):
                    tmp[pl.ds(pl.multiple_of(SR + s * red.step, CH), red.step), :] = v

                red.finish(q, store)

                @pl.when(red.used(me_d, q))
                def _():
                    for lane in range(LANES):
                        values = tmp[pl.ds(SR + lane, RW, stride=LANES), :]
                        tmp[pl.ds(q * LANES + lane, RW, stride=NQ * LANES), :] = values

            @pl.when(jnp.logical_not(red.used(me_d, 0)))
            def _():
                tmp[pl.ds(0, SR), :] = jnp.zeros((SR, 128), F32)

            weights_out()
            red.drain()
            for q in halves(NQ):
                ship(w3_here, w3_between, q, w_s, 0).wait_send()
            nt_copy(NQ).wait_send()
            for k in range(MICRO):
                sub_hop(k).wait_send()
            for q in range(NQ):
                up_copy(q).wait_send()
            for slot in range(4 * NQ):
                drain_b(slot)

        def cot_copy(m, q):
            src, dst = cot_h.at[m, :, pl.ds(q * W, W)], xb.at[q, block(my_m)]
            return (src, dst, ct_s.at[m], ct_r.at[my_m], 3, m * G + my_c)

        def cot_all(m):
            return (cot_h.at[m], cot_h.at[m], ct_s.at[m], ct_r.at[my_m], 3, m * G + my_c)

        def gate_copy(m):
            return (gate_v.at[m], gateb.at[my_m], gt_s.at[m], gt_r.at[my_m], 3, m * G + my_c)

        def out_copy(k):
            return (xb.at[pl.ds(NQ, NQ), block(k)], orecv, out_s.at[k], out_r, my_m, k * G + my_c)

        @pl.when(me_p == 3)
        def _():
            r = lax.broadcasted_iota(jnp.int32, (OUT, 128), 0)
            small = r - geo.out_big
            for m in range(MICRO):
                g = jnp.zeros((OUT, 128), F32)
                for i in range(geo.crops[0]):
                    area = geo.out_big // geo.crops[0]
                    g = jnp.where((r >= i * area) & (r < (i + 1) * area), gate_big[i, m].astype(F32), g)
                for i in range(geo.crops[1]):
                    mine = (small >= 0) & (lax.rem(small + geo.crops[1] * OUT, geo.crops[1]) == i)
                    g = jnp.where(mine, gate_small[i, m].astype(F32), g)
                gate_v[m] = g
            for m in range(MICRO):
                push(*gate_copy(m))
                for q in range(NQ):
                    push(*cot_copy(m, q))
            fetch_narrow(nab)
            fetch_wide(nab * W // C_OUT, C_MID, lambda q: nab + q * C_MID)
            take(w3_at, NQ)
            arrived(nt2, nt_r)
            A, B, T1, T2, U3 = 2 * NQ, 2 * NQ + 1, 2 * NQ + 2, 2 * NQ + 3, 2 * NQ + 4
            DB, DA, H1, H2 = NQ, NQ + 1, NQ + 2, NQ + 3
            S3, PM = 4 + 2 * NQ, 2 + NQ

            def wa(q):
                return weight(q * W)

            def wb(tap):
                return weight(C_OUT + tap * C_MID)

            def wc(q):
                return weight(nab + q * C_MID)

            def w3(q):
                return weight(nabc + q * C_MID)

            def begin(index, slot):
                put(own_b, slot, reduce_rows(MICRO, runs_out, squares(lambda b, f: fw[index, at(b, f), :]), 2))
                send_b(slot)

            def hidden(index, slot, target):
                def act(b, f, bc, vc):
                    n = normed(fw[index, at(b, f), :], slot, bc)
                    dwide[target, at(b, f), :] = kept(n * sigmoid(n), my_m, bc).astype(BF)

                map_rows(MICRO, runs_out, act)

            def gather(source, target):
                def one(k, c):
                    target(k, dot(pb[...], dwide[source, block(k), :]).astype(BF).reshape(9, OUT, W))
                    return c

                lax.fori_loop(0, MICRO, one, 0)

            def a2_on(k):
                return remote(rsm.at[k], rsm.at[k], sm_t.at[k], sm_r.at[k], 2, me_d)

            for k in range(MICRO):
                arrived(rsm.at[k], sm_r.at[k])
                a2_on(k).start()

            def main(q, c):
                fw[U3 + q, full, :] = dot(rsm[...].reshape(ROWS, W), w3(q))
                begin(U3 + q, S3 + q)
                return c

            lax.fori_loop(0, NQ, main, 0)

            def join(q, c):
                finish_norm(total_b(S3 + q), PM + q, nt2, q, count_out)
                arrived(stage.at[q, full], up_r.at[q])

                def act(b, f, bc, vc):
                    n = normed(fw[U3 + q, at(b, f), :], PM + q, bc) + stage[q, at(b, f), :].astype(F32)
                    rbig[q, at(b, f), :] = (n * sigmoid(n)).astype(BF)

                map_rows(MICRO, runs_out, act)
                return c

            lax.fori_loop(0, NQ, join, 0)
            fw[A, full, :] = sum(dot(rbig[q, full, :], wa(q)) for q in range(NQ))
            begin(A, 0)
            finish_norm(total_b(0), 0, nt, 0, count_out)
            hidden(A, 0, H1)

            def to_col(k, v):
                col[:, k] = v

            gather(H1, to_col)

            fw[B, full, :] = sum(dot(col[tap].reshape(ROWS, W), wb(tap)) for tap in range(9))
            begin(B, 1)
            finish_norm(total_b(1), 1, nt, 1, count_out)
            hidden(B, 1, H2)

            for q in range(NQ):
                fw[q, full, :] = dot(dwide[H2, full, :], wc(q))

            def widen(q, c):
                begin(q, 2 + q)
                return c

            lax.fori_loop(0, NQ, widen, 0)
            for k in range(MICRO):
                arrived(gateb.at[k], gt_r.at[k])
                arrived(xb.at[pl.ds(0, NQ), block(k)], ct_r.at[k])

            def gate_at(b, f):
                g = gateb[b, rows(f), :]
                return jnp.concatenate([g] * LANES, axis=1)

            def ends(q, c):
                finish_norm(total_b(2 + q), 2 + q, nt, 2 + q, count_out)

                def sums(b, f, bc, vc):
                    u = fw[q, at(b, f), :]
                    g = gate_at(b, f)
                    v = rbig[q, at(b, f), :].astype(F32) + g * normed(u, 2 + q, bc)
                    sg = sigmoid(v)
                    xb[NQ + q, at(b, f), :] = (v * sg).astype(BF)
                    d = xb[q, at(b, f), :].astype(F32) * (sg * (1.0 + v * (1.0 - sg)))
                    fw[NQ + q, at(b, f), :] = d
                    d = g * d
                    return (d, d * centered(u, 2 + q, bc))

                put(own_b, 2 + NQ + q, reduce_rows(MICRO, runs_out, sums, 2))
                send_b(2 + NQ + q)
                return c

            lax.fori_loop(0, NQ, ends, 0)

            def ends_back(q, c):
                total = total_b(2 + NQ + q)
                put_cof(0, total, count_out)
                add_norm_grads(ng_o, 2 + q, total)

                def grad(b, f, bc, vc):
                    z = centered(fw[q, at(b, f), :], 2 + q, bc)
                    d = gate_at(b, f) * fw[NQ + q, at(b, f), :]
                    dwide[q, at(b, f), :] = back(d, z, 0, 0, 2 + q, bc, vc)

                map_rows(MICRO, runs_out, grad)
                return c

            lax.fori_loop(0, NQ, ends_back, 0)
            fw[T1, full, :] = sum(dot_nt(dwide[q, full, :], wc(q)) for q in range(NQ))
            for k in range(MICRO):
                push(*out_copy(k))

            def middle(index, pslot, slot, target):
                def sums(b, f, bc, vc):
                    u = fw[index, at(b, f), :]
                    d = kept(fw[T1, at(b, f), :] * slope_of(normed(u, pslot, bc)), my_m, bc)
                    fw[T2, at(b, f), :] = d
                    return (d, d * centered(u, pslot, bc))

                put(own_b, slot, reduce_rows(MICRO, runs_out, sums, 2))
                send_b(slot)
                total = total_b(slot)
                put_cof(0, total, count_out)
                add_norm_grads(ng_o, pslot, total)

                def grad(b, f, bc, vc):
                    z = centered(fw[index, at(b, f), :], pslot, bc)
                    dwide[target, at(b, f), :] = back(fw[T2, at(b, f), :], z, 0, 0, pslot, bc, vc)

                map_rows(MICRO, runs_out, grad)

            middle(B, 1, 2 + 2 * NQ, DB)

            def to_taps(k, v):
                tgb[:, block(k), :] = v

            gather(DB, to_taps)

            fw[T1, full, :] = sum(dot_nt(tgb[tap, full, :], wb(8 - tap)) for tap in range(9))
            middle(A, 0, 3 + 2 * NQ, DA)

            def dy_copy(q):
                return remote(stage.at[q, full], rbig.at[q, full], big_s.at[q], big_r.at[q], 2, me_d)

            for q in range(NQ):
                fw[NQ + q, full, :] += dot_nt(dwide[DA, full, :], wa(q))

            def to_y(q, c):
                def sums(b, f, bc, vc):
                    dy = fw[NQ + q, at(b, f), :].astype(BF)
                    u = fw[U3 + q, at(b, f), :]
                    n = normed(u, PM + q, bc) + stage[q, at(b, f), :].astype(F32)
                    stage[q, at(b, f), :] = dy
                    d = dy.astype(F32) * slope_of(n)
                    fw[q, at(b, f), :] = d
                    return (d, d * centered(u, PM + q, bc))

                put(own_b, S3 + NQ + q, reduce_rows(MICRO, runs_out, sums, 2))
                send_b(S3 + NQ + q)
                dy_copy(q).start()
                return c

            lax.fori_loop(0, NQ, to_y, 0)

            def through_w3(q, c):
                put_cof(0, total_b(S3 + NQ + q), count_out)

                def grad(b, f, bc, vc):
                    z = centered(fw[U3 + q, at(b, f), :], PM + q, bc)
                    xb[q, at(b, f), :] = back(fw[q, at(b, f), :], z, 0, 0, PM + q, bc, vc)

                map_rows(MICRO, runs_out, grad)
                return c

            lax.fori_loop(0, NQ, through_w3, 0)
            fw[T1, full, :] = sum(dot_nt(xb[q, full, :], w3(q)) for q in range(NQ))

            def da2_copy(k):
                return remote(ssm.at[k], rsm.at[my_m], sm_s.at[k], sm_r.at[my_m], 1, k * G + my_c)

            def back_a2(k, c):
                ssm[k] = fw[T1, block(k), :].astype(BF)
                da2_copy(k).start()
                return c

            lax.fori_loop(0, MICRO, back_a2, 0)

            def weights_a(q, c):
                keep_narrow(q * W, dot_tn(rbig[q, full, :], dwide[DA, full, :]))
                return c

            def weights_b(tap, c):
                keep_narrow(C_OUT + tap * C_MID, dot_tn(col[tap].reshape(ROWS, W), dwide[DB, full, :]))
                return c

            share_norm_grads()
            red = flat(nabc * LANES)
            t1, t2 = (C_OUT + C_MID) * LANES // (2 * SR), -(-(nab - C_MID) * LANES // (2 * SR))
            order = ((t2, N), (0, t1), (t1, t2))
            keep_wide(nab * W // C_OUT, lambda r: dwide[H2, full, r], 0)
            weights_b(8, 0)
            launch(red, *order[0])
            lax.fori_loop(0, NQ, weights_a, 0)
            weights_b(0, 0)
            launch(red, *order[1])
            lax.fori_loop(1, 8, weights_b, 0)
            launch(red, *order[2])
            for low, high in order:
                red.relay(everything, low, high)
            finals()
            take_norm_grads()
            finish_flat(red)
            pass_on(w3_at, NQ, lambda ref, q, copy: copy.wait_send())
            for m in range(MICRO):
                pushed(*gate_copy(m))
                pushed(*cot_all(m))
                pushed(*out_copy(m))
                da2_copy(m).wait_send()
                a2_on(m).wait_send()
            for q in range(NQ):
                dy_copy(q).wait_send()
            for slot in range(S3 + 2 * NQ):
                drain_b(slot)

    return kernel


def radix(count, most):
    if count <= most:
        return count
    return next(r for r in range(most, 0, -1) if count % r == 0)


def handed_on(arrays):
    count = len(arrays)

    def kernel(*refs):
        for i in range(count):
            refs[count + i][...] = refs[i][...]

    vmem = pl.BlockSpec(memory_space=pltpu.VMEM)
    return pl.pallas_call(
        kernel,
        out_shape=tuple(jax.ShapeDtypeStruct(a.shape, a.dtype) for a in arrays),
        in_specs=[vmem] * count,
        out_specs=(vmem,) * count,
    )(*arrays)


def solution(mesh):
    R, NP = mesh.shape["dp"], mesh.shape["pipe"]

    def on_device(x_big, x_small, cot_big, cot_small, section_weights, section_norms, gate_big, gate_small, width_step):
        MICRO = x_big.shape[0]
        G = R // MICRO
        geo = Geometry((x_big.shape[1], x_small.shape[1]), (x_big.shape[2], x_small.shape[2]))
        IN, OUT, ROWS = geo.IN, geo.OUT, MICRO * geo.OUT
        PW = section_weights.shape[1]
        NB = section_norms.shape[2] // W
        wide = max(IN, ROWS)

        def joined(big, small, width, length):
            parts = [big.reshape(MICRO, -1, width), small.transpose(0, 2, 3, 1, 4).reshape(MICRO, -1, width)]
            v = jnp.concatenate(parts, axis=1)
            return jnp.pad(v, ((0, 0), (0, length - v.shape[1]), (0, 0)))

        x = joined(x_big, x_small, C_IN, IN)
        cot = joined(cot_big, cot_small, C_OUT, OUT)
        w4 = section_weights.reshape(PW // W, LANES, 1, 128)
        w16 = section_weights.reshape(PW // C_OUT, NQ * LANES, 1, 128)
        SR = PW // 128 // R
        PC = 4 if SR % (4 * CH) == 0 else 2 if SR % (2 * CH) == 0 else 1
        RW = SR // (NQ * LANES)
        SRP = max(SR, NQ * up16(RW * LANES))
        tmp_rows = max(HALF * NQ * LANES, -(-(C_MID + C_IN) // RW) * RW * LANES, SR + up16(RW * LANES))
        nt = section_norms[0].reshape(4, NB, W).transpose(1, 0, 2)
        p2 = geo.windows(2)
        sub = geo.every_second()
        consts = [p2, geo.windows(1), sub]
        consts = [jnp.asarray(c, BF) for c in consts]
        vmem, hbm = pl.BlockSpec(memory_space=pltpu.VMEM), pl.BlockSpec(memory_space=pl.ANY)
        smem = pl.BlockSpec(memory_space=pltpu.SMEM)
        V, D = pltpu.VMEM, pltpu.SemaphoreType.DMA
        RA, RB = radix(R, 8), radix(G, 4)
        nb, sb, ns, ss = geo.crops[0], geo.sides[0], geo.crops[1], geo.sides[1]
        SA, SB = 3 * MICRO, 4 + 4 * NQ

        def sums(slots, first, all_of):
            later = max(all_of // first - 1, 1)
            kept_slots = slots if all_of > first else 1
            return [
                V((slots, 4, W), F32),
                V((slots, max(first - 1, 1), 4, W), F32),
                V((kept_slots, 4, W), F32),
                V((kept_slots, later, 4, W), F32),
            ]

        results = pl.pallas_call(
            make_kernel(geo, R, NP, MICRO, SR, PC),
            out_shape=(
                jax.ShapeDtypeStruct((nb * sb // 2, sb // 2, C_OUT), BF),
                jax.ShapeDtypeStruct((ss * ss // 4, ns, C_OUT), BF),
                jax.ShapeDtypeStruct((nb * sb, sb, C_IN), BF),
                jax.ShapeDtypeStruct((ss * ss, ns, C_IN), BF),
                jax.ShapeDtypeStruct((SR, 128), F32),
                jax.ShapeDtypeStruct((NB, 4, W), F32),
            ),
            in_specs=[hbm, hbm, smem, smem, smem, hbm, hbm, vmem] + [vmem] * 3,
            out_specs=(vmem, vmem, vmem, vmem, hbm, vmem),
            scratch_shapes=[
                V((PW // W + C_OUT, W), BF),
                V((4, LANES, 128, 1, 128), BF),
                V((2 * MICRO, wide, W), BF),
                V((MICRO, OUT, 128), F32),
                V((MICRO, OUT, 128), F32),
                V((MICRO, 1, W), F32),
                V((NQ, wide, W), BF),
                V((NQ, wide, W), BF),
                V((MICRO, OUT, W), BF),
                V((MICRO, OUT, W), BF),
                V((3 * NQ + 4, wide, W), F32),
                V((2 * NQ, wide, W), BF),
                V((9, MICRO, OUT, W), BF),
                V((9, wide, W), BF),
                V((tmp_rows, 128), F32),
                V((2, IN, W), BF),
                V((2, OUT, W), BF),
                V((NQ, OUT, W), BF),
                V((PW // 128, 128), BF),
                V((R // 2, SRP, 128), BF),
                V((R // 2 + 1, SRP, 128), BF),
                V((NQ, 4, W), F32),
                *sums(SA, RA, R),
                *sums(SB, RB, G),
                V((max(2 * MICRO, 2 + 2 * NQ), 8, W), F32),
                V((2, 4, W), F32),
                V((NB, 4, W), F32),
                V((MICRO - 1, NB, 4, W), F32),
                D((3,)),
                D((4, LANES)),
                D((4,)), D((4,)),
                D((4,)), D((4,)), D((4,)),
                D((4,)), D((4,)),
                D((4,)), D((4,)),
                D((4,)), D((4,)),
                D((4,)), D((4,)),
                D((4,)), D((4,)),
                D, D,
                D((4,)), D,
                D((4,)), D,
                D((4,)), D,
                D((SA,)), D((SA,)), D((SA,)), D((SA,)),
                D((SB,)), D((SB,)), D((SB,)), D((SB,)),
                D((MICRO - 1,)), D((MICRO - 1,)),
                D((R // 2, 8)), D((R // 2, 8)),
                D((R // 2, 8)), D((R // 2 + 1, 8)),
            ],
            compiler_params=pltpu.CompilerParams(
                collective_id=0, has_side_effects=True, vmem_limit_bytes=63 << 20
            ),
        )(x, cot, gate_big.T, gate_small.T, width_step, w4, w16, nt, *consts)

        ob, os, gb, gs, dw, ng = handed_on(results)

        def small(v, side, width):
            return v.reshape(side, side, ns, width).transpose(2, 0, 1, 3)[None]

        return (
            ob.reshape(1, nb, sb // 2, sb // 2, C_OUT),
            small(os, ss // 2, C_OUT),
            gb.reshape(1, nb, sb, sb, C_IN),
            small(gs, ss, C_IN),
            dw.reshape(1, PW // R),
            ng.transpose(1, 0, 2).reshape(1, 4, NB * W),
        )

    images = P(None, "dp", None, None, None)
    ends = P("pipe", "dp", None, None, None)
    return jax.shard_map(
        on_device,
        mesh=mesh,
        in_specs=(images,) * 4 + (P("pipe", None), P("pipe", None, None), P(None, "dp"), P(None, "dp"), P()),
        out_specs=(ends,) * 4 + (P("pipe", "dp"), P("pipe", None, None)),
        check_vma=False,
    )
```

```python
import functools

import jax
import jax.numpy as jnp
import numpy as np
from jax import lax
from jax.experimental import pallas as pl
from jax.experimental.pallas import tpu as pltpu
from jax.sharding import PartitionSpec as P

C_IN = 1024
C_MID = 512
C_OUT = 2048
EPS = 1e-05
W = 512
NQ = C_OUT // W
CH = 16
LANES = W // 128
HALF = W // 2
BF = jnp.bfloat16
F32 = jnp.float32
MESH = pl.DeviceIdType.MESH


def up16(n):
    return -(-n // 16) * 16


class Geometry:
    def __init__(self, crops, sides):
        self.crops, self.sides = crops, sides
        self.in_big = crops[0] * sides[0] ** 2
        self.in_all = self.in_big + crops[1] * sides[1] ** 2
        self.out_big = crops[0] * (sides[0] // 2) ** 2
        self.out_all = self.out_big + crops[1] * (sides[1] // 2) ** 2
        self.IN, self.OUT = up16(self.in_all), up16(self.out_all)

    def pixels(self, halves):
        index, table = 0, {}
        for group in (0, 1):
            side = self.sides[group] // 2 if halves else self.sides[group]
            crops, sides = range(self.crops[group]), range(side)
            if group == 0:
                places = [(crop, r, c) for crop in crops for r in sides for c in sides]
            else:
                places = [(crop, r, c) for r in sides for c in sides for crop in crops]
            for place in places:
                table[(group,) + place] = index
                index += 1
        return table

    def windows(self, stride):
        ins, outs = self.pixels(stride == 1), self.pixels(True)
        picks = np.zeros((9, self.OUT, self.OUT if stride == 1 else self.IN), np.float32)
        for (group, crop, r, c), row in outs.items():
            for tap in range(9):
                at = (group, crop, stride * r + tap // 3 - 1, stride * c + tap % 3 - 1)
                if at in ins:
                    picks[tap, row, ins[at]] = 1.0
        return picks.reshape(9 * self.OUT, -1)

    def every_second(self):
        ins, outs = self.pixels(False), self.pixels(True)
        picks = np.zeros((self.OUT, self.IN), np.float32)
        for (group, crop, r, c), row in outs.items():
            picks[row, ins[group, crop, 2 * r, 2 * c]] = 1.0
        return picks


def dot(a, b):
    return jnp.dot(a, b, preferred_element_type=F32)


def dot_nt(a, b):
    return lax.dot_general(a, b, (((1,), (1,)), ((), ())), preferred_element_type=F32)


def dot_tn(a, b):
    return lax.dot_general(a, b, (((0,), (0,)), ((), ())), preferred_element_type=F32)


def sigmoid(v):
    return 0.5 * jnp.tanh(0.5 * v) + 0.5


def slope_of(v):
    s = sigmoid(v)
    return s * (1.0 + v * (1.0 - s))


def runs_of(n_big, n_all, rows):
    runs = []
    for first in range(0, rows, CH):
        kind = (min(max(n_big - first, 0), CH), min(max(n_all - first, 0), CH))
        if runs and runs[-1][2:] == kind:
            runs[-1] = (runs[-1][0], runs[-1][1] + 1) + kind
        else:
            runs.append((first, 1) + kind)
    return runs


def row_ids():
    return lax.broadcasted_iota(jnp.int32, (CH, W), 0)


def part(v, low, high):
    if low >= high:
        return None
    if low == 0 and high == CH:
        return v
    r = row_ids()
    return jnp.where((r >= low) & (r < high), v, 0.0)


def pick(vb, vs, bc):
    if bc == CH:
        return vb
    if bc == 0:
        return vs
    return jnp.where(row_ids() < bc, vb, vs)


def each_step(blocks, runs, body, carry):
    def one_block(b, carry):
        for first, length, bc, vc in runs:
            if length == 1:
                carry = body(b, first, bc, vc, carry)
            else:
                carry = lax.fori_loop(
                    0,
                    length,
                    lambda i, c: body(b, pl.multiple_of(first + CH * i, CH), bc, vc, c),
                    carry,
                    unroll=min(length, 4) if length % min(length, 4) == 0 else 1,
                )
        return carry

    if blocks == 1:
        return one_block(0, carry)
    return lax.fori_loop(0, blocks, one_block, carry)


def reduce_rows(blocks, runs, fn, count):
    def body(b, first, bc, vc, carry):
        values = fn(b, first, bc, vc)
        new = []
        for i, v in enumerate(values):
            for g, piece in enumerate((part(v, 0, bc), part(v, bc, vc))):
                total = carry[g * count + i]
                new.append((g * count + i, total if piece is None else total + piece[:8] + piece[8:]))
        return tuple(v for _, v in sorted(new, key=lambda t: t[0]))

    zero = jnp.zeros((8, W), F32)
    totals = each_step(blocks, runs, body, (zero,) * (2 * count))
    return [jnp.sum(t, axis=0, keepdims=True) for t in totals]


def map_rows(blocks, runs, fn):
    def body(b, first, bc, vc, carry):
        fn(b, first, bc, vc)
        return carry

    each_step(blocks, runs, body, 0)


def make_kernel(geo, R, NP, MICRO, SR, PC):
    G = R // MICRO
    N = R // 2
    PR = SR // PC
    RW = SR // (NQ * LANES)
    PRQ = up16(RW * LANES)
    IN, OUT = geo.IN, geo.OUT
    ROWS = MICRO * OUT
    runs_in = runs_of(geo.in_big, geo.in_all, IN)
    runs_out = runs_of(geo.out_big, geo.out_all, OUT)
    count_in = (float(R * geo.in_big), float(R * (geo.in_all - geo.in_big)))
    count_out = (float(R * geo.out_big), float(R * (geo.out_all - geo.out_big)))
    RA, RB = radix(R, 8), radix(G, 4)
    n1 = C_IN
    n2 = 9 * C_MID
    n3 = C_MID + C_IN
    nab = C_OUT + 9 * C_MID
    nabc = nab + C_OUT
    S2 = -(-n3 // RW)

    def kernel(
        x_h, cot_h, gate_big, gate_small, width_step, w4_h, w16_h, nt, p2, pb, ps,
        ob_o, os_o, gb_o, gs_o, dw_o, ng_o,
        wbuf, raw, xb, gate_v, gateb, keep, stage, rbig, ssm, rsm, fw, dwide, col, tgb, tmp, mrecv, srecv, orecv,
        dwl, pbuf, rv, nt2,
        own_a, rcv_a, mid_a, out_a, own_b, rcv_b, mid_b, out_b, par, cof, ngs, ngr,
        ld, raw_s, big_s, big_r, sm_s, sm_t, sm_r, up_s, up_r, xs_s, xs_r, ct_s, ct_r, gt_s, gt_r, w_s, w_r, nt_s, nt_r,
        out_s, out_r, mn_s, mn_r, sb_s, sb_r, sta_s, sta_r, stc_s, stc_r, stb_s, stb_r, std_s, std_r, stn_s, stn_r,
        pa_s, pa_r, ch_s, ch_r,
    ):
        me_p, me_d = lax.axis_index("pipe"), lax.axis_index("dp")
        my_m, my_c = me_d // G, me_d % G
        core = lax.rem(me_d, 2)
        sibling = me_d + 1 - 2 * core
        full = pl.ds(0, ROWS)

        def remote(src, dst, ss, rs, p, d):
            return pltpu.make_async_remote_copy(
                src_ref=src, dst_ref=dst, send_sem=ss, recv_sem=rs, device_id=(p, d), device_id_type=MESH
            )

        def push(src, dst, ss, rs, p, d):
            here = (me_p == p) & (me_d == d)

            @pl.when(here)
            def _():
                pltpu.make_async_copy(src, dst, rs).start()

            @pl.when(jnp.logical_not(here))
            def _():
                remote(src, dst, ss, rs, p, d).start()

        def pushed(src, dst, ss, rs, p, d):
            @pl.when(jnp.logical_not((me_p == p) & (me_d == d)))
            def _():
                remote(src, dst, ss, rs, p, d).wait_send()

        def arrived(dst, rs):
            remote(dst, dst, rs, rs, me_p, me_d).wait_recv()

        def sent(src, ss):
            remote(src, src, ss, ss, me_p, me_d).wait_send()

        def spread_out(src, target, ss, rs, base, place, step, count):
            def one(k, c):
                peer = base + step * lax.rem(place + k, count)
                remote(src, target.at[k - 1], ss, rs, me_p, peer).start()
                return c

            lax.fori_loop(1, count, one, 0, unroll=count <= 8)

        def gather_up(first, received, count):
            return lax.fori_loop(0, count - 1, lambda k, t: t + received[k], first, unroll=count <= 8)

        def summer(own, rcv, mid, out, s1, r1, s2, r2, base, place, count, inner):
            low, high = lax.rem(place, inner), place // inner
            outer = count // inner

            def send(slot):
                spread_out(own.at[slot], rcv.at[slot], s1.at[slot], r1.at[slot], base + high * inner, low, 1, inner)

            def total(slot):
                arrived(rcv.at[slot], r1.at[slot])
                sums = gather_up(own[slot], rcv.at[slot], inner)
                if outer > 1:
                    mid[slot] = sums
                    spread_out(mid.at[slot], out.at[slot], s2.at[slot], r2.at[slot], base + low, high, inner, outer)
                    arrived(out.at[slot], r2.at[slot])
                    sums = gather_up(sums, out.at[slot], outer)
                return sums

            def drain(slot):
                sent(rcv.at[slot], s1.at[slot])
                if outer > 1:
                    sent(out.at[slot], s2.at[slot])

            return send, total, drain

        send_a, total_a, drain_a = summer(
            own_a, rcv_a, mid_a, out_a, sta_s, sta_r, stc_s, stc_r, 0, me_d, R, RA
        )
        send_b, total_b, drain_b = summer(
            own_b, rcv_b, mid_b, out_b, stb_s, stb_r, std_s, std_r, my_m * G, my_c, G, RB
        )

        def put(ref, slot, sums):
            for i, s in enumerate(sums):
                ref[slot, pl.ds(i, 1), :] = s

        def finish_norm(total, slot, table, cb, counts):
            for g in (0, 1):
                mean = total[2 * g : 2 * g + 1] * (1.0 / counts[g])
                var = total[2 * g + 1 : 2 * g + 2] * (1.0 / counts[g]) - mean * mean
                rstd = lax.rsqrt(var + EPS)
                scale = rstd * table[cb, 2 * g : 2 * g + 1, :]
                par[slot, pl.ds(4 * g, 1), :] = mean
                par[slot, pl.ds(4 * g + 1, 1), :] = rstd
                par[slot, pl.ds(4 * g + 2, 1), :] = scale
                par[slot, pl.ds(4 * g + 3, 1), :] = table[cb, 2 * g + 1 : 2 * g + 2, :] - mean * scale

        def param(slot, i, bc):
            return pick(par[slot, pl.ds(i, 1), :], par[slot, pl.ds(4 + i, 1), :], bc)

        def normed(u, slot, bc):
            return u * param(slot, 2, bc) + param(slot, 3, bc)

        def centered(u, slot, bc):
            return (u - param(slot, 0, bc)) * param(slot, 1, bc)

        def put_cof(slot, total, counts):
            for g in (0, 1):
                cof[slot, pl.ds(2 * g, 2), :] = total[2 * g : 2 * g + 2] * (1.0 / counts[g])

        def back(d, z, cslot, zslot, pslot, bc, vc):
            a = pick(cof[cslot, pl.ds(0, 1), :], cof[cslot, pl.ds(2, 1), :], bc)
            b = pick(cof[zslot, pl.ds(1, 1), :], cof[zslot, pl.ds(3, 1), :], bc)
            du = param(pslot, 2, bc) * (d - a - z * b)
            return (du if vc == CH else part(du, 0, vc) if vc else jnp.zeros_like(du)).astype(BF)

        def kept(v, m, bc):
            return v if bc == CH else v * pick(jnp.ones((1, W), F32), keep[m], bc)

        def rows(first, n=CH):
            return pl.ds(first, n)

        def at(b, first):
            return pl.ds(pl.multiple_of(b * OUT + first, CH), CH)

        def block(k):
            return pl.ds(pl.multiple_of(k * OUT, CH), OUT)

        def weight(first):
            return wbuf[pl.ds(pl.multiple_of(first, W), W), :]

        def squares(load):
            def sums(b, f, bc, vc):
                u = load(b, f)
                return (u, u * u)

            return sums

        def add_norm_grads(ref, cb, total):
            for g in (0, 1):
                ref[cb, pl.ds(2 * g, 1), :] += total[2 * g + 1 : 2 * g + 2]
                ref[cb, pl.ds(2 * g + 1, 1), :] += total[2 * g : 2 * g + 1]

        SLOTS, HW = raw.shape[0], raw.shape[2]

        def fetch(count, source, target):
            def copies(b, slot):
                return [
                    pltpu.make_async_copy(source(b, lane), raw.at[slot, lane], raw_s.at[slot, lane])
                    for lane in range(LANES)
                ]

            for ahead in range(min(SLOTS - 1, count)):
                for copy in copies(ahead, ahead):
                    copy.start()

            def one(b, c):
                slot = lax.rem(b, SLOTS)

                @pl.when(b + SLOTS - 1 < count)
                def _():
                    for copy in copies(b + SLOTS - 1, lax.rem(b + SLOTS - 1, SLOTS)):
                        copy.start()

                for lane, copy in enumerate(copies(b, slot)):
                    copy.wait()
                    values = raw[slot, lane, :, 0, :].astype(F32).astype(BF)
                    wbuf[pl.ds(pl.multiple_of(target(b), HW), HW), pl.ds(lane * 128, 128)] = values
                return c

            lax.fori_loop(0, count, one, 0)

        def fetch_narrow(count):
            fetch(count // HW, lambda b, lane: w4_h.at[pl.ds(b * HW, HW), lane], lambda b: b * HW)

        def fetch_wide(first, count, target):
            per = count // HW
            fetch(
                NQ * per,
                lambda b, lane: w16_h.at[pl.ds(first + lax.rem(b, per) * HW, HW), b // per * LANES + lane],
                lambda b: target(b // per) + lax.rem(b, per) * HW,
            )

        def halves(count):
            return [core * (count // 2) + i for i in range(count // 2)]

        def ship(source, target, q, ss, p):
            return remote(wbuf.at[pl.ds(source(q), W)], wbuf.at[pl.ds(target(q), W)], ss.at[q], w_r.at[q], p, me_d)

        def pass_on(target, count, go):
            for q in halves(count):
                ref = wbuf.at[pl.ds(target(q), W)]
                go(ref, q, remote(ref, ref, w_s.at[q], w_r.at[q], me_p, sibling))

        def take(target, count):
            def first(ref, q, copy):
                arrived(ref, w_r.at[q])
                copy.start()

            pass_on(target, count, first)
            for i in range(count // 2):
                q = (1 - core) * (count // 2) + i
                arrived(wbuf.at[pl.ds(target(q), W)], w_r.at[q])

        def w1_at(q):
            return pl.multiple_of(n2 + q * W, W)

        def w3_at(q):
            return pl.multiple_of(nabc + q * W, W)

        def w3_between(q):
            return pl.multiple_of(n1 + q * W, W)

        def lay_narrow(first, grad):
            for lane in range(LANES):
                tmp[pl.ds(first + lane, W, stride=LANES), :] = grad[:, lane * 128 : (lane + 1) * 128]

        def keep_narrow(first, grad):
            lay_narrow(0, grad)
            start = pl.multiple_of(first * LANES, W)
            dwl[pl.ds(start, W * LANES), :] = tmp[pl.ds(0, W * LANES), :].astype(BF)

        def keep_wide(first, lhs, index):
            step = NQ * LANES
            for half in range(W // HALF):
                for q in range(NQ):
                    grad = dot_tn(lhs(pl.ds(half * HALF, HALF)), dwide[index + q, full, :])
                    for lane in range(LANES):
                        part_of = grad[:, lane * 128 : (lane + 1) * 128]
                        tmp[pl.ds(q * LANES + lane, HALF, stride=step), :] = part_of
                dwl[pl.ds((first + half * HALF) * step, HALF * step), :] = tmp[pl.ds(0, HALF * step), :].astype(BF)

        class Reduction:
            def __init__(self, pieces, rows_of, start, used):
                self.pieces, self.rows_of, self.start, self.used = pieces, rows_of, start, used
                self.step = next(a for a in (64, 48, 32, 16) if rows_of % a == 0)
                self.i = me_d // 2

            def at(self, pc):
                return pl.ds(pl.multiple_of(pc * self.rows_of, CH), self.rows_of)

            def each(self, pcs, fn):
                if len(pcs) == 1:
                    fn(pcs[0])
                    return

                def one(pc, c):
                    fn(pc)
                    return c

                lax.fori_loop(pcs[0], pcs[-1] + 1, one, 0)

            def pair(self, t, pc):
                src = dwl.at[pl.ds(pl.multiple_of(self.start(2 * t + 1 - core, pc), CH), self.rows_of)]
                return remote(src, pbuf.at[t, self.at(pc)], pa_s.at[t, pc], pa_r.at[t, pc], me_p, sibling)

            def rightward(self, t, pc):
                ref = rv.at[t, self.at(pc)]
                return remote(ref, ref, ch_s.at[t, pc], ch_r.at[t, pc], me_p, me_d + 2)

            def leftward(self, t, pc):
                slot = jnp.where(t == self.i - 1, N, t)
                src, dst = rv.at[t, self.at(pc)], rv.at[slot, self.at(pc)]
                return remote(src, dst, ch_s.at[t, pc], ch_r.at[slot, pc], me_p, me_d - 2)

            def add(self, t, pc, others, store):
                first, step = self.start(2 * t + core, pc), self.step

                def one(s, c):
                    at_s = pl.ds(pl.multiple_of(pc * self.rows_of + s * step, CH), step)
                    v = dwl[pl.ds(pl.multiple_of(first + s * step, CH), step), :].astype(F32)
                    v += pbuf[t, at_s, :].astype(F32)
                    for slot in others:
                        v += rv[slot, at_s, :].astype(F32)
                    store(at_s, s, v)
                    return c

                lax.fori_loop(0, self.rows_of // step, one, 0)

            def send_pairs(self, pcs, low=0, high=N):
                def one(j, c):
                    t = jnp.where(lax.rem(j, 2) == 0, high - 1 - j // 2, low + j // 2)

                    def send(pc):
                        @pl.when(self.used(2 * t + 1 - core, pc))
                        def _():
                            self.pair(t, pc).start()

                    self.each(pcs, send)
                    return c

                lax.fori_loop(0, high - low, one, 0)

            def forward(self, t, pc, wanted, received, copy):
                def store(at_s, s, v):
                    rv[t, at_s, :] = v.astype(BF)

                @pl.when(wanted & self.used(2 * t + core, pc))
                def _():
                    self.pair(t, pc).wait_recv()
                    if received:
                        arrived(rv.at[t, self.at(pc)], ch_r.at[t, pc])
                    self.add(t, pc, (t,) if received else (), store)
                    copy(t, pc).start()

            def originate(self, pcs, low=0, high=N):
                def one(j, c):
                    right, left = high - 1 - j, low + j

                    def both(pc):
                        self.forward(right, pc, (self.i == 0) & (right > 0), False, self.rightward)
                        self.forward(left, pc, (self.i == N - 1) & (left < N - 1), False, self.leftward)

                    self.each(pcs, both)
                    return c

                lax.fori_loop(0, high - low, one, 0)

            def relay(self, pcs, low=0, high=N):
                def one(j, c):
                    right, left = high - 1 - j, low + j

                    def both(pc):
                        self.forward(right, pc, (self.i > 0) & (right > self.i), True, self.rightward)
                        self.forward(left, pc, (self.i < N - 1) & (left < self.i), True, self.leftward)

                    self.each(pcs, both)
                    return c

                lax.fori_loop(0, high - low, one, 0)

            def finish(self, pc, store):
                i = self.i

                @pl.when(self.used(2 * i + core, pc))
                def _():
                    self.pair(i, pc).wait_recv()
                    for low, high in ((True, True), (True, False), (False, True)):

                        @pl.when(((i > 0) == low) & ((i < N - 1) == high))
                        def _(low=low, high=high):
                            others = ()
                            if low:
                                arrived(rv.at[i, self.at(pc)], ch_r.at[i, pc])
                                others += (i,)
                            if high:
                                arrived(rv.at[N, self.at(pc)], ch_r.at[N, pc])
                                others += (N,)
                            self.add(i, pc, others, store)

            def drain(self):
                def one(j, c):
                    def waits(pc):
                        @pl.when(self.used(2 * j + 1 - core, pc))
                        def _():
                            self.pair(j, pc).wait_send()

                        @pl.when((j > self.i) & self.used(2 * j + core, pc))
                        def _():
                            self.rightward(j, pc).wait_send()

                        @pl.when((j < self.i) & self.used(2 * j + core, pc))
                        def _():
                            self.leftward(j, pc).wait_send()

                    self.each(range(self.pieces), waits)
                    return c

                lax.fori_loop(0, N, one, 0)

        def weights_out():
            copy = pltpu.make_async_copy(tmp.at[pl.ds(0, SR)], dw_o, ld.at[1])
            copy.start()
            copy.wait()

        everything = range(PC)

        def flat(used_rows, pieces=PC):
            PR = SR // pieces
            filled = -(-used_rows // PR) * PR
            if filled > used_rows:
                dwl[pl.ds(used_rows, filled - used_rows), :] = jnp.zeros((filled - used_rows, 128), BF)
            return Reduction(pieces, PR, lambda s, pc: s * SR + pc * PR, lambda s, pc: s * SR + pc * PR < used_rows)

        def launch(red, low=0, high=N):
            red.send_pairs(range(red.pieces), low, high)
            red.originate(range(red.pieces), low, high)

        def finish_flat(red):
            tmp[pl.ds(0, SR), :] = jnp.zeros((SR, 128), F32)

            def finish(pc):
                def store(at_s, s, v):
                    first = pc * red.rows_of + s * red.step
                    tmp[pl.ds(pl.multiple_of(first, CH), red.step), :] = v

                red.finish(pc, store)

            red.each(range(red.pieces), finish)
            weights_out()
            red.drain()

        barrier = pltpu.get_barrier_semaphore()
        loads_x = [
            pltpu.make_async_copy(
                x_h.at[:, :, pl.ds(h * W, W)], xb.at[pl.ds(h * MICRO, MICRO), pl.ds(0, IN)], ld.at[2 * h]
            )
            for h in range(2)
        ]

        @pl.when(me_p < 3)
        def _():
            for copy in loads_x:
                copy.start()

        def greet(i, c):
            p, d = i // R, lax.rem(i, R)

            @pl.when((p != me_p) | (d != me_d))
            def _():
                pl.semaphore_signal(barrier, inc=1, device_id=(p, d), device_id_type=MESH)

            return c

        lax.fori_loop(0, NP * R, greet, 0)

        @pl.when(me_p == 0)
        def _():
            fetch_narrow(n1)

        @pl.when(me_p == 2)
        def _():
            fetch_wide(0, C_MID, lambda q: q * n3)

        ng_o[...] = jnp.zeros_like(ng_o)
        ngs[...] = jnp.zeros_like(ngs)
        for m in range(MICRO):
            lanes = lax.broadcasted_iota(jnp.int32, (1, W), 1)
            keep[m] = jnp.where(lanes < C_MID * width_step[m] // 4, 1.0, 0.0)

        pl.semaphore_wait(barrier, NP * R - 1)

        def lay_out(values, lanes, big_o, small_o, big_rows, side):
            fw[0, pl.ds(0, values.shape[0]), :] = values
            for r in range(big_rows // side):
                big_o[r, :, lanes] = fw[0, pl.ds(r * side, side), :].astype(BF)
            crops = geo.crops[1]
            for p in range(small_o.shape[0]):
                small_o[p, :, lanes] = fw[0, pl.ds(big_rows + p * crops, crops), :].astype(BF)

        def finals():
            arrived(orecv, out_r)
            for q in range(NQ):
                lay_out(orecv[q].astype(F32), pl.ds(q * W, W), ob_o, os_o, geo.out_big, geo.sides[0] // 2)
            arrived(srecv, sb_r)
            arrived(mrecv, mn_r)
            for h in range(2):
                total = mrecv[h].astype(F32) + dot_tn(ps[...], srecv[h])
                lay_out(total, pl.ds(h * W, W), gb_o, gs_o, geo.in_big, geo.sides[0])

        def sub_hop(k):
            ref = col.at[pl.ds(6, 2), k]
            return remote(ref, ref, xs_s.at[k], xs_r.at[k], 0, me_d)

        def sub_back(k):
            return (col.at[pl.ds(6, 2), k], srecv, sb_s.at[k], sb_r, my_m, k * G + my_c)

        def nt_copy(count):
            return remote(nt.at[pl.ds(0, count)], nt2.at[pl.ds(0, count)], nt_s, nt_r, me_p + 1, me_d)

        def main_copy(m):
            return (tgb.at[pl.ds(2 * m, 2), pl.ds(0, IN)], mrecv, mn_s.at[m], mn_r, m, me_d)

        def w1_here(q):
            return pl.multiple_of(q * W, W)

        def section_0(m, first):
            fw[m, pl.ds(0, IN), :] = dot(xb[m, pl.ds(0, IN), :], weight(first)) + dot(
                xb[MICRO + m, pl.ds(0, IN), :], weight(first + W)
            )
            put(own_a, m, reduce_rows(1, runs_in, squares(lambda b, f: fw[m, rows(f), :]), 2))
            send_a(m)

        @pl.when(me_p == 0)
        def _():
            for q in halves(2):
                ship(w1_here, w1_at, q, w_s, 1).start()
            nt_copy(1).start()
            for q in halves(NQ):
                arrived(wbuf.at[pl.ds(w3_between(q), W)], w_r.at[q])
                ship(w3_between, w3_at, q, big_s, 3).start()
            for copy in loads_x:
                copy.wait()

            def first(m, c):
                section_0(m, 0)
                return c

            lax.fori_loop(0, MICRO, first, 0)
            for m in range(MICRO):
                finish_norm(total_a(m), m, nt, 0, count_in)

            tmp[pl.ds(0, n1 * LANES), :] = jnp.zeros((n1 * LANES, 128), F32)

            def back_sums(m):
                arrived(rbig.at[m, pl.ds(0, IN)], big_r.at[m])

                def sums(b, f, bc, vc):
                    u = fw[m, rows(f), :]
                    d = kept(rbig[m, rows(f), :].astype(F32) * slope_of(normed(u, m, bc)), m, bc)
                    fw[MICRO + m, rows(f), :] = d
                    return (d, d * centered(u, m, bc))

                put(own_a, MICRO + m, reduce_rows(1, runs_in, sums, 2))
                send_a(MICRO + m)

            def dx(m):
                total = total_a(MICRO + m)
                put_cof(0, total, count_in)
                add_norm_grads(ng_o, 0, total)

                def grad(b, f, bc, vc):
                    z = centered(fw[m, rows(f), :], m, bc)
                    dwide[m, rows(f), :] = back(fw[MICRO + m, rows(f), :], z, 0, 0, m, bc, vc)

                map_rows(1, runs_in, grad)
                for h in range(2):
                    piece = dot_tn(xb[h * MICRO + m, pl.ds(0, IN), :], dwide[m, pl.ds(0, IN), :])
                    for lane in range(LANES):
                        at_l = pl.ds(h * W * LANES + lane, W, stride=LANES)
                        tmp[at_l, :] += piece[:, lane * 128 : (lane + 1) * 128]
                for h in range(2):
                    tgb[2 * m + h, pl.ds(0, IN), :] = dot_nt(dwide[m, pl.ds(0, IN), :], weight(h * W)).astype(BF)
                push(*main_copy(m))

            def backward(step, c):
                @pl.when(step < MICRO)
                def _():
                    back_sums(step)

                @pl.when(step > 0)
                def _():
                    dx(step - 1)

                return c

            lax.fori_loop(0, MICRO + 1, backward, 0)
            dwl[pl.ds(0, n1 * LANES), :] = tmp[pl.ds(0, n1 * LANES), :].astype(BF)
            red = flat(n1 * LANES, 2 * PC if PR % (2 * CH) == 0 else PC)
            launch(red)
            for k in range(MICRO):
                arrived(col.at[pl.ds(6, 2), k], xs_r.at[k])
                push(*sub_back(k))
            red.relay(range(red.pieces))
            finish_flat(red)
            finals()
            for slot in range(2 * MICRO):
                drain_a(slot)
            for q in halves(2):
                ship(w1_here, w1_at, q, w_s, 1).wait_send()
            for q in halves(NQ):
                ship(w3_between, w3_at, q, big_s, 3).wait_send()
            nt_copy(1).wait_send()
            for m in range(MICRO):
                pushed(*main_copy(m))
                pushed(*sub_back(m))

        @pl.when(me_p == 1)
        def _():
            A2, D2 = MICRO, MICRO + 1
            fetch_narrow(n2)
            for copy in loads_x:
                copy.wait()
            take(w1_at, 2)
            arrived(nt2.at[pl.ds(0, 1)], nt_r)

            def first(m, c):
                section_0(m, n2)
                return c

            lax.fori_loop(0, MICRO, first, 0)

            def windows(m, c):
                finish_norm(total_a(m), m, nt2, 0, count_in)

                def act(b, f, bc, vc):
                    n = normed(fw[m, rows(f), :], m, bc)
                    stage[m, rows(f), :] = kept(n * sigmoid(n), m, bc).astype(BF)

                map_rows(1, runs_in, act)
                col[:, m] = dot(p2[...], stage[m, pl.ds(0, IN), :]).astype(BF).reshape(9, OUT, W)
                return c

            def conv(tap, c):
                fw[A2, full, :] += dot(col[tap].reshape(ROWS, W), weight(tap * C_MID))
                return c

            def conv_sums(m, c):
                put(own_a, MICRO + m, reduce_rows(1, runs_out, squares(lambda b, f: fw[A2, at(m, f), :]), 2))
                send_a(MICRO + m)
                return c

            def a2_copy(m):
                return remote(ssm.at[m], rsm.at[my_m], sm_s.at[m], sm_r.at[my_m], 3, m * G + my_c)

            def give(m, c):
                slot = MICRO + m
                finish_norm(total_a(slot), slot, nt, 0, count_out)

                def act(b, f, bc, vc):
                    n = normed(fw[A2, at(m, f), :], slot, bc)
                    ssm[m, rows(f), :] = kept(n * sigmoid(n), m, bc).astype(BF)

                map_rows(1, runs_out, act)
                a2_copy(m).start()
                return c

            lax.fori_loop(0, MICRO, windows, 0)
            fw[A2, full, :] = dot(col[0].reshape(ROWS, W), weight(0))
            lax.fori_loop(1, 9, conv, 0)
            lax.fori_loop(0, MICRO, conv_sums, 0)
            lax.fori_loop(0, MICRO, give, 0)

            def back_two(m):
                arrived(rsm.at[m], sm_r.at[m])
                slot = MICRO + m

                def sums(b, f, bc, vc):
                    u = fw[A2, at(m, f), :]
                    d = kept(rsm[m, rows(f), :].astype(F32) * slope_of(normed(u, slot, bc)), m, bc)
                    fw[D2, at(m, f), :] = d
                    return (d, d * centered(u, slot, bc))

                put(own_a, 2 * MICRO + m, reduce_rows(1, runs_out, sums, 2))
                send_a(2 * MICRO + m)

            def back_mid(m):
                total = total_a(2 * MICRO + m)
                slot = MICRO + m
                put_cof(0, total, count_out)
                add_norm_grads(ng_o, 0, total)

                def grad(b, f, bc, vc):
                    z = centered(fw[A2, at(m, f), :], slot, bc)
                    dwide[0, at(m, f), :] = back(fw[D2, at(m, f), :], z, 0, 0, slot, bc, vc)

                map_rows(1, runs_out, grad)

            def back_taps(tap, c):
                tgb[tap, full, :] = dot_nt(dwide[0, full, :], weight(tap * C_MID)).astype(BF)
                return c

            def back_one(m, c):
                taps = tgb[:, block(m), :].reshape(9 * OUT, W)
                stage[m, pl.ds(0, IN), :] = dot_tn(p2[...], taps).astype(BF)
                da1_copy(m).start()
                return c

            def da1_copy(m):
                ref = pl.ds(0, IN)
                return remote(stage.at[m, ref], rbig.at[m, ref], big_s.at[m], big_r.at[m], 0, me_d)

            def backward(step, c):
                @pl.when(step < MICRO)
                def _():
                    back_two(step)

                @pl.when(step > 0)
                def _():
                    back_mid(step - 1)

                return c

            def weights(tap, c):
                keep_narrow(tap * C_MID, dot_tn(col[tap].reshape(ROWS, W), dwide[0, full, :]))
                return c

            lax.fori_loop(0, MICRO + 1, backward, 0)
            for tap in range(9):
                back_taps(tap, 0)
            lax.fori_loop(0, MICRO, back_one, 0)
            red = flat(n2 * LANES)
            cut = 5 * C_MID * LANES // (2 * SR)
            for tap in range(5):
                weights(tap, 0)
            launch(red, 0, cut)
            for tap in range(5, 9):
                weights(tap, 0)
            launch(red, cut, N)
            red.relay(everything, 0, cut)
            red.relay(everything, cut, N)
            finals()
            finish_flat(red)
            pass_on(w1_at, 2, lambda ref, q, copy: copy.wait_send())
            for m in range(MICRO):
                da1_copy(m).wait_send()
                a2_copy(m).wait_send()
            for slot in range(3 * MICRO):
                drain_a(slot)

        def share_copy(k):
            return remote(ngs, ngr.at[k - 1], stn_s.at[k - 1], stn_r.at[k - 1], me_p, lax.rem(me_d + k * G, R))

        def share_norm_grads():
            ngs[...] = ng_o[...]
            for k in range(1, MICRO):
                share_copy(k).start()

        def take_norm_grads():
            for k in range(1, MICRO):
                arrived(ngr.at[k - 1], stn_r.at[k - 1])
                ng_o[...] += ngr[k - 1]
            for k in range(1, MICRO):
                share_copy(k).wait_send()

        def sub_copy(m):
            return (col.at[pl.ds(4, 2), m], col.at[pl.ds(0, 2), my_m], xs_s.at[m], xs_r.at[my_m], 2, m * G + my_c)

        def w3_here(q):
            return pl.multiple_of(q * n3, W)

        @pl.when(me_p == 2)
        def _():
            for q in halves(NQ):
                ship(w3_here, w3_between, q, w_s, 0).start()
            nt_copy(NQ).start()
            for copy in loads_x:
                copy.wait()

            def send_x(m, c):
                for h in range(2):
                    col[4 + h, m] = dot(ps[...], xb[h * MICRO + m, pl.ds(0, IN), :]).astype(BF)
                push(*sub_copy(m))
                return c

            lax.fori_loop(0, MICRO, send_x, 0)
            fetch_wide(C_MID, C_IN, lambda q: q * n3 + C_MID)
            for k in range(MICRO):
                arrived(col.at[pl.ds(0, 2), k], xs_r.at[k])

            def w3(q):
                return weight(q * n3)

            def wp(q, h):
                return weight(q * n3 + C_MID + h * W)

            def xsub(h):
                return col[h].reshape(ROWS, W)

            def product(index, value, slot):
                fw[index, full, :] = value
                put(own_b, slot, reduce_rows(MICRO, runs_out, squares(lambda b, f: fw[index, at(b, f), :]), 2))
                send_b(slot)

            def up_copy(q):
                return remote(stage.at[q, full], stage.at[q, full], up_s.at[q], up_r.at[q], 3, me_d)

            def short(q):
                product(NQ + q, dot(xsub(0), wp(q, 0)) + dot(xsub(1), wp(q, 1)), NQ + q)

            def short_out(q):
                finish_norm(total_b(NQ + q), NQ + q, nt, NQ + q, count_out)

                def act(b, f, bc, vc):
                    stage[q, at(b, f), :] = normed(fw[NQ + q, at(b, f), :], NQ + q, bc).astype(BF)

                map_rows(MICRO, runs_out, act)
                up_copy(q).start()

            def shorts(step, c):
                @pl.when(step < NQ)
                def _():
                    short(step)

                @pl.when(step > 0)
                def _():
                    short_out(step - 1)

                return c

            lax.fori_loop(0, NQ + 1, shorts, 0)
            for k in range(MICRO):
                arrived(rsm.at[k], sm_r.at[k])

            def main(q, c):
                product(q, dot(rsm[...].reshape(ROWS, W), w3(q)), q)
                return c

            lax.fori_loop(0, NQ, main, 0)

            def main_norm(q, c):
                finish_norm(total_b(q), q, nt, q, count_out)
                return c

            lax.fori_loop(0, NQ, main_norm, 0)
            tmp[...] = jnp.zeros_like(tmp)
            red = Reduction(
                NQ, PRQ, lambda s, pc: (pc * S2 + s) * PRQ, lambda s, pc: s < S2
            )
            D, SUB = 2 * NQ, 2 * NQ + 1

            def lay_part(s, q):
                start = pl.multiple_of((q * S2 + s) * PRQ, CH)
                at_s = pl.multiple_of(s * RW * LANES, 8)
                dwl[pl.ds(start, RW * LANES), :] = tmp[pl.ds(at_s, RW * LANES), :].astype(BF)

            for q in range(NQ):
                arrived(rbig.at[q, full], big_r.at[q])

                def sums(b, f, bc, vc):
                    um, us = fw[q, at(b, f), :], fw[NQ + q, at(b, f), :]
                    n = normed(um, q, bc) + normed(us, NQ + q, bc)
                    d = rbig[q, at(b, f), :].astype(F32) * slope_of(n)
                    fw[D, at(b, f), :] = d
                    return (d, d * centered(um, q, bc), d * centered(us, NQ + q, bc))

                db, mb, sb, ds, ms, ss = reduce_rows(MICRO, runs_out, sums, 3)
                put(own_b, 2 * NQ + q, (db, mb, ds, ms))
                put(own_b, 3 * NQ + q, (db, sb, ds, ss))
                send_b(2 * NQ + q)
                send_b(3 * NQ + q)
                for i, cb in ((0, q), (1, NQ + q)):
                    total = total_b((2 + i) * NQ + q)
                    put_cof(i, total, count_out)
                    add_norm_grads(ng_o, cb, total)

                def grad(b, f, bc, vc):
                    d = fw[D, at(b, f), :]
                    zm = centered(fw[q, at(b, f), :], q, bc)
                    zs = centered(fw[NQ + q, at(b, f), :], NQ + q, bc)
                    dwide[q, at(b, f), :] = back(d, zm, 0, 0, q, bc, vc)
                    dwide[NQ + q, at(b, f), :] = back(d, zs, 1, 1, NQ + q, bc, vc)

                map_rows(MICRO, runs_out, grad)
                lay_narrow(0, dot_tn(rsm[...].reshape(ROWS, W), dwide[q, full, :]))
                for h in range(2):
                    lay_narrow((1 + h) * W * LANES, dot_tn(xsub(h), dwide[NQ + q, full, :]))

                def lay(s, c):
                    lay_part(s, q)
                    return c

                lax.fori_loop(0, S2, lay, 0)
                red.send_pairs((q,))
                for h in range(2):
                    piece = dot_nt(dwide[NQ + q, full, :], wp(q, h))
                    fw[SUB + h, full, :] = piece if q == 0 else fw[SUB + h, full, :] + piece
                red.originate((q,))

            share_norm_grads()
            for h in range(2):
                for k in range(MICRO):
                    col[6 + h, k] = fw[SUB + h, block(k), :].astype(BF)
            for m in range(MICRO):
                pushed(*sub_copy(m))
            for k in range(MICRO):
                sub_hop(k).start()
            for q in range(NQ):
                red.relay((q,))
            finals()
            take_norm_grads()
            for q in range(NQ):

                def store(at_s, s, v):
                    tmp[pl.ds(pl.multiple_of(SR + s * red.step, CH), red.step), :] = v

                red.finish(q, store)

                @pl.when(red.used(me_d, q))
                def _():
                    for lane in range(LANES):
                        values = tmp[pl.ds(SR + lane, RW, stride=LANES), :]
                        tmp[pl.ds(q * LANES + lane, RW, stride=NQ * LANES), :] = values

            @pl.when(jnp.logical_not(red.used(me_d, 0)))
            def _():
                tmp[pl.ds(0, SR), :] = jnp.zeros((SR, 128), F32)

            weights_out()
            red.drain()
            for q in halves(NQ):
                ship(w3_here, w3_between, q, w_s, 0).wait_send()
            nt_copy(NQ).wait_send()
            for k in range(MICRO):
                sub_hop(k).wait_send()
            for q in range(NQ):
                up_copy(q).wait_send()
            for slot in range(4 * NQ):
                drain_b(slot)

        def cot_copy(m, q):
            src, dst = cot_h.at[m, :, pl.ds(q * W, W)], xb.at[q, block(my_m)]
            return (src, dst, ct_s.at[m], ct_r.at[my_m], 3, m * G + my_c)

        def cot_all(m):
            return (cot_h.at[m], cot_h.at[m], ct_s.at[m], ct_r.at[my_m], 3, m * G + my_c)

        def gate_copy(m):
            return (gate_v.at[m], gateb.at[my_m], gt_s.at[m], gt_r.at[my_m], 3, m * G + my_c)

        def out_copy(k):
            return (xb.at[pl.ds(NQ, NQ), block(k)], orecv, out_s.at[k], out_r, my_m, k * G + my_c)

        @pl.when(me_p == 3)
        def _():
            r = lax.broadcasted_iota(jnp.int32, (OUT, 128), 0)
            small = r - geo.out_big
            for m in range(MICRO):
                g = jnp.zeros((OUT, 128), F32)
                for i in range(geo.crops[0]):
                    area = geo.out_big // geo.crops[0]
                    g = jnp.where((r >= i * area) & (r < (i + 1) * area), gate_big[i, m].astype(F32), g)
                for i in range(geo.crops[1]):
                    mine = (small >= 0) & (lax.rem(small + geo.crops[1] * OUT, geo.crops[1]) == i)
                    g = jnp.where(mine, gate_small[i, m].astype(F32), g)
                gate_v[m] = g
            for m in range(MICRO):
                push(*gate_copy(m))
                for q in range(NQ):
                    push(*cot_copy(m, q))
            fetch_narrow(nab)
            fetch_wide(nab * W // C_OUT, C_MID, lambda q: nab + q * C_MID)
            take(w3_at, NQ)
            arrived(nt2, nt_r)
            A, B, T1, T2, U3 = 2 * NQ, 2 * NQ + 1, 2 * NQ + 2, 2 * NQ + 3, 2 * NQ + 4
            DB, DA, H1, H2 = NQ, NQ + 1, NQ + 2, NQ + 3
            S3, PM = 4 + 2 * NQ, 2 + NQ

            def wa(q):
                return weight(q * W)

            def wb(tap):
                return weight(C_OUT + tap * C_MID)

            def wc(q):
                return weight(nab + q * C_MID)

            def w3(q):
                return weight(nabc + q * C_MID)

            def begin(index, slot):
                put(own_b, slot, reduce_rows(MICRO, runs_out, squares(lambda b, f: fw[index, at(b, f), :]), 2))
                send_b(slot)

            def hidden(index, slot, target):
                def act(b, f, bc, vc):
                    n = normed(fw[index, at(b, f), :], slot, bc)
                    dwide[target, at(b, f), :] = kept(n * sigmoid(n), my_m, bc).astype(BF)

                map_rows(MICRO, runs_out, act)

            def gather(source, target):
                def one(k, c):
                    target(k, dot(pb[...], dwide[source, block(k), :]).astype(BF).reshape(9, OUT, W))
                    return c

                lax.fori_loop(0, MICRO, one, 0)

            def a2_on(k):
                return remote(rsm.at[k], rsm.at[k], sm_t.at[k], sm_r.at[k], 2, me_d)

            for k in range(MICRO):
                arrived(rsm.at[k], sm_r.at[k])
                a2_on(k).start()

            def main(q, c):
                fw[U3 + q, full, :] = dot(rsm[...].reshape(ROWS, W), w3(q))
                begin(U3 + q, S3 + q)
                return c

            lax.fori_loop(0, NQ, main, 0)

            def join(q, c):
                finish_norm(total_b(S3 + q), PM + q, nt2, q, count_out)
                arrived(stage.at[q, full], up_r.at[q])

                def act(b, f, bc, vc):
                    n = normed(fw[U3 + q, at(b, f), :], PM + q, bc) + stage[q, at(b, f), :].astype(F32)
                    rbig[q, at(b, f), :] = (n * sigmoid(n)).astype(BF)

                map_rows(MICRO, runs_out, act)
                return c

            lax.fori_loop(0, NQ, join, 0)
            fw[A, full, :] = sum(dot(rbig[q, full, :], wa(q)) for q in range(NQ))
            begin(A, 0)
            finish_norm(total_b(0), 0, nt, 0, count_out)
            hidden(A, 0, H1)

            def to_col(k, v):
                col[:, k] = v

            gather(H1, to_col)

            fw[B, full, :] = sum(dot(col[tap].reshape(ROWS, W), wb(tap)) for tap in range(9))
            begin(B, 1)
            finish_norm(total_b(1), 1, nt, 1, count_out)
            hidden(B, 1, H2)

            for q in range(NQ):
                fw[q, full, :] = dot(dwide[H2, full, :], wc(q))

            def widen(q, c):
                begin(q, 2 + q)
                return c

            lax.fori_loop(0, NQ, widen, 0)
            for k in range(MICRO):
                arrived(gateb.at[k], gt_r.at[k])
                arrived(xb.at[pl.ds(0, NQ), block(k)], ct_r.at[k])

            def gate_at(b, f):
                g = gateb[b, rows(f), :]
                return jnp.concatenate([g] * LANES, axis=1)

            def ends(q, c):
                finish_norm(total_b(2 + q), 2 + q, nt, 2 + q, count_out)

                def sums(b, f, bc, vc):
                    u = fw[q, at(b, f), :]
                    g = gate_at(b, f)
                    v = rbig[q, at(b, f), :].astype(F32) + g * normed(u, 2 + q, bc)
                    sg = sigmoid(v)
                    xb[NQ + q, at(b, f), :] = (v * sg).astype(BF)
                    d = xb[q, at(b, f), :].astype(F32) * (sg * (1.0 + v * (1.0 - sg)))
                    fw[NQ + q, at(b, f), :] = d
                    d = g * d
                    return (d, d * centered(u, 2 + q, bc))

                put(own_b, 2 + NQ + q, reduce_rows(MICRO, runs_out, sums, 2))
                send_b(2 + NQ + q)
                return c

            lax.fori_loop(0, NQ, ends, 0)

            def ends_back(q, c):
                total = total_b(2 + NQ + q)
                put_cof(0, total, count_out)
                add_norm_grads(ng_o, 2 + q, total)

                def grad(b, f, bc, vc):
                    z = centered(fw[q, at(b, f), :], 2 + q, bc)
                    d = gate_at(b, f) * fw[NQ + q, at(b, f), :]
                    dwide[q, at(b, f), :] = back(d, z, 0, 0, 2 + q, bc, vc)

                map_rows(MICRO, runs_out, grad)
                return c

            lax.fori_loop(0, NQ, ends_back, 0)
            fw[T1, full, :] = sum(dot_nt(dwide[q, full, :], wc(q)) for q in range(NQ))
            for k in range(MICRO):
                push(*out_copy(k))

            def middle(index, pslot, slot, target):
                def sums(b, f, bc, vc):
                    u = fw[index, at(b, f), :]
                    d = kept(fw[T1, at(b, f), :] * slope_of(normed(u, pslot, bc)), my_m, bc)
                    fw[T2, at(b, f), :] = d
                    return (d, d * centered(u, pslot, bc))

                put(own_b, slot, reduce_rows(MICRO, runs_out, sums, 2))
                send_b(slot)
                total = total_b(slot)
                put_cof(0, total, count_out)
                add_norm_grads(ng_o, pslot, total)

                def grad(b, f, bc, vc):
                    z = centered(fw[index, at(b, f), :], pslot, bc)
                    dwide[target, at(b, f), :] = back(fw[T2, at(b, f), :], z, 0, 0, pslot, bc, vc)

                map_rows(MICRO, runs_out, grad)

            middle(B, 1, 2 + 2 * NQ, DB)

            def to_taps(k, v):
                tgb[:, block(k), :] = v

            gather(DB, to_taps)

            fw[T1, full, :] = sum(dot_nt(tgb[tap, full, :], wb(8 - tap)) for tap in range(9))
            middle(A, 0, 3 + 2 * NQ, DA)

            def dy_copy(q):
                return remote(stage.at[q, full], rbig.at[q, full], big_s.at[q], big_r.at[q], 2, me_d)

            for q in range(NQ):
                fw[NQ + q, full, :] += dot_nt(dwide[DA, full, :], wa(q))

            def to_y(q, c):
                def sums(b, f, bc, vc):
                    dy = fw[NQ + q, at(b, f), :].astype(BF)
                    u = fw[U3 + q, at(b, f), :]
                    n = normed(u, PM + q, bc) + stage[q, at(b, f), :].astype(F32)
                    stage[q, at(b, f), :] = dy
                    d = dy.astype(F32) * slope_of(n)
                    fw[q, at(b, f), :] = d
                    return (d, d * centered(u, PM + q, bc))

                put(own_b, S3 + NQ + q, reduce_rows(MICRO, runs_out, sums, 2))
                send_b(S3 + NQ + q)
                dy_copy(q).start()
                return c

            lax.fori_loop(0, NQ, to_y, 0)

            def through_w3(q, c):
                put_cof(0, total_b(S3 + NQ + q), count_out)

                def grad(b, f, bc, vc):
                    z = centered(fw[U3 + q, at(b, f), :], PM + q, bc)
                    xb[q, at(b, f), :] = back(fw[q, at(b, f), :], z, 0, 0, PM + q, bc, vc)

                map_rows(MICRO, runs_out, grad)
                return c

            lax.fori_loop(0, NQ, through_w3, 0)
            fw[T1, full, :] = sum(dot_nt(xb[q, full, :], w3(q)) for q in range(NQ))

            def da2_copy(k):
                return remote(ssm.at[k], rsm.at[my_m], sm_s.at[k], sm_r.at[my_m], 1, k * G + my_c)

            def back_a2(k, c):
                ssm[k] = fw[T1, block(k), :].astype(BF)
                da2_copy(k).start()
                return c

            lax.fori_loop(0, MICRO, back_a2, 0)

            def weights_a(q, c):
                keep_narrow(q * W, dot_tn(rbig[q, full, :], dwide[DA, full, :]))
                return c

            def weights_b(tap, c):
                keep_narrow(C_OUT + tap * C_MID, dot_tn(col[tap].reshape(ROWS, W), dwide[DB, full, :]))
                return c

            share_norm_grads()
            red = flat(nabc * LANES)
            t1, t2 = (C_OUT + C_MID) * LANES // (2 * SR), -(-(nab - C_MID) * LANES // (2 * SR))
            order = ((t2, N), (0, t1), (t1, t2))
            keep_wide(nab * W // C_OUT, lambda r: dwide[H2, full, r], 0)
            weights_b(8, 0)
            launch(red, *order[0])
            lax.fori_loop(0, NQ, weights_a, 0)
            weights_b(0, 0)
            launch(red, *order[1])
            lax.fori_loop(1, 8, weights_b, 0)
            launch(red, *order[2])
            for low, high in order:
                red.relay(everything, low, high)
            finals()
            take_norm_grads()
            finish_flat(red)
            pass_on(w3_at, NQ, lambda ref, q, copy: copy.wait_send())
            for m in range(MICRO):
                pushed(*gate_copy(m))
                pushed(*cot_all(m))
                pushed(*out_copy(m))
                da2_copy(m).wait_send()
                a2_on(m).wait_send()
            for q in range(NQ):
                dy_copy(q).wait_send()
            for slot in range(S3 + 2 * NQ):
                drain_b(slot)

    return kernel


def radix(count, most):
    if count <= most:
        return count
    return next(r for r in range(most, 0, -1) if count % r == 0)


def handed_on(arrays):
    count = len(arrays)
    jobs = []
    for i, a in enumerate(arrays):
        parts = 4 if a.ndim == 2 and a.shape[0] % 32 == 0 else 1
        jobs += [(i, k * (a.shape[0] // parts), a.shape[0] // parts) for k in range(parts)]

    def kernel(*refs):
        held, sems = refs[2 * count : 3 * count], refs[-1]

        def move(n, src, dst):
            i, first, length = jobs[n]
            part_of = pl.ds(first, length)
            return pltpu.make_async_copy(src[i].at[part_of], dst[i].at[part_of], sems.at[n])

        for n in range(len(jobs)):
            move(n, refs[:count], held).start()
        for n in range(len(jobs)):
            move(n, refs[:count], held).wait()
            move(n, held, refs[count : 2 * count]).start()
        for n in range(len(jobs)):
            move(n, held, refs[count : 2 * count]).wait()

    hbm = pl.BlockSpec(memory_space=pl.ANY)
    return pl.pallas_call(
        kernel,
        out_shape=tuple(jax.ShapeDtypeStruct(a.shape, a.dtype) for a in arrays),
        in_specs=[hbm] * count,
        out_specs=(hbm,) * count,
        scratch_shapes=[pltpu.VMEM(a.shape, a.dtype) for a in arrays] + [pltpu.SemaphoreType.DMA((len(jobs),))],
    )(*arrays)


def solution(mesh):
    R, NP = mesh.shape["dp"], mesh.shape["pipe"]

    def on_device(x_big, x_small, cot_big, cot_small, section_weights, section_norms, gate_big, gate_small, width_step):
        MICRO = x_big.shape[0]
        G = R // MICRO
        geo = Geometry((x_big.shape[1], x_small.shape[1]), (x_big.shape[2], x_small.shape[2]))
        IN, OUT, ROWS = geo.IN, geo.OUT, MICRO * geo.OUT
        PW = section_weights.shape[1]
        NB = section_norms.shape[2] // W
        wide = max(IN, ROWS)

        def joined(big, small, width, length):
            parts = [big.reshape(MICRO, -1, width), small.transpose(0, 2, 3, 1, 4).reshape(MICRO, -1, width)]
            v = jnp.concatenate(parts, axis=1)
            return jnp.pad(v, ((0, 0), (0, length - v.shape[1]), (0, 0)))

        x = joined(x_big, x_small, C_IN, IN)
        cot = joined(cot_big, cot_small, C_OUT, OUT)
        w4 = section_weights.reshape(PW // W, LANES, 1, 128)
        w16 = section_weights.reshape(PW // C_OUT, NQ * LANES, 1, 128)
        SR = PW // 128 // R
        PC = 4 if SR % (4 * CH) == 0 else 2 if SR % (2 * CH) == 0 else 1
        RW = SR // (NQ * LANES)
        SRP = max(SR, NQ * up16(RW * LANES))
        tmp_rows = max(HALF * NQ * LANES, -(-(C_MID + C_IN) // RW) * RW * LANES, SR + up16(RW * LANES))
        nt = section_norms[0].reshape(4, NB, W).transpose(1, 0, 2)
        p2 = geo.windows(2)
        sub = geo.every_second()
        consts = [p2, geo.windows(1), sub]
        consts = [jnp.asarray(c, BF) for c in consts]
        vmem, hbm = pl.BlockSpec(memory_space=pltpu.VMEM), pl.BlockSpec(memory_space=pl.ANY)
        smem = pl.BlockSpec(memory_space=pltpu.SMEM)
        V, D = pltpu.VMEM, pltpu.SemaphoreType.DMA
        RA, RB = radix(R, 8), radix(G, 4)
        nb, sb, ns, ss = geo.crops[0], geo.sides[0], geo.crops[1], geo.sides[1]
        SA, SB = 3 * MICRO, 4 + 4 * NQ

        def sums(slots, first, all_of):
            later = max(all_of // first - 1, 1)
            kept_slots = slots if all_of > first else 1
            return [
                V((slots, 4, W), F32),
                V((slots, max(first - 1, 1), 4, W), F32),
                V((kept_slots, 4, W), F32),
                V((kept_slots, later, 4, W), F32),
            ]

        results = pl.pallas_call(
            make_kernel(geo, R, NP, MICRO, SR, PC),
            out_shape=(
                jax.ShapeDtypeStruct((nb * sb // 2, sb // 2, C_OUT), BF),
                jax.ShapeDtypeStruct((ss * ss // 4, ns, C_OUT), BF),
                jax.ShapeDtypeStruct((nb * sb, sb, C_IN), BF),
                jax.ShapeDtypeStruct((ss * ss, ns, C_IN), BF),
                jax.ShapeDtypeStruct((SR, 128), F32),
                jax.ShapeDtypeStruct((NB, 4, W), F32),
            ),
            in_specs=[hbm, hbm, smem, smem, smem, hbm, hbm, vmem] + [vmem] * 3,
            out_specs=(vmem, vmem, vmem, vmem, hbm, vmem),
            scratch_shapes=[
                V((PW // W + C_OUT, W), BF),
                V((4, LANES, 128, 1, 128), BF),
                V((2 * MICRO, wide, W), BF),
                V((MICRO, OUT, 128), F32),
                V((MICRO, OUT, 128), F32),
                V((MICRO, 1, W), F32),
                V((NQ, wide, W), BF),
                V((NQ, wide, W), BF),
                V((MICRO, OUT, W), BF),
                V((MICRO, OUT, W), BF),
                V((3 * NQ + 4, wide, W), F32),
                V((2 * NQ, wide, W), BF),
                V((9, MICRO, OUT, W), BF),
                V((9, wide, W), BF),
                V((tmp_rows, 128), F32),
                V((2, IN, W), BF),
                V((2, OUT, W), BF),
                V((NQ, OUT, W), BF),
                V((PW // 128, 128), BF),
                V((R // 2, SRP, 128), BF),
                V((R // 2 + 1, SRP, 128), BF),
                V((NQ, 4, W), F32),
                *sums(SA, RA, R),
                *sums(SB, RB, G),
                V((max(2 * MICRO, 2 + 2 * NQ), 8, W), F32),
                V((2, 4, W), F32),
                V((NB, 4, W), F32),
                V((MICRO - 1, NB, 4, W), F32),
                D((3,)),
                D((4, LANES)),
                D((4,)), D((4,)),
                D((4,)), D((4,)), D((4,)),
                D((4,)), D((4,)),
                D((4,)), D((4,)),
                D((4,)), D((4,)),
                D((4,)), D((4,)),
                D((4,)), D((4,)),
                D, D,
                D((4,)), D,
                D((4,)), D,
                D((4,)), D,
                D((SA,)), D((SA,)), D((SA,)), D((SA,)),
                D((SB,)), D((SB,)), D((SB,)), D((SB,)),
                D((MICRO - 1,)), D((MICRO - 1,)),
                D((R // 2, 8)), D((R // 2, 8)),
                D((R // 2, 8)), D((R // 2 + 1, 8)),
            ],
            compiler_params=pltpu.CompilerParams(
                collective_id=0, has_side_effects=True, vmem_limit_bytes=63 << 20
            ),
        )(x, cot, gate_big.T, gate_small.T, width_step, w4, w16, nt, *consts)

        ob, os, gb, gs, dw, ng = handed_on(results)

        def small(v, side, width):
            return v.reshape(side, side, ns, width).transpose(2, 0, 1, 3)[None]

        return (
            ob.reshape(1, nb, sb // 2, sb // 2, C_OUT),
            small(os, ss // 2, C_OUT),
            gb.reshape(1, nb, sb, sb, C_IN),
            small(gs, ss, C_IN),
            dw.reshape(1, PW // R),
            ng.transpose(1, 0, 2).reshape(1, 4, NB * W),
        )

    images = P(None, "dp", None, None, None)
    ends = P("pipe", "dp", None, None, None)
    return jax.shard_map(
        on_device,
        mesh=mesh,
        in_specs=(images,) * 4 + (P("pipe", None), P("pipe", None, None), P(None, "dp"), P(None, "dp"), P()),
        out_specs=(ends,) * 4 + (P("pipe", "dp"), P("pipe", None, None)),
        check_vma=False,
    )
```
